128 devices in a mesh: ctx: 8 (over z, x_lo), exp: 16 (over y, x_hi, core).
Axes of the slice: x: 4 (x_hi: 2, x_lo: 2; x = x_hi * 2 + x_lo), y: 4, z: 4, core: 2. Of those that a mesh axis runs over, the one named last changes fastest.
Arguments:
- tokens: bfloat16 [16, 1024, 1024], P('exp', 'ctx'), may hold values from -6 to 6
- cotangent: bfloat16 [16, 1024, 1024], P('exp', 'ctx'), may hold values from -6 to 6
- routes: int32 [16, 1024, 8], P('exp', 'ctx'), may hold values from 0 to 31, all different within a row; in each aligned block of 128 rows (0 to 127, 128 to 255, ..., all dimensions but the last counted through in order) at most 48 rows name the same one
- query_weight: bfloat16 [1024, 1024], P(None, 'exp'), may hold values from -0.25 to 0.25
- kv_weight: bfloat16 [1024, 1024], P(None, 'exp'), may hold values from -0.25 to 0.25
- output_weight: bfloat16 [1024, 1024], P(None, 'exp'), may hold values from -1 to 1
- router: float32 [1024, 32], P(None, 'exp'), may hold values from -0.09375 to 0.09375
- gains: float32 [2, 1024], P(None, 'exp'), may hold values from 0.5 to 1.5
- gate_weight: bfloat16 [32, 1024, 512], P('exp', 'ctx'), may hold values from -0.1875 to 0.1875
- up_weight: bfloat16 [32, 1024, 512], P('exp', 'ctx'), may hold values from -0.1875 to 0.1875
- down_weight: bfloat16 [32, 1024, 512], P('exp', 'ctx'), may hold values from -0.75 to 0.75
- query_momentum: float32 [1024, 1024], P(None, 'exp'), may hold values from -224 to 224
- kv_momentum: float32 [1024, 1024], P(None, 'exp'), may hold values from -224 to 224
- output_momentum: float32 [1024, 1024], P(None, 'exp'), may hold values from -112 to 112
- gate_momentum: float32 [32, 1024, 512], P('exp', 'ctx'), may hold values from -112 to 112
- up_momentum: float32 [32, 1024, 512], P('exp', 'ctx'), may hold values from -112 to 112
- down_momentum: float32 [32, 1024, 512], P('exp', 'ctx'), may hold values from -32 to 32
- router_first: float32 [1024, 32], P(None, 'exp'), may hold values from -320 to 320
- router_second: float32 [1024, 32], P(None, 'exp'), may hold values from 10240 to 40960
- gains_first: float32 [2, 1024], P(None, 'exp'), may hold values from -160 to 160
- gains_second: float32 [2, 1024], P(None, 'exp'), may hold values from 3276.8 to 13107.2
Outputs:
- block_out: bfloat16 [16, 1024, 1024], P('exp', 'ctx')
- input_grad: float32 [16, 1024, 1024], P('exp', 'ctx')
- query_momentum_new: float32 [1024, 1024], P(None, 'exp')
- query_new: float32 [1024, 1024], P(None, 'exp')
- kv_momentum_new: float32 [1024, 1024], P(None, 'exp')
- kv_new: float32 [1024, 1024], P(None, 'exp')
- output_momentum_new: float32 [1024, 1024], P(None, 'exp')
- output_new: float32 [1024, 1024], P(None, 'exp')
- gate_momentum_new: float32 [32, 1024, 512], P('exp', 'ctx')
- gate_new: float32 [32, 1024, 512], P('exp', 'ctx')
- up_momentum_new: float32 [32, 1024, 512], P('exp', 'ctx')
- up_new: float32 [32, 1024, 512], P('exp', 'ctx')
- down_momentum_new: float32 [32, 1024, 512], P('exp', 'ctx')
- down_new: float32 [32, 1024, 512], P('exp', 'ctx')
- router_first_new: float32 [1024, 32], P(None, 'exp')
- router_second_new: float32 [1024, 32], P(None, 'exp')
- router_new: float32 [1024, 32], P(None, 'exp')
- gains_first_new: float32 [2, 1024], P(None, 'exp')
- gains_second_new: float32 [2, 1024], P(None, 'exp')
- gains_new: float32 [2, 1024], P(None, 'exp')
The draws below stay inside these ranges and needn't reach their ends.
Inputs may be any that keep to these rules, and one draw needn't show every extreme that they name: `routes`: each token names 8 different experts. Among the tokens of one device, in sequence order, no expert is named by more than 48 tokens, a bound that some block reaches.
All inputs are finite; a program needn't handle non-finite values.
Results may differ from the reference program's by a relative error of at most 0.015.
The reference program's roundings to bfloat16 on the way count: a program that leaves them out, or rounds other values in their place, can miss the bound.
Values may be sent and summed in bfloat16 or wider, within the bound.
No kernel may reach another device: no remote copies, remote signals or barrier semaphores. Data moves between devices by JAX's collectives and lax.ppermute only.
A program may use at most 192 MiB of HBM per device.

```python
import math
import jax
import jax.numpy as jnp
import numpy as np
from jax import lax

D = 1024
HEADS = 16
KV = 8
HD = 64
FF = 512
TOP = 8
STEP = 10
EXPERTS = 32
SEQS = 16
SEQ_LEN = 1024
LOCAL = 128
MOST = 48


def shard_levels(stream_key, shape, split, least, top_value):
    def one(dim, blocks):
        steps = jax.random.uniform(jax.random.fold_in(jax.random.fold_in(stream_key, 6), dim), (blocks,), jnp.float32, least / len(split), top_value / len(split))
        return jnp.repeat(jnp.exp(steps), shape[dim] // blocks).reshape((-1,) + (1,) * (len(shape) - dim - 1))

    level = one(*split[0])
    for cut in split[1:]:
        level = level * one(*cut)
    return level


def routed_block(own_key, own, number, rows, amount, top, bound, lean):
    order = jax.random.permutation(own_key, amount)
    crowded, common = shares(amount, rows * top, bound, lean, True), shares(amount, rows * top, bound, lean, False)
    places = jnp.arange(amount)

    def named(tallies, rotation):
        used = int((tallies > 0).sum())
        fixed = max(1, used // 4)
        passed = fixed + (places - fixed + rotation * (used - fixed)) % max(1, amount - fixed)
        return jnp.zeros((amount,), jnp.int32).at[order[jnp.where(places < fixed, places, passed)]].set(jnp.asarray(tallies, jnp.int32))

    tallies = jnp.where(number % 4 == 0, named(crowded, number // 4), named(common, number - number // 4 - 1))
    mixed = jax.random.permutation(jax.random.fold_in(own, 3), amount)
    source_of, receiver = mixed[0:amount // 2 * 2:2], mixed[1:amount // 2 * 2:2]
    margin = jnp.minimum(tallies[source_of] - 1, bound - tallies[receiver]) // 2
    margin = jnp.where((source_of == order[0]) | (receiver == order[0]) | (tallies[receiver] == 0), 0, jnp.maximum(margin, 0))
    passed = jax.random.randint(jax.random.fold_in(own, 4), (amount // 2,), 0, 1 << 20) % (margin + 1)
    tallies = tallies.at[source_of].add(-passed).at[receiver].add(passed)
    items = jnp.searchsorted(jnp.cumsum(tallies), jnp.arange(rows * top), side="right").astype(jnp.int32)
    grid = items.reshape(top, rows).T
    grid = grid[jax.random.permutation(jax.random.fold_in(own, 1), rows)]
    rotation = jax.random.randint(jax.random.fold_in(own, 2), (rows, 1), 0, top)
    return jnp.take_along_axis(grid, (jnp.arange(top)[None, :] + rotation) % top, axis=1)


def shares(number_of, total, bound, skew, full):
    loads = [(1 << 20) // math.isqrt(grade ** skew) + 1 for grade in range(1, number_of + 1)]
    largest = bound if full else min(bound, max(-(-total // number_of), total * loads[0] // sum(loads)))
    least = 1 if total - largest >= number_of - 1 else 0
    counts, spare = [largest] + [least] * (number_of - 1), total - largest - least * (number_of - 1)
    while spare > 0:
        candidates = [i for i in range(1, number_of) if counts[i] < largest] or [i for i in range(1, number_of) if counts[i] < bound]
        whole, left = sum([loads[i] for i in candidates]), spare
        for i in candidates:
            extra = min(bound - counts[i], max(1, left * loads[i] // whole), spare)
            counts[i] = counts[i] + extra
            spare = spare - extra
    return np.array(counts)


def normal_values(rng, dims, spread, bound, split=(), kind=jnp.bfloat16):
    level = shard_levels(rng, dims, split, -0.22, 0.18) if split else 1.0
    array = jax.random.normal(rng, dims, jnp.float32) * spread * level
    return jnp.minimum(jnp.maximum(array, -bound), bound).astype(kind)


def setup_inputs(seed: int = 0) -> dict:
    key_list = jax.random.split(jax.random.key(seed), 22)
    tokens = normal_values(key_list[0], (SEQS, SEQ_LEN, D), 1.0, 6.0, ((0, 16), (1, 8)))
    cotangent = normal_values(key_list[1], (SEQS, SEQ_LEN, D), 1.0, 6.0, ((0, 16), (1, 8)))
    routes_keys = jax.random.split(jax.random.fold_in(key_list[2], 1), SEQS * SEQ_LEN // LOCAL)
    routes_turns = jax.random.permutation(jax.random.fold_in(key_list[2], 3), SEQS * SEQ_LEN // LOCAL)
    routes = jax.vmap(lambda own, number: routed_block(jax.random.fold_in(key_list[2], 2), own, number, LOCAL, EXPERTS, TOP, MOST, 1))(routes_keys, routes_turns).reshape((SEQS, SEQ_LEN, TOP))
    query_weight = normal_values(key_list[3], (D, HEADS * HD), (D // 2) ** -0.5, 0.25, ((1, 16),))
    kv_weight = normal_values(key_list[4], (D, 2 * KV * HD), (D // 2) ** -0.5, 0.25, ((1, 16),))
    output_weight = normal_values(key_list[5], (D, HEADS * HD), (HD // 2) ** -0.5, 1.0, ((1, 16),))
    router = normal_values(key_list[6], (D, EXPERTS), (4 * D) ** -0.5, 0.09375, ((1, 16),), jnp.float32)
    gains = jnp.clip(1.0 + 0.1 * jax.random.normal(key_list[7], (2, D), jnp.float32), 0.5, 1.5)
    gate_weight = normal_values(key_list[8], (EXPERTS, D, FF), D ** -0.5, 0.1875, ((0, 16), (1, 8)))
    up_weight = normal_values(key_list[9], (EXPERTS, D, FF), D ** -0.5, 0.1875, ((0, 16), (1, 8)))
    down_weight = normal_values(key_list[10], (EXPERTS, D, FF), (FF // 8) ** -0.5, 0.75, ((0, 16), (1, 8)))
    query_momentum = normal_values(key_list[11], (D, HEADS * HD), (0.3 * (SEQS * SEQ_LEN) ** 0.5), 224.0, ((1, 16),), jnp.float32)
    kv_momentum = normal_values(key_list[12], (D, 2 * KV * HD), (0.3 * (SEQS * SEQ_LEN) ** 0.5), 224.0, ((1, 16),), jnp.float32)
    output_momentum = normal_values(key_list[13], (D, HEADS * HD), (0.15 * (SEQS * SEQ_LEN) ** 0.5), 112.0, ((1, 16),), jnp.float32)
    gate_momentum = normal_values(key_list[14], (EXPERTS, D, FF), (0.3 * (SEQS * SEQ_LEN * TOP // EXPERTS) ** 0.5), 112.0, ((0, 16), (1, 8)), jnp.float32)
    up_momentum = normal_values(key_list[15], (EXPERTS, D, FF), (0.3 * (SEQS * SEQ_LEN * TOP // EXPERTS) ** 0.5), 112.0, ((0, 16), (1, 8)), jnp.float32)
    down_momentum = normal_values(key_list[16], (EXPERTS, D, FF), (0.08 * (SEQS * SEQ_LEN * TOP // EXPERTS) ** 0.5), 32.0, ((0, 16), (1, 8)), jnp.float32)
    router_first = normal_values(key_list[17], (D, EXPERTS), (0.8 * (SEQS * SEQ_LEN * TOP // EXPERTS) ** 0.5), 320.0, ((1, 16),), jnp.float32)
    router_second = jnp.clip(jnp.exp(math.log(40960.0) - 1.3862944 * jax.random.uniform(key_list[18], (D, EXPERTS), jnp.float32) ** shard_levels(key_list[18], (D, EXPERTS), ((1, 16),), -0.2, 0.2)), 10240.0, 40960.0)
    gains_first = normal_values(key_list[19], (2, D), (0.2 * (SEQS * SEQ_LEN) ** 0.5), 160.0, ((1, 16),), jnp.float32)
    gains_second = jnp.clip(jnp.exp(math.log(13107.2) - 1.3862944 * jax.random.uniform(key_list[20], (2, D), jnp.float32) ** shard_levels(key_list[20], (2, D), ((1, 16),), -0.2, 0.2)), 3276.8, 13107.2)
    return dict(tokens=tokens, cotangent=cotangent, routes=routes, query_weight=query_weight, kv_weight=kv_weight, output_weight=output_weight, router=router, gains=gains, gate_weight=gate_weight, up_weight=up_weight, down_weight=down_weight, query_momentum=query_momentum, kv_momentum=kv_momentum, output_momentum=output_momentum, gate_momentum=gate_momentum, up_momentum=up_momentum, down_momentum=down_momentum, router_first=router_first, router_second=router_second, gains_first=gains_first, gains_second=gains_second)


@jax.custom_vjp
def low(v):
    return lax.optimization_barrier(v.astype(jnp.bfloat16)).astype(jnp.float32)

@jax.custom_vjp
def low_back(v):
    return v

def low_keep(v):
    return (low(v), None)

def low_pass(kept, grad):
    return (grad,)

def back_keep(v):
    return (v, None)

def back_low(kept, grad):
    return (low(grad),)
low.defvjp(low_keep, low_pass)
low_back.defvjp(back_keep, back_low)
eps_norm = 1e-05
rope_base = 10000.0
mom_rate = 0.95
muon_rate = 0.15
decay_rate = 0.1
adam_one = 0.9
adam_two = 0.95
adam_eps = 1e-08
router_rate = 0.015
gain_rate = 0.2
coef_one = 3.4445
coef_two = -4.775
coef_three = 2.0315
highest = lax.Precision.HIGHEST

def rope_tables(token_count):
    half_width = HD // 2
    frequency = rope_base ** (-jnp.arange(half_width, dtype=jnp.float32) * 2.0 / HD)
    position = jnp.arange(token_count, dtype=jnp.int32).astype(jnp.float32)
    angle_grid = position[:, None] * frequency[None, :]
    return (jnp.cos(angle_grid), jnp.sin(angle_grid))

def rotate(vector, cosine, sine):
    half_width = vector.shape[-1] // 2
    front_half = vector[..., :half_width]
    back_half = vector[..., half_width:]
    cos_rows = cosine[:, None, :]
    sin_rows = sine[:, None, :]
    return jnp.concatenate([front_half * cos_rows - back_half * sin_rows, back_half * cos_rows + front_half * sin_rows], axis=-1)

def route_ranks(route_block):
    flat_ids = route_block.reshape(-1)
    route_hits = (flat_ids[:, None] == jnp.arange(EXPERTS, dtype=jnp.int32)[None, :]).astype(jnp.int32)
    earlier = jnp.cumsum(route_hits, axis=0) - route_hits
    return lax.optimization_barrier(jnp.sum(earlier * route_hits, axis=1))

def layer_sequence(inputs, route_ids, query_weight, kv_weight, output_weight, router_low, gains_low, gate_weight, up_weight, down_weight, cosine, sine):
    token_count = inputs.shape[0]
    inv_one = lax.rsqrt(lax.optimization_barrier(jnp.mean(inputs * inputs, axis=-1, keepdims=True)) + eps_norm)
    normed_one = low(inputs * inv_one * gains_low[0])
    query_raw = jnp.dot(normed_one, query_weight, precision=highest)
    kv_raw = jnp.dot(normed_one, kv_weight, precision=highest)
    queries = low(rotate(low_back(query_raw).reshape(token_count, HEADS, HD), cosine, sine))
    keys = low(rotate(low_back(kv_raw[:, :KV * HD]).reshape(token_count, KV, HD), cosine, sine))
    values = low(low_back(kv_raw[:, KV * HD:])).reshape(token_count, KV, HD)
    group_size = HEADS // KV
    query_groups = queries.reshape(token_count, KV, group_size, HD)
    scores = low_back(jnp.einsum('ikgd,jkd->kgij', query_groups, keys, precision=highest) * HD ** (-0.5))
    causal = jnp.arange(token_count)[None, :] <= jnp.arange(token_count)[:, None]
    scores = jnp.where(causal, scores, -1e+30)
    weights_low = low(jax.nn.softmax(scores, axis=-1))
    mixed = jnp.einsum('kgij,jkd->ikgd', weights_low, values, precision=highest).reshape(token_count, HEADS * HD)
    mixed = low(low_back(mixed))
    attended = low_back(jnp.dot(mixed, output_weight.T, precision=highest))
    residual = inputs + attended
    inv_two = lax.rsqrt(lax.optimization_barrier(jnp.mean(residual * residual, axis=-1, keepdims=True)) + eps_norm)
    normed_two = low(residual * inv_two * gains_low[1])
    logits = low_back(jnp.dot(normed_two, router_low, precision=highest))
    chosen = jnp.take_along_axis(logits, route_ids, axis=1)
    gate_weights = jax.nn.softmax(chosen, axis=-1)
    block_count = token_count // LOCAL
    rank = jax.vmap(route_ranks)(route_ids.reshape(block_count, LOCAL, TOP)).reshape(token_count, TOP)
    slot = (jnp.arange(token_count, dtype=jnp.int32) // LOCAL)[:, None] * MOST + rank
    token_ids = jnp.repeat(jnp.arange(token_count, dtype=jnp.int32), TOP)
    slot_table = jnp.full((EXPERTS, block_count * MOST), token_count, jnp.int32).at[route_ids.reshape(-1), slot.reshape(-1)].set(token_ids)
    padded = jnp.concatenate([normed_two, jnp.zeros((1, D), jnp.float32)], axis=0)
    expert_inputs = low_back(padded[slot_table])
    gate_pre = low_back(jnp.einsum('ecd,edf->ecf', expert_inputs, gate_weight, precision=highest))
    up_pre = low_back(jnp.einsum('ecd,edf->ecf', expert_inputs, up_weight, precision=highest))
    hidden = low(jax.nn.silu(gate_pre) * up_pre)
    produced = low(low_back(jnp.einsum('ecf,edf->ecd', hidden, down_weight, precision=highest)))
    route_values = produced[route_ids, slot]
    return residual + lax.optimization_barrier(jnp.sum(gate_weights[:, :, None] * route_values, axis=1))

def forward(inputs, query_weight, kv_weight, output_weight, router, gains, gate_weight, up_weight, down_weight, routes):
    gains_low = low(gains)
    router_low = low(router)
    cosine, sine = rope_tables(SEQ_LEN)

    def one_sequence(item):
        return layer_sequence(item[0], item[1], query_weight, kv_weight, output_weight, router_low, gains_low, gate_weight, up_weight, down_weight, cosine, sine)
    return lax.map(jax.checkpoint(one_sequence), (inputs, routes))

def orthogonalize(matrices):
    magnitude = jnp.sqrt(lax.optimization_barrier(jnp.sum(matrices * matrices, axis=(-2, -1), keepdims=True)))
    matrices = matrices / (magnitude + 1e-07)
    for iteration in range(5):
        gram_mat = jnp.einsum('bij,bkj->bik', matrices, matrices, precision=highest)
        poly_term = coef_two * gram_mat + coef_three * jnp.einsum('bij,bjk->bik', gram_mat, gram_mat, precision=highest)
        matrices = coef_one * matrices + jnp.einsum('bij,bjk->bik', poly_term, matrices, precision=highest)
    return matrices

def step_weight(weight, ortho):
    return weight.astype(jnp.float32) * (1.0 - muon_rate * decay_rate) - muon_rate * 0.2 * math.sqrt(D) * ortho

def head_update(weight, momentum, grad):
    fresh = mom_rate * momentum + grad
    row_count, col_count = fresh.shape
    blocks = jnp.transpose(fresh.reshape(row_count, col_count // HD, HD), (1, 2, 0))
    ortho = jnp.transpose(orthogonalize(blocks), (2, 0, 1)).reshape(row_count, col_count)
    return (fresh, step_weight(weight, ortho))

def expert_update(weight, momentum, grad):
    fresh = mom_rate * momentum + grad
    ortho = jnp.swapaxes(orthogonalize(jnp.swapaxes(fresh, 1, 2)), 1, 2)
    return (fresh, step_weight(weight, ortho))

def adam_update(param, first, second, grad, rate, decay):
    first = adam_one * first + (1.0 - adam_one) * grad
    second = adam_two * second + (1.0 - adam_two) * grad * grad
    fixed_one = first / (1.0 - adam_one ** STEP)
    fixed_two = second / (1.0 - adam_two ** STEP)
    return (first, second, param * (1.0 - rate * decay) - rate * fixed_one / (jnp.sqrt(fixed_two) + adam_eps))

def reference(tokens, cotangent, routes, query_weight, kv_weight, output_weight, router, gains, gate_weight, up_weight, down_weight, query_momentum, kv_momentum, output_momentum, gate_momentum, up_momentum, down_momentum, router_first, router_second, gains_first, gains_second):
    primals = (tokens.astype(jnp.float32), query_weight.astype(jnp.float32), kv_weight.astype(jnp.float32), output_weight.astype(jnp.float32), router, gains, gate_weight.astype(jnp.float32), up_weight.astype(jnp.float32), down_weight.astype(jnp.float32))
    block_value, pullback = jax.vjp(lambda *items: forward(*items, routes), *primals)
    grads = pullback(cotangent.astype(jnp.float32))
    input_grad, grad_query, grad_kv, grad_output, grad_router, grad_gains, grad_gate, grad_up, grad_down = grads
    query_fresh, query_new = head_update(query_weight, query_momentum, grad_query)
    kv_fresh, kv_new = head_update(kv_weight, kv_momentum, grad_kv)
    output_fresh, output_new = head_update(output_weight, output_momentum, grad_output)
    gate_fresh, gate_new = expert_update(gate_weight, gate_momentum, grad_gate)
    up_fresh, up_new = expert_update(up_weight, up_momentum, grad_up)
    down_fresh, down_new = expert_update(down_weight, down_momentum, grad_down)
    router_one, router_two, router_new = adam_update(router, router_first, router_second, grad_router, router_rate, decay_rate)
    gains_one, gains_two, gains_new = adam_update(gains, gains_first, gains_second, grad_gains, gain_rate, 0.0)
    return (block_value.astype(jnp.bfloat16), input_grad, query_fresh, query_new, kv_fresh, kv_new, output_fresh, output_new, gate_fresh, gate_new, up_fresh, up_new, down_fresh, down_new, router_one, router_two, router_new, gains_one, gains_two, gains_new)
```

```python
import math

import jax
import jax.numpy as jnp
from jax import lax
from jax.experimental import pallas as pl
from jax.experimental.pallas import tpu as pltpu
from jax.sharding import PartitionSpec as P

D = 1024
HEADS = 16
KV = 8
HD = 64
TOP = 8
STEP = 10


eps_norm = 1e-05
rope_base = 10000.0
mom_rate = 0.95
muon_rate = 0.15
decay_rate = 0.1
adam_one = 0.9
adam_two = 0.95
adam_eps = 1e-08
router_rate = 0.015
gain_rate = 0.2
coef_one = 3.4445
coef_two = -4.775
coef_three = 2.0315
highest = lax.Precision.HIGHEST


def rope_tables(first_row, token_count):
    half_width = HD // 2
    frequency = rope_base ** (-jnp.arange(half_width, dtype=jnp.float32) * 2.0 / HD)
    position = (first_row + jnp.arange(token_count, dtype=jnp.int32)).astype(jnp.float32)
    angle_grid = position[:, None] * frequency[None, :]
    return (jnp.cos(angle_grid), jnp.sin(angle_grid))


def rotate(vector, cosine, sine):
    half_width = vector.shape[-1] // 2
    front_half = vector[..., :half_width]
    back_half = vector[..., half_width:]
    cos_rows = cosine[:, None, :]
    sin_rows = sine[:, None, :]
    return jnp.concatenate(
        [
            front_half * cos_rows - back_half * sin_rows,
            back_half * cos_rows + front_half * sin_rows,
        ],
        axis=-1,
    )


EXPERTS = 32
CAP = 48
WIDE = 128
FF = 512
ROWS = 16 * CAP
CHUNKS = 2


def exchange(blocks, axis, groups=None):
    return lax.all_to_all(
        blocks, axis, split_axis=0, concat_axis=0, tiled=True, axis_index_groups=groups
    )


def spread(block, axis, groups=None, count=8):
    return exchange(jnp.broadcast_to(block[None], (count,) + block.shape), axis, groups)


def parity_groups(count):
    return [list(range(core, count, 2)) for core in range(2)]


def core_swap(block, count):
    return lax.ppermute(block, "exp", [(i, i ^ 1) for i in range(count)])


def three_parts(value):
    high = value.astype(jnp.bfloat16)
    rest = value - high.astype(jnp.float32)
    middle = rest.astype(jnp.bfloat16)
    low = (rest - middle.astype(jnp.float32)).astype(jnp.bfloat16)
    return high, middle, low


def polynomial(gram, steps, precision):
    total = None
    for step in range(steps):
        square = jnp.matmul(gram, gram, precision=precision)
        eye = jnp.eye(gram.shape[-1], dtype=jnp.float32)
        factor = coef_one * eye + coef_two * gram + coef_three * square
        total = factor if total is None else jnp.matmul(factor, total, precision=precision)
        if step < steps - 1:
            gram = jnp.matmul(
                jnp.matmul(factor, gram, precision=precision), factor, precision=precision
            )
    return total


def step_weight(weight, ortho):
    return (
        weight.astype(jnp.float32) * (1.0 - muon_rate * decay_rate)
        - muon_rate * 0.2 * math.sqrt(D) * ortho
    )


def adam_update(param, first, second, grad, rate, decay):
    first = adam_one * first + (1.0 - adam_one) * grad
    second = adam_two * second + (1.0 - adam_two) * grad * grad
    fixed_one = first / (1.0 - adam_one**STEP)
    fixed_two = second / (1.0 - adam_two**STEP)
    return (
        first,
        second,
        param * (1.0 - rate * decay) - rate * fixed_one / (jnp.sqrt(fixed_two) + adam_eps),
    )


def contract_rows(left, right, precision=None):
    return lax.dot_general(
        left,
        right,
        (((0,), (0,)), ((), ())),
        preferred_element_type=jnp.float32,
        precision=precision,
    )


def contract_cols(left, right):
    return lax.dot_general(
        left, right, (((1,), (1,)), ((), ())), preferred_element_type=jnp.float32
    )


def mat(left, right):
    return jnp.dot(left, right, preferred_element_type=jnp.float32)


def head_blocks(sums, momenta, weights):
    fresh = mom_rate * momenta + sums
    width = fresh.shape[1]
    block = jnp.arange(width) // HD
    same = block[:, None] == block[None, :]
    gram = jnp.where(same, contract_rows(fresh, fresh, highest), 0.0)
    square = jnp.sum(jnp.where(jnp.eye(width, dtype=bool), gram, 0.0), axis=0, keepdims=True)
    total = jnp.sum(jnp.where(same, square.T, 0.0), axis=0, keepdims=True)
    scale = 1.0 / (jnp.sqrt(total) + 1e-07)
    poly = polynomial(gram * scale * scale.T, 5, highest)
    ortho = jnp.dot(fresh * scale, poly, precision=highest)
    return fresh, step_weight(weights, ortho)


def expert_kernel(own_ref, arrived_ref, grads_ref, weight_ref, made_ref, back_ref, sums_ref,
                  rows_ref, hidden_ref, dgate_ref, dup_ref, dy_ref):
    expert = own_ref[0] + pl.program_id(0)
    full_gate = weight_ref[:, 0, 0].reshape(D, FF)
    full_up = weight_ref[:, 1, 0].reshape(D, FF)
    full_down = weight_ref[:, 2, 0].reshape(D, FF)
    chunk = ROWS // CHUNKS
    seqs = chunk // CAP

    def forward(step, carry):
        first = pl.multiple_of(step * seqs, seqs)
        where = pl.ds(pl.multiple_of(step * chunk, chunk), chunk)
        both = arrived_ref[pl.ds(first, seqs), 0].reshape(chunk, D + WIDE)
        rows = both[:, :D]
        lane = lax.broadcasted_iota(jnp.int32, (chunk, WIDE), 1)
        pick = (lane % EXPERTS == expert) & (lane < 3 * EXPERTS)
        gate = jnp.sum(
            jnp.where(pick, both[:, D:].astype(jnp.float32), 0.0), axis=1, keepdims=True
        )
        gate_pre = mat(rows, full_gate)
        up_pre = mat(rows, full_up)
        sigma = jax.nn.sigmoid(gate_pre)
        activated = gate_pre * sigma
        hidden = (activated * up_pre).astype(jnp.bfloat16)
        made = contract_cols(hidden, full_down).astype(jnp.bfloat16)
        made_ref[pl.ds(first, seqs), 0] = made.reshape(seqs, CAP, D)
        grad_f32 = grads_ref[pl.ds(first, seqs), 0].reshape(chunk, D).astype(jnp.float32)
        grad_made = (gate * grad_f32).astype(jnp.bfloat16)
        grad_gate_value = jnp.sum(made.astype(jnp.float32) * grad_f32, axis=1, keepdims=True)
        grad_hidden = mat(grad_made, full_down)
        grad_gate_pre = (
            grad_hidden * up_pre * sigma * (1.0 + gate_pre * (1.0 - sigma))
        ).astype(jnp.bfloat16)
        grad_up_pre = (grad_hidden * activated).astype(jnp.bfloat16)
        back = contract_cols(grad_gate_pre, full_gate) + contract_cols(grad_up_pre, full_up)
        back_ref[pl.ds(first, seqs), 0, :, :D] = back.astype(jnp.bfloat16).reshape(seqs, CAP, D)
        high, middle, low = [
            part.astype(jnp.float32) for part in three_parts(grad_gate_value)
        ]
        slot = jnp.where(
            lane < EXPERTS, high, jnp.where(lane < 2 * EXPERTS, middle, low)
        )
        back_ref[pl.ds(first, seqs), 0, :, D:] = (
            jnp.where(pick, slot, 0.0).astype(jnp.bfloat16).reshape(seqs, CAP, WIDE)
        )
        rows_ref[where] = rows
        hidden_ref[where] = hidden
        dgate_ref[where] = grad_gate_pre
        dup_ref[where] = grad_up_pre
        dy_ref[where] = grad_made
        return carry

    lax.fori_loop(0, CHUNKS, forward, 0)
    parts = sums_ref.shape[0]
    width = D // parts

    def gradients(part, carry):
        columns = pl.ds(pl.multiple_of(part * width, width), width)
        rows = rows_ref[:, columns]
        sums_ref[part, 0, 0] = contract_rows(rows, dgate_ref[...]).astype(jnp.bfloat16)
        sums_ref[part, 1, 0] = contract_rows(rows, dup_ref[...]).astype(jnp.bfloat16)
        sums_ref[part, 2, 0] = contract_rows(dy_ref[:, columns], hidden_ref[...]).astype(
            jnp.bfloat16
        )
        return carry

    lax.fori_loop(0, parts, gradients, 0)


def expert_math(arrived, grad_rows, weights):
    seqs, per_group = arrived.shape[:2]
    own = (lax.axis_index("exp") * per_group).astype(jnp.int32).reshape(1)
    count = weights.shape[0]

    def rows_spec(width):
        return pl.BlockSpec((seqs, 1, CAP, width), lambda e, own: (0, e, 0, 0))

    weight_spec = pl.BlockSpec(
        (count, 3, 1, D // count, FF), lambda e, own: (0, 0, e, 0, 0)
    )
    return pl.pallas_call(
        expert_kernel,
        grid_spec=pltpu.PrefetchScalarGridSpec(
            num_scalar_prefetch=1,
            grid=(per_group,),
            in_specs=[rows_spec(D + WIDE), rows_spec(D), weight_spec],
            out_specs=[rows_spec(D), rows_spec(D + WIDE), weight_spec],
            scratch_shapes=[
                pltpu.VMEM((ROWS, D), jnp.bfloat16),
                pltpu.VMEM((ROWS, FF), jnp.bfloat16),
                pltpu.VMEM((ROWS, FF), jnp.bfloat16),
                pltpu.VMEM((ROWS, FF), jnp.bfloat16),
                pltpu.VMEM((ROWS, D), jnp.bfloat16),
            ],
        ),
        out_shape=[
            jax.ShapeDtypeStruct((seqs, per_group, CAP, D), jnp.bfloat16),
            jax.ShapeDtypeStruct((seqs, per_group, CAP, D + WIDE), jnp.bfloat16),
            jax.ShapeDtypeStruct(weights.shape, jnp.bfloat16),
        ],
        compiler_params=pltpu.CompilerParams(vmem_limit_bytes=56 * 2**20),
        cost_estimate=pl.CostEstimate(
            flops=18 * ROWS * per_group * D * FF,
            bytes_accessed=30 * 2**20,
            transcendentals=ROWS * per_group * FF,
        ),
        name="experts",
    )(own, arrived, grad_rows, weights)


def split_two(value):
    high = value.astype(jnp.bfloat16)
    return high, (value - high.astype(jnp.float32)).astype(jnp.bfloat16)


def mat_three(left, right):
    return mat(left[0], right[0]) + (mat(left[0], right[1]) + mat(left[1], right[0]))


def owner_kernel(matrix_ref, out_ref, gram_ref, total_ref):
    gram = contract_rows(matrix_ref[...], matrix_ref[...])
    width = gram_ref.shape[0]
    row = lax.broadcasted_iota(jnp.int32, (width, width), 0)
    column = lax.broadcasted_iota(jnp.int32, (width, width), 1)
    eye = (row == column).astype(jnp.float32)
    square = jnp.sum(jnp.sum(eye * gram, axis=1, keepdims=True), axis=0, keepdims=True)
    scale = 1.0 / (jnp.sqrt(square) + 1e-07)
    gram_ref[...] = gram * scale * scale
    total_ref[...] = eye

    def step(index, carry):
        gram = gram_ref[...]
        gram_two = split_two(gram)
        factor = coef_one * eye + coef_two * gram + coef_three * mat_three(gram_two, gram_two)
        factor_two = split_two(factor)
        total_ref[...] = mat_three(factor_two, split_two(total_ref[...]))
        gram_ref[...] = mat_three(split_two(mat_three(factor_two, gram_two)), factor_two)
        return carry

    lax.fori_loop(0, 5, step, 0)
    high, low = split_two(total_ref[...])
    matrix = matrix_ref[...]
    out_ref[...] = ((mat(matrix, high) + mat(matrix, low)) * scale).astype(out_ref.dtype)


def owner_orthogonal(stacked):
    rows, width = stacked.shape
    return pl.pallas_call(
        owner_kernel,
        out_shape=jax.ShapeDtypeStruct(stacked.shape, jnp.bfloat16),
        in_specs=[pl.BlockSpec(memory_space=pltpu.VMEM)],
        out_specs=pl.BlockSpec(memory_space=pltpu.VMEM),
        scratch_shapes=[
            pltpu.VMEM((width, width), jnp.float32),
            pltpu.VMEM((width, width), jnp.float32),
        ],
        compiler_params=pltpu.CompilerParams(vmem_limit_bytes=48 * 2**20),
        cost_estimate=pl.CostEstimate(
            flops=6 * (22 * width**3 + 2 * rows * width**2),
            bytes_accessed=4 * rows * width,
            transcendentals=0,
        ),
        name="owner",
    )(stacked)


def probabilities(queries, keys, first):
    scores = contract_cols(queries, keys) * HD ** (-0.5)
    token = lax.broadcasted_iota(jnp.int32, scores.shape, 0) % (scores.shape[0] // 2)
    key = lax.broadcasted_iota(jnp.int32, scores.shape, 1)
    scores = jnp.where(key <= first + token, scores, -1e30)
    running_max = jnp.max(scores, axis=1, keepdims=True)
    raised = jnp.exp(scores - running_max)
    return raised * (1.0 / jnp.sum(raised, axis=1, keepdims=True))


def two_heads(block, group):
    left = block[:, 2 * group * HD : (2 * group + 1) * HD]
    right = block[:, (2 * group + 1) * HD : (2 * group + 2) * HD]
    return jnp.concatenate([left, right], axis=0)


def side_by_side(stacked):
    half = stacked.shape[0] // 2
    return jnp.concatenate([stacked[:half], stacked[half:]], axis=1)


def attend_kernel(first_ref, query_ref, key_ref, value_ref, mixed_ref):
    queries, keys, values = query_ref[...], key_ref[...], value_ref[...]
    mixed = []
    for group in range(2):
        columns = slice(group * HD, (group + 1) * HD)
        weights = probabilities(two_heads(queries, group), keys[:, columns], first_ref[0])
        mixed.append(side_by_side(mat(weights.astype(jnp.bfloat16), values[:, columns])))
    mixed_ref[...] = jnp.concatenate(mixed, axis=1).astype(mixed_ref.dtype)


def attend_back_kernel(
    first_ref, query_ref, key_ref, value_ref, grad_ref, dquery_ref, dkey_ref, dvalue_ref
):
    queries, keys, values, grads = query_ref[...], key_ref[...], value_ref[...], grad_ref[...]
    dquery, dkey, dvalue = [], [], []
    for group in range(2):
        columns = slice(group * HD, (group + 1) * HD)
        query, grad = two_heads(queries, group), two_heads(grads, group)
        weights = probabilities(query, keys[:, columns], first_ref[0])
        grad_weights = contract_cols(grad, values[:, columns])
        inner = jnp.sum(weights * grad_weights, axis=1, keepdims=True)
        grad_scores = (weights * (grad_weights - inner)).astype(jnp.bfloat16)
        dquery.append(side_by_side(mat(grad_scores, keys[:, columns]) * HD ** (-0.5)))
        dkey.append(contract_rows(grad_scores, query) * HD ** (-0.5))
        dvalue.append(contract_rows(weights.astype(jnp.bfloat16), grad))
    dquery_ref[...] = jnp.concatenate(dquery, axis=1)
    dkey_ref[...] = jnp.concatenate(dkey, axis=1).astype(dkey_ref.dtype)
    dvalue_ref[...] = jnp.concatenate(dvalue, axis=1).astype(dvalue_ref.dtype)


def attention_call(kernel, operands, grads, first, name):
    queries, all_kv = operands
    rows, keys = queries.shape[0], all_kv.shape[0]
    steps = KV // 2
    wide = pl.BlockSpec((rows, 4 * HD), lambda g, first: (0, g))
    key_spec = pl.BlockSpec((keys, 2 * HD), lambda g, first: (0, g))
    value_spec = pl.BlockSpec((keys, 2 * HD), lambda g, first: (0, g + steps))
    if grads is None:
        arrays, specs = (queries, all_kv, all_kv), [wide, key_spec, value_spec]
        out_shape = jax.ShapeDtypeStruct(queries.shape, jnp.bfloat16)
        out_specs = wide
    else:
        arrays, specs = (queries, all_kv, all_kv, grads), [wide, key_spec, value_spec, wide]
        out_shape = [
            jax.ShapeDtypeStruct(queries.shape, jnp.float32),
            jax.ShapeDtypeStruct((keys, KV * HD), jnp.bfloat16),
            jax.ShapeDtypeStruct((keys, KV * HD), jnp.bfloat16),
        ]
        out_specs = [wide, key_spec, key_spec]
    factor = 4 if grads is None else 10
    return pl.pallas_call(
        kernel,
        grid_spec=pltpu.PrefetchScalarGridSpec(
            num_scalar_prefetch=1, grid=(steps,), in_specs=specs, out_specs=out_specs
        ),
        out_shape=out_shape,
        compiler_params=pltpu.CompilerParams(vmem_limit_bytes=48 * 2**20),
        cost_estimate=pl.CostEstimate(
            flops=factor * rows * keys * HEADS * HD,
            bytes_accessed=4 * 2**20,
            transcendentals=rows * keys * HEADS,
        ),
        name=name,
    )(first.astype(jnp.int32).reshape(1), *arrays)


def body(
    tokens,
    cotangent,
    routes,
    query_weight,
    kv_weight,
    output_weight,
    router,
    gains,
    gate_weight,
    up_weight,
    down_weight,
    query_momentum,
    kv_momentum,
    output_momentum,
    gate_momentum,
    up_momentum,
    down_momentum,
    router_first,
    router_second,
    gains_first,
    gains_second,
):
    bf16 = jnp.bfloat16
    ctx_count = lax.axis_size("ctx")
    exp_count = lax.axis_size("exp")
    exp_index = lax.axis_index("exp")
    row_count = tokens.shape[1]
    per_group = EXPERTS // exp_count
    inputs = tokens[0].astype(jnp.float32)
    grad_out = cotangent[0].astype(jnp.float32)
    route_ids = routes[0]

    packed = jnp.concatenate(
        [
            jnp.concatenate([query_weight, kv_weight], axis=1).T,
            router.astype(bf16).T,
            jnp.pad(gains.astype(bf16).reshape(1, -1), ((0, 0), (0, D - 2 * HD))),
            jnp.zeros((5, D), bf16),
        ],
        axis=0,
    )
    mine = spread(packed, "exp", parity_groups(exp_count), exp_count // 2)
    other = core_swap(mine, exp_count)
    even = (exp_index % 2 == 0)

    def ordered(first, last):
        left, right = mine[:, first:last], other[:, first:last]
        return jnp.stack(
            [jnp.where(even, left, right), jnp.where(even, right, left)], axis=1
        ).reshape((exp_count, last - first, D))

    full_qkv = ordered(0, 2 * HD).reshape(exp_count * 2 * HD, D)
    full_router = ordered(2 * HD, 2 * HD + per_group).reshape(EXPERTS, D)
    full_gains = ordered(2 * HD + per_group, 2 * HD + per_group + 1)[:, 0, : 2 * HD]
    full_gains = full_gains.reshape(exp_count, 2, HD).transpose(1, 0, 2).reshape(2, D)
    gain_one = full_gains[0].astype(jnp.float32)
    gain_two = full_gains[1].astype(jnp.float32)

    full_experts = lax.all_gather(
        jnp.stack([gate_weight, up_weight, down_weight]), "ctx", axis=0, tiled=False
    )
    full_output = lax.all_gather(output_weight.T, "exp", axis=0, tiled=True)

    expert_ids = jnp.arange(EXPERTS, dtype=jnp.int32)
    named = jnp.any(route_ids[:, :, None] == expert_ids[None, None, :], axis=1)
    named_low = named.astype(bf16)
    token_ids = jnp.arange(row_count)
    earlier = (token_ids[None, :] < token_ids[:, None]).astype(bf16)
    rank = mat(earlier, named_low)
    place = jnp.where(named, rank + 1.0, 0.0).astype(bf16)
    slot_ids = jnp.arange(EXPERTS * CAP, dtype=jnp.int32)
    widen = (slot_ids[None, :] // CAP == expert_ids[:, None]).astype(bf16)
    chosen_slot = mat(place, widen) == (slot_ids % CAP + 1).astype(jnp.float32)[None, :]
    select = chosen_slot.astype(bf16)

    sent_grads = contract_rows(select, cotangent[0]).astype(bf16)
    grad_rows = exchange(sent_grads.reshape(exp_count, per_group * CAP, D), "exp")

    inv_one = lax.rsqrt(jnp.mean(inputs * inputs, axis=-1, keepdims=True) + eps_norm)
    normed_one = (inputs * inv_one * gain_one).astype(bf16)
    all_normed = lax.all_gather(normed_one, "exp", axis=0, tiled=True)
    projected = contract_cols(normed_one, full_qkv).reshape(row_count, exp_count, 2 * HD)
    query_raw = projected[:, :, :HD]
    kv_raw = projected[:, :, HD:]
    first_row = lax.axis_index("ctx") * row_count
    cosine, sine = rope_tables(first_row, row_count)
    queries = rotate(query_raw, cosine, sine).astype(bf16)
    keys = rotate(kv_raw[:, :KV], cosine, sine).astype(bf16)
    values = kv_raw[:, KV:].astype(bf16)
    sent_kv = jnp.concatenate([keys, values], axis=1).reshape(row_count, 2 * KV * HD)
    all_kv = spread(sent_kv, "ctx", None, ctx_count).reshape(ctx_count * row_count, 2 * KV * HD)
    flat_queries = queries.reshape(row_count, HEADS * HD)
    mixed_low = attention_call(attend_kernel, (flat_queries, all_kv), None, first_row, "attend")
    head_mixed = exchange(
        mixed_low.reshape(row_count, exp_count, HD).transpose(1, 0, 2), "exp"
    ).reshape(exp_count * row_count, HD)
    attended = mat(mixed_low, full_output)
    residual = inputs + attended
    inv_two = lax.rsqrt(jnp.mean(residual * residual, axis=-1, keepdims=True) + eps_norm)
    normed_two = (residual * inv_two * gain_two).astype(bf16)
    logits = contract_cols(normed_two, full_router)
    gates = jax.nn.softmax(jnp.where(named, logits, -1e30), axis=-1)
    gates = jnp.where(named, gates, 0.0)
    gate_parts = three_parts(gates)
    extended = jnp.concatenate(
        [normed_two, *gate_parts, jnp.zeros((row_count, WIDE - 3 * EXPERTS), bf16)], axis=1
    )
    sent_rows = contract_rows(select, extended).astype(bf16)
    arrived = exchange(sent_rows.reshape(exp_count, per_group * CAP, D + WIDE), "exp")
    produced, back, expert_grads = expert_math(
        arrived.reshape(exp_count, per_group, CAP, D + WIDE),
        grad_rows.reshape(exp_count, per_group, CAP, D),
        full_experts,
    )
    returned = exchange(back.reshape(exp_count, per_group * CAP, D + WIDE), "exp")
    returned = returned.reshape(EXPERTS * CAP, D + WIDE)
    route_values = exchange(produced.reshape(exp_count, per_group * CAP, D), "exp")
    route_values = route_values.reshape(EXPERTS * CAP, D)
    expert_sums = exchange(expert_grads, "ctx")

    summed_back = mat(select, returned)
    tail = summed_back[:, D:]
    grad_gates = (
        tail[:, :EXPERTS] + tail[:, EXPERTS : 2 * EXPERTS] + tail[:, 2 * EXPERTS : 3 * EXPERTS]
    )
    grad_logits = (
        gates * (grad_gates - jnp.sum(gates * grad_gates, axis=-1, keepdims=True))
    ).astype(bf16)
    grad_normed_two = summed_back[:, :D] + mat(grad_logits, full_router)
    scaled_two = grad_normed_two * gain_two
    grad_gain_two = jnp.sum(grad_normed_two * residual * inv_two, axis=0)
    grad_residual = (
        grad_out
        + inv_two * scaled_two
        - residual * inv_two**3 * jnp.mean(scaled_two * residual, axis=-1, keepdims=True)
    )
    grad_attended = grad_residual.astype(bf16)
    all_attended = lax.all_gather(grad_attended, "exp", axis=0, tiled=True)
    grad_mixed = contract_cols(grad_attended, full_output).astype(bf16)
    grad_queries, key_terms, value_terms = attention_call(
        attend_back_kernel, (flat_queries, all_kv), grad_mixed, first_row, "attend_back"
    )
    kv_terms = jnp.concatenate([key_terms, value_terms], axis=1)
    kv_terms = exchange(kv_terms.reshape(ctx_count, row_count, 2 * KV * HD), "ctx")
    grad_query_raw = rotate(
        grad_queries.reshape(row_count, HEADS, HD), cosine, -sine
    ).astype(bf16)
    kv_sums = jnp.sum(kv_terms.astype(jnp.float32), axis=0).reshape(row_count, 2 * KV, HD)
    grad_key_raw = rotate(kv_sums[:, :KV], cosine, -sine).astype(bf16)
    grad_kv_raw = jnp.concatenate([grad_key_raw, kv_sums[:, KV:].astype(bf16)], axis=1)
    grad_projected = jnp.concatenate([grad_query_raw, grad_kv_raw], axis=2)
    head_grads = exchange(jnp.transpose(grad_projected, (1, 0, 2)), "exp")
    head_grads = head_grads.reshape(exp_count * row_count, 2 * HD)
    grad_normed_one = mat(grad_projected.reshape(row_count, exp_count * 2 * HD), full_qkv)
    scaled_one = grad_normed_one * gain_one
    grad_gain_one = jnp.sum(grad_normed_one * inputs * inv_one, axis=0)
    input_grad = (
        grad_residual
        + inv_one * scaled_one
        - inputs * inv_one**3 * jnp.mean(scaled_one * inputs, axis=-1, keepdims=True)
    )

    small = jnp.concatenate(
        [
            contract_rows(grad_logits, normed_two),
            grad_gain_one[None],
            grad_gain_two[None],
            jnp.zeros((6, D), jnp.float32),
        ],
        axis=0,
    )
    small = lax.psum(small, ("exp", "ctx"))
    sum_router = lax.dynamic_slice(small, (exp_index * per_group, 0), (per_group, D)).T
    sum_gains = lax.dynamic_slice(small, (EXPERTS, exp_index * HD), (2, HD))
    router_one, router_two, router_new = adam_update(
        router, router_first, router_second, sum_router, router_rate, decay_rate
    )
    gains_one, gains_two, gains_new = adam_update(
        gains, gains_first, gains_second, sum_gains, gain_rate, 0.0
    )

    part = jnp.concatenate(
        [contract_rows(all_normed, head_grads), contract_rows(all_attended, head_mixed)], axis=1
    )
    part = exchange(part.astype(bf16).reshape(ctx_count, D // ctx_count, 3 * HD), "ctx")
    part = jnp.sum(part.astype(jnp.float32), axis=0)
    sums = spread(part, "ctx", None, ctx_count).reshape(D, 3 * HD)
    head_fresh, head_new = head_blocks(
        sums,
        jnp.concatenate([query_momentum, kv_momentum, output_momentum], axis=1),
        jnp.concatenate([query_weight, kv_weight, output_weight], axis=1),
    )

    expert_sums = jnp.sum(expert_sums.astype(jnp.float32), axis=0)
    momenta = jnp.stack([gate_momentum, up_momentum, down_momentum])
    fresh = mom_rate * momenta + expert_sums
    matrix_count = 3 * per_group
    rows_each = fresh.shape[2]
    sent_fresh = jnp.pad(
        fresh.astype(bf16).reshape(matrix_count, rows_each, -1),
        ((0, ctx_count - matrix_count), (0, 0), (0, 0)),
    )
    owned = exchange(sent_fresh, "ctx").reshape(ctx_count * rows_each, -1)
    ortho = owner_orthogonal(owned).astype(bf16)
    ortho = exchange(ortho.reshape(ctx_count, rows_each, -1), "ctx")
    ortho = ortho[:matrix_count].reshape(fresh.shape).astype(jnp.float32)
    new = step_weight(jnp.stack([gate_weight, up_weight, down_weight]), ortho)

    gates_wide = [mat(part, widen) for part in gate_parts]
    block_value = residual
    for wide in gates_wide:
        weighted = jnp.where(chosen_slot, wide, 0.0).astype(bf16)
        block_value = block_value + mat(weighted, route_values)
    return (
        block_value.astype(bf16)[None],
        input_grad[None],
        head_fresh[:, :HD],
        head_new[:, :HD],
        head_fresh[:, HD : 2 * HD],
        head_new[:, HD : 2 * HD],
        head_fresh[:, 2 * HD :],
        head_new[:, 2 * HD :],
        fresh[0],
        new[0],
        fresh[1],
        new[1],
        fresh[2],
        new[2],
        router_one,
        router_two,
        router_new,
        gains_one,
        gains_two,
        gains_new,
    )


def solution(mesh):
    return jax.shard_map(
        body,
        mesh=mesh,
        in_specs=(
            P("exp", "ctx", None),
            P("exp", "ctx", None),
            P("exp", "ctx", None),
            P(None, "exp"),
            P(None, "exp"),
            P(None, "exp"),
            P(None, "exp"),
            P(None, "exp"),
            P("exp", "ctx", None),
            P("exp", "ctx", None),
            P("exp", "ctx", None),
            P(None, "exp"),
            P(None, "exp"),
            P(None, "exp"),
            P("exp", "ctx", None),
            P("exp", "ctx", None),
            P("exp", "ctx", None),
            P(None, "exp"),
            P(None, "exp"),
            P(None, "exp"),
            P(None, "exp"),
        ),
        out_specs=(
            P("exp", "ctx", None),
            P("exp", "ctx", None),
            P(None, "exp"),
            P(None, "exp"),
            P(None, "exp"),
            P(None, "exp"),
            P(None, "exp"),
            P(None, "exp"),
            P("exp", "ctx", None),
            P("exp", "ctx", None),
            P("exp", "ctx", None),
            P("exp", "ctx", None),
            P("exp", "ctx", None),
            P("exp", "ctx", None),
            P(None, "exp"),
            P(None, "exp"),
            P(None, "exp"),
            P(None, "exp"),
            P(None, "exp"),
            P(None, "exp"),
        ),
        check_vma=False,
    )
```

```python
import math

import jax
import jax.numpy as jnp
from jax import lax
from jax.experimental import pallas as pl
from jax.experimental.pallas import tpu as pltpu
from jax.sharding import PartitionSpec as P

D = 1024
HEADS = 16
KV = 8
HD = 64
TOP = 8
STEP = 10


eps_norm = 1e-05
rope_base = 10000.0
mom_rate = 0.95
muon_rate = 0.15
decay_rate = 0.1
adam_one = 0.9
adam_two = 0.95
adam_eps = 1e-08
router_rate = 0.015
gain_rate = 0.2
coef_one = 3.4445
coef_two = -4.775
coef_three = 2.0315
highest = lax.Precision.HIGHEST


def rope_tables(first_row, token_count):
    half_width = HD // 2
    frequency = rope_base ** (-jnp.arange(half_width, dtype=jnp.float32) * 2.0 / HD)
    position = (first_row + jnp.arange(token_count, dtype=jnp.int32)).astype(jnp.float32)
    angle_grid = position[:, None] * frequency[None, :]
    return (jnp.cos(angle_grid), jnp.sin(angle_grid))


def rotate(vector, cosine, sine):
    half_width = vector.shape[-1] // 2
    front_half = vector[..., :half_width]
    back_half = vector[..., half_width:]
    cos_rows = cosine[:, None, :]
    sin_rows = sine[:, None, :]
    return jnp.concatenate(
        [
            front_half * cos_rows - back_half * sin_rows,
            back_half * cos_rows + front_half * sin_rows,
        ],
        axis=-1,
    )


EXPERTS = 32
CAP = 48
WIDE = 128
FF = 512
ROWS = 16 * CAP
CHUNKS = 2
LOCAL = 128


def exchange(blocks, axis, groups=None):
    return lax.all_to_all(
        blocks, axis, split_axis=0, concat_axis=0, tiled=True, axis_index_groups=groups
    )


def spread(block, axis, groups=None, count=8):
    return exchange(jnp.broadcast_to(block[None], (count,) + block.shape), axis, groups)


def parity_groups(count):
    return [list(range(core, count, 2)) for core in range(2)]


def core_swap(block, count):
    return lax.ppermute(block, "exp", [(i, i ^ 1) for i in range(count)])


def ctx_move(block, up, other):
    pairs = [
        (2 * z + x, 2 * ((z + up) % 4) + (x ^ other)) for z in range(4) for x in range(2)
    ]
    return lax.ppermute(block, "ctx", pairs)


def gather_rows(block):
    same = jnp.stack([block, ctx_move(block, 0, 1)])
    below = ctx_move(same, 1, 0)
    above = ctx_move(same, 3, 0)
    return same, below, above, ctx_move(below[0], 1, 0), ctx_move(above[1], 3, 0)


def reduce_rows(same, up, down, far):
    total = same.astype(jnp.float32) + ctx_move(up, 1, 0).astype(jnp.float32)
    total = total + ctx_move(down, 3, 0).astype(jnp.float32)
    total = total + ctx_move(far, 2, 0).astype(jnp.float32)
    return total[0] + ctx_move(total[1].astype(jnp.bfloat16), 0, 1).astype(jnp.float32)


def three_parts(value):
    high = value.astype(jnp.bfloat16)
    rest = value - high.astype(jnp.float32)
    middle = rest.astype(jnp.bfloat16)
    low = (rest - middle.astype(jnp.float32)).astype(jnp.bfloat16)
    return high, middle, low


def polynomial(gram, steps, precision):
    total = None
    for step in range(steps):
        square = jnp.matmul(gram, gram, precision=precision)
        eye = jnp.eye(gram.shape[-1], dtype=jnp.float32)
        factor = coef_one * eye + coef_two * gram + coef_three * square
        total = factor if total is None else jnp.matmul(factor, total, precision=precision)
        if step < steps - 1:
            gram = jnp.matmul(
                jnp.matmul(factor, gram, precision=precision), factor, precision=precision
            )
    return total


def step_weight(weight, ortho):
    return (
        weight.astype(jnp.float32) * (1.0 - muon_rate * decay_rate)
        - muon_rate * 0.2 * math.sqrt(D) * ortho
    )


def adam_update(param, first, second, grad, rate, decay):
    first = adam_one * first + (1.0 - adam_one) * grad
    second = adam_two * second + (1.0 - adam_two) * grad * grad
    fixed_one = first / (1.0 - adam_one**STEP)
    fixed_two = second / (1.0 - adam_two**STEP)
    return (
        first,
        second,
        param * (1.0 - rate * decay) - rate * fixed_one / (jnp.sqrt(fixed_two) + adam_eps),
    )


def contract_rows(left, right, precision=None):
    return lax.dot_general(
        left,
        right,
        (((0,), (0,)), ((), ())),
        preferred_element_type=jnp.float32,
        precision=precision,
    )


def contract_cols(left, right):
    return lax.dot_general(
        left, right, (((1,), (1,)), ((), ())), preferred_element_type=jnp.float32
    )


def mat(left, right):
    return jnp.dot(left, right, preferred_element_type=jnp.float32)


def head_blocks(sums, momenta, weights):
    fresh = mom_rate * momenta + sums
    width = fresh.shape[1]
    block = jnp.arange(width) // HD
    same = block[:, None] == block[None, :]
    gram = jnp.where(same, contract_rows(fresh, fresh, highest), 0.0)
    square = jnp.sum(jnp.where(jnp.eye(width, dtype=bool), gram, 0.0), axis=0, keepdims=True)
    total = jnp.sum(jnp.where(same, square.T, 0.0), axis=0, keepdims=True)
    scale = 1.0 / (jnp.sqrt(total) + 1e-07)
    poly = polynomial(gram * scale * scale.T, 5, highest)
    ortho = jnp.dot(fresh * scale, poly, precision=highest)
    return fresh, step_weight(weights, ortho)


def expert_kernel(own_ref, arrived_ref, grads_ref, same_ref, below_ref, above_ref, far_ref, far_two_ref,
                  made_ref, back_ref, sums_ref, sums_up_ref, sums_down_ref, sums_far_ref,
                  weight_ref, rows_ref, hidden_ref, dgate_ref, dup_ref, dy_ref):
    expert = own_ref[0] + pl.program_id(0)
    level, side = own_ref[1], own_ref[2]
    width = D // 8

    def part(up, other):
        index = 2 * lax.rem(level + up, 4) + (1 - side if other else side)
        return pl.ds(pl.multiple_of(index * width, width), width)

    for up, ref in ((0, same_ref), (3, below_ref), (1, above_ref)):
        for other in range(2):
            for kind in range(3):
                weight_ref[kind, part(up, other)] = ref[other, kind, 0]
    for kind in range(3):
        weight_ref[kind, part(2, 0)] = far_ref[kind, 0]
        weight_ref[kind, part(2, 1)] = far_two_ref[kind, 0]
    full_gate, full_up, full_down = weight_ref[0], weight_ref[1], weight_ref[2]
    chunk = ROWS // CHUNKS
    seqs = chunk // CAP

    def forward(step, carry):
        first = pl.multiple_of(step * seqs, seqs)
        where = pl.ds(pl.multiple_of(step * chunk, chunk), chunk)
        both = arrived_ref[pl.ds(first, seqs), 0].reshape(chunk, D + WIDE)
        rows = both[:, :D]
        lane = lax.broadcasted_iota(jnp.int32, (chunk, WIDE), 1)
        pick = (lane % EXPERTS == expert) & (lane < 3 * EXPERTS)
        gate = jnp.sum(
            jnp.where(pick, both[:, D:].astype(jnp.float32), 0.0), axis=1, keepdims=True
        )
        gate_pre = mat(rows, full_gate)
        up_pre = mat(rows, full_up)
        sigma = jax.nn.sigmoid(gate_pre)
        activated = gate_pre * sigma
        hidden = (activated * up_pre).astype(jnp.bfloat16)
        made = contract_cols(hidden, full_down).astype(jnp.bfloat16)
        made_ref[pl.ds(first, seqs), 0] = made.reshape(seqs, CAP, D)
        slot_ids = lax.broadcasted_iota(jnp.int32, (LOCAL, CAP), 1).astype(jnp.float32) + 1.0
        token_lane = lax.broadcasted_iota(jnp.int32, (LOCAL, WIDE), 1)
        taken = []
        for seq in range(seqs):
            source = grads_ref[first + seq]
            places = jnp.where(token_lane == expert, source[:, D:].astype(jnp.float32), 0.0)
            chosen = jnp.sum(places, axis=1, keepdims=True) == slot_ids
            taken.append(contract_rows(chosen.astype(jnp.bfloat16), source[:, :D]))
        grad_f32 = jnp.concatenate(taken, axis=0)
        grad_made = (gate * grad_f32).astype(jnp.bfloat16)
        grad_gate_value = jnp.sum(made.astype(jnp.float32) * grad_f32, axis=1, keepdims=True)
        grad_hidden = mat(grad_made, full_down)
        grad_gate_pre = (
            grad_hidden * up_pre * sigma * (1.0 + gate_pre * (1.0 - sigma))
        ).astype(jnp.bfloat16)
        grad_up_pre = (grad_hidden * activated).astype(jnp.bfloat16)
        back = contract_cols(grad_gate_pre, full_gate) + contract_cols(grad_up_pre, full_up)
        back_ref[pl.ds(first, seqs), 0, :, :D] = back.astype(jnp.bfloat16).reshape(seqs, CAP, D)
        high, middle, low = [
            part.astype(jnp.float32) for part in three_parts(grad_gate_value)
        ]
        slot = jnp.where(
            lane < EXPERTS, high, jnp.where(lane < 2 * EXPERTS, middle, low)
        )
        back_ref[pl.ds(first, seqs), 0, :, D:] = (
            jnp.where(pick, slot, 0.0).astype(jnp.bfloat16).reshape(seqs, CAP, WIDE)
        )
        rows_ref[where] = rows
        hidden_ref[where] = hidden
        dgate_ref[where] = grad_gate_pre
        dup_ref[where] = grad_up_pre
        dy_ref[where] = grad_made
        return carry

    lax.fori_loop(0, CHUNKS, forward, 0)
    for up, ref in ((0, sums_ref), (1, sums_up_ref), (3, sums_down_ref), (2, sums_far_ref)):
        for other in range(2):
            columns = part(up, other)
            rows = rows_ref[:, columns]
            ref[other, 0, 0] = contract_rows(rows, dgate_ref[...]).astype(jnp.bfloat16)
            ref[other, 1, 0] = contract_rows(rows, dup_ref[...]).astype(jnp.bfloat16)
            ref[other, 2, 0] = contract_rows(dy_ref[:, columns], hidden_ref[...]).astype(
                jnp.bfloat16
            )


def expert_math(arrived, all_grads, weights):
    seqs, per_group = arrived.shape[:2]
    place = lax.axis_index("ctx")
    own = jnp.stack([lax.axis_index("exp") * per_group, place // 2, place % 2]).astype(jnp.int32)
    rows_each = D // 8

    def rows_spec(width):
        return pl.BlockSpec((seqs, 1, CAP, width), lambda e, own: (0, e, 0, 0))

    two = pl.BlockSpec((2, 3, 1, rows_each, FF), lambda e, own: (0, 0, e, 0, 0))
    one = pl.BlockSpec((3, 1, rows_each, FF), lambda e, own: (0, e, 0, 0))
    whole = pl.BlockSpec(all_grads.shape, lambda e, own: (0, 0, 0))
    return pl.pallas_call(
        expert_kernel,
        grid_spec=pltpu.PrefetchScalarGridSpec(
            num_scalar_prefetch=1,
            grid=(per_group,),
            in_specs=[rows_spec(D + WIDE), whole, two, two, two, one, one],
            out_specs=[rows_spec(D), rows_spec(D + WIDE), two, two, two, two],
            scratch_shapes=[
                pltpu.VMEM((3, D, FF), jnp.bfloat16),
                pltpu.VMEM((ROWS, D), jnp.bfloat16),
                pltpu.VMEM((ROWS, FF), jnp.bfloat16),
                pltpu.VMEM((ROWS, FF), jnp.bfloat16),
                pltpu.VMEM((ROWS, FF), jnp.bfloat16),
                pltpu.VMEM((ROWS, D), jnp.bfloat16),
            ],
        ),
        out_shape=[
            jax.ShapeDtypeStruct((seqs, per_group, CAP, D), jnp.bfloat16),
            jax.ShapeDtypeStruct((seqs, per_group, CAP, D + WIDE), jnp.bfloat16),
        ]
        + [jax.ShapeDtypeStruct((2, 3, per_group, rows_each, FF), jnp.bfloat16)] * 4,
        compiler_params=pltpu.CompilerParams(vmem_limit_bytes=56 * 2**20),
        cost_estimate=pl.CostEstimate(
            flops=18 * ROWS * per_group * D * FF,
            bytes_accessed=30 * 2**20,
            transcendentals=ROWS * per_group * FF,
        ),
        name="experts",
    )(own, arrived, all_grads, *weights)


def split_two(value):
    high = value.astype(jnp.bfloat16)
    return high, (value - high.astype(jnp.float32)).astype(jnp.bfloat16)


def mat_three(left, right):
    return mat(left[0], right[0]) + (mat(left[0], right[1]) + mat(left[1], right[0]))


def owner_kernel(matrix_ref, out_ref, gram_ref, total_ref):
    gram = contract_rows(matrix_ref[...], matrix_ref[...])
    width = gram_ref.shape[0]
    row = lax.broadcasted_iota(jnp.int32, (width, width), 0)
    column = lax.broadcasted_iota(jnp.int32, (width, width), 1)
    eye = (row == column).astype(jnp.float32)
    square = jnp.sum(jnp.sum(eye * gram, axis=1, keepdims=True), axis=0, keepdims=True)
    scale = 1.0 / (jnp.sqrt(square) + 1e-07)
    gram_ref[...] = gram * scale * scale
    total_ref[...] = eye

    def step(index, carry):
        gram = gram_ref[...]
        gram_two = split_two(gram)
        factor = coef_one * eye + coef_two * gram + coef_three * mat_three(gram_two, gram_two)
        factor_two = split_two(factor)
        total_ref[...] = mat_three(factor_two, split_two(total_ref[...]))
        gram_ref[...] = mat_three(split_two(mat_three(factor_two, gram_two)), factor_two)
        return carry

    lax.fori_loop(0, 5, step, 0)
    high, low = split_two(total_ref[...])
    matrix = matrix_ref[...]
    out_ref[...] = ((mat(matrix, high) + mat(matrix, low)) * scale).astype(out_ref.dtype)


def owner_orthogonal(stacked):
    rows, width = stacked.shape
    return pl.pallas_call(
        owner_kernel,
        out_shape=jax.ShapeDtypeStruct(stacked.shape, jnp.bfloat16),
        in_specs=[pl.BlockSpec(memory_space=pltpu.VMEM)],
        out_specs=pl.BlockSpec(memory_space=pltpu.VMEM),
        scratch_shapes=[
            pltpu.VMEM((width, width), jnp.float32),
            pltpu.VMEM((width, width), jnp.float32),
        ],
        compiler_params=pltpu.CompilerParams(vmem_limit_bytes=48 * 2**20),
        cost_estimate=pl.CostEstimate(
            flops=6 * (22 * width**3 + 2 * rows * width**2),
            bytes_accessed=4 * rows * width,
            transcendentals=0,
        ),
        name="owner",
    )(stacked)


def probabilities(queries, keys, first):
    scores = contract_cols(queries, keys) * HD ** (-0.5)
    token = lax.broadcasted_iota(jnp.int32, scores.shape, 0) % (scores.shape[0] // 2)
    key = lax.broadcasted_iota(jnp.int32, scores.shape, 1)
    scores = jnp.where(key <= first + token, scores, -1e30)
    running_max = jnp.max(scores, axis=1, keepdims=True)
    raised = jnp.exp(scores - running_max)
    return raised * (1.0 / jnp.sum(raised, axis=1, keepdims=True))


def two_heads(block, group):
    left = block[:, 2 * group * HD : (2 * group + 1) * HD]
    right = block[:, (2 * group + 1) * HD : (2 * group + 2) * HD]
    return jnp.concatenate([left, right], axis=0)


def side_by_side(stacked):
    half = stacked.shape[0] // 2
    return jnp.concatenate([stacked[:half], stacked[half:]], axis=1)


def attend_kernel(first_ref, query_ref, key_ref, value_ref, mixed_ref):
    queries, keys, values = query_ref[...], key_ref[...], value_ref[...]
    mixed = []
    for group in range(2):
        columns = slice(group * HD, (group + 1) * HD)
        weights = probabilities(two_heads(queries, group), keys[:, columns], first_ref[0])
        mixed.append(side_by_side(mat(weights.astype(jnp.bfloat16), values[:, columns])))
    mixed_ref[...] = jnp.concatenate(mixed, axis=1).astype(mixed_ref.dtype)


def attend_back_kernel(
    first_ref, query_ref, key_ref, value_ref, grad_ref, dquery_ref, dkey_ref, dvalue_ref
):
    queries, keys, values, grads = query_ref[...], key_ref[...], value_ref[...], grad_ref[...]
    dquery, dkey, dvalue = [], [], []
    for group in range(2):
        columns = slice(group * HD, (group + 1) * HD)
        query, grad = two_heads(queries, group), two_heads(grads, group)
        weights = probabilities(query, keys[:, columns], first_ref[0])
        grad_weights = contract_cols(grad, values[:, columns])
        inner = jnp.sum(weights * grad_weights, axis=1, keepdims=True)
        grad_scores = (weights * (grad_weights - inner)).astype(jnp.bfloat16)
        dquery.append(side_by_side(mat(grad_scores, keys[:, columns]) * HD ** (-0.5)))
        dkey.append(contract_rows(grad_scores, query) * HD ** (-0.5))
        dvalue.append(contract_rows(weights.astype(jnp.bfloat16), grad))
    dquery_ref[...] = jnp.concatenate(dquery, axis=1)
    dkey_ref[...] = jnp.concatenate(dkey, axis=1).astype(dkey_ref.dtype)
    dvalue_ref[...] = jnp.concatenate(dvalue, axis=1).astype(dvalue_ref.dtype)


def attention_call(kernel, operands, grads, first, name):
    queries, all_kv = operands
    rows, keys = queries.shape[0], all_kv.shape[0]
    steps = KV // 2
    wide = pl.BlockSpec((rows, 4 * HD), lambda g, first: (0, g))
    key_spec = pl.BlockSpec((keys, 2 * HD), lambda g, first: (0, g))
    value_spec = pl.BlockSpec((keys, 2 * HD), lambda g, first: (0, g + steps))
    if grads is None:
        arrays, specs = (queries, all_kv, all_kv), [wide, key_spec, value_spec]
        out_shape = jax.ShapeDtypeStruct(queries.shape, jnp.bfloat16)
        out_specs = wide
    else:
        arrays, specs = (queries, all_kv, all_kv, grads), [wide, key_spec, value_spec, wide]
        out_shape = [
            jax.ShapeDtypeStruct(queries.shape, jnp.float32),
            jax.ShapeDtypeStruct((keys, KV * HD), jnp.bfloat16),
            jax.ShapeDtypeStruct((keys, KV * HD), jnp.bfloat16),
        ]
        out_specs = [wide, key_spec, key_spec]
    factor = 4 if grads is None else 10
    return pl.pallas_call(
        kernel,
        grid_spec=pltpu.PrefetchScalarGridSpec(
            num_scalar_prefetch=1, grid=(steps,), in_specs=specs, out_specs=out_specs
        ),
        out_shape=out_shape,
        compiler_params=pltpu.CompilerParams(vmem_limit_bytes=48 * 2**20),
        cost_estimate=pl.CostEstimate(
            flops=factor * rows * keys * HEADS * HD,
            bytes_accessed=4 * 2**20,
            transcendentals=rows * keys * HEADS,
        ),
        name=name,
    )(first.astype(jnp.int32).reshape(1), *arrays)


def body(
    tokens,
    cotangent,
    routes,
    query_weight,
    kv_weight,
    output_weight,
    router,
    gains,
    gate_weight,
    up_weight,
    down_weight,
    query_momentum,
    kv_momentum,
    output_momentum,
    gate_momentum,
    up_momentum,
    down_momentum,
    router_first,
    router_second,
    gains_first,
    gains_second,
):
    bf16 = jnp.bfloat16
    ctx_count = lax.axis_size("ctx")
    exp_count = lax.axis_size("exp")
    exp_index = lax.axis_index("exp")
    row_count = tokens.shape[1]
    per_group = EXPERTS // exp_count
    inputs = tokens[0].astype(jnp.float32)
    grad_out = cotangent[0].astype(jnp.float32)
    route_ids = routes[0]

    packed = jnp.concatenate(
        [
            jnp.concatenate([query_weight, kv_weight], axis=1).T,
            router.astype(bf16).T,
            jnp.pad(gains.astype(bf16).reshape(1, -1), ((0, 0), (0, D - 2 * HD))),
            jnp.zeros((5, D), bf16),
        ],
        axis=0,
    )
    mine = spread(packed, "exp", parity_groups(exp_count), exp_count // 2)
    other = core_swap(mine, exp_count)
    even = (exp_index % 2 == 0)

    def ordered(first, last):
        left, right = mine[:, first:last], other[:, first:last]
        return jnp.stack(
            [jnp.where(even, left, right), jnp.where(even, right, left)], axis=1
        ).reshape((exp_count, last - first, D))

    full_qkv = ordered(0, 2 * HD).reshape(exp_count * 2 * HD, D)
    full_router = ordered(2 * HD, 2 * HD + per_group).reshape(EXPERTS, D)
    full_gains = ordered(2 * HD + per_group, 2 * HD + per_group + 1)[:, 0, : 2 * HD]
    full_gains = full_gains.reshape(exp_count, 2, HD).transpose(1, 0, 2).reshape(2, D)
    gain_one = full_gains[0].astype(jnp.float32)
    gain_two = full_gains[1].astype(jnp.float32)

    full_experts = gather_rows(jnp.stack([gate_weight, up_weight, down_weight]))
    full_output = lax.all_gather(output_weight.T, "exp", axis=0, tiled=True)

    expert_ids = jnp.arange(EXPERTS, dtype=jnp.int32)
    named = jnp.any(route_ids[:, :, None] == expert_ids[None, None, :], axis=1)
    named_low = named.astype(bf16)
    token_ids = jnp.arange(row_count)
    earlier = (token_ids[None, :] < token_ids[:, None]).astype(bf16)
    rank = mat(earlier, named_low)
    place = jnp.where(named, rank + 1.0, 0.0).astype(bf16)
    slot_ids = jnp.arange(EXPERTS * CAP, dtype=jnp.int32)
    widen = (slot_ids[None, :] // CAP == expert_ids[:, None]).astype(bf16)
    chosen_slot = mat(place, widen) == (slot_ids % CAP + 1).astype(jnp.float32)[None, :]
    select = chosen_slot.astype(bf16)

    sent_grads = jnp.concatenate(
        [cotangent[0], place, jnp.zeros((row_count, WIDE - EXPERTS), bf16)], axis=1
    )
    all_grads = lax.all_gather(sent_grads, "exp", axis=0, tiled=False)

    inv_one = lax.rsqrt(jnp.mean(inputs * inputs, axis=-1, keepdims=True) + eps_norm)
    normed_one = (inputs * inv_one * gain_one).astype(bf16)
    projected = contract_cols(normed_one, full_qkv).reshape(row_count, exp_count, 2 * HD)
    query_raw = projected[:, :, :HD]
    kv_raw = projected[:, :, HD:]
    first_row = lax.axis_index("ctx") * row_count
    cosine, sine = rope_tables(first_row, row_count)
    queries = rotate(query_raw, cosine, sine).astype(bf16)
    keys = rotate(kv_raw[:, :KV], cosine, sine).astype(bf16)
    values = kv_raw[:, KV:].astype(bf16)
    sent_kv = jnp.concatenate([keys, values], axis=1).reshape(row_count, 2 * KV * HD)
    all_kv = spread(sent_kv, "ctx", None, ctx_count).reshape(ctx_count * row_count, 2 * KV * HD)
    flat_queries = queries.reshape(row_count, HEADS * HD)
    mixed_low = attention_call(attend_kernel, (flat_queries, all_kv), None, first_row, "attend")
    sent_mixed = mixed_low.reshape(row_count, exp_count, HD).transpose(1, 0, 2)
    sent_mixed = sent_mixed.reshape(exp_count, row_count * HD // D, D)
    attended = mat(mixed_low, full_output)
    residual = inputs + attended
    inv_two = lax.rsqrt(jnp.mean(residual * residual, axis=-1, keepdims=True) + eps_norm)
    normed_two = (residual * inv_two * gain_two).astype(bf16)
    logits = contract_cols(normed_two, full_router)
    gates = jax.nn.softmax(jnp.where(named, logits, -1e30), axis=-1)
    gates = jnp.where(named, gates, 0.0)
    gate_parts = three_parts(gates)
    extended = jnp.concatenate(
        [normed_two, *gate_parts, jnp.zeros((row_count, WIDE - 3 * EXPERTS), bf16)], axis=1
    )
    sent_rows = contract_rows(select, extended).astype(bf16)
    arrived = exchange(sent_rows.reshape(exp_count, per_group * CAP, D + WIDE), "exp")
    later_normed, arrived = lax.optimization_barrier((normed_one, arrived))
    all_normed = lax.all_gather(later_normed, "exp", axis=0, tiled=True)
    produced, back, *expert_grads = expert_math(
        arrived.reshape(exp_count, per_group, CAP, D + WIDE), all_grads, full_experts
    )
    returned = exchange(back.reshape(exp_count, per_group * CAP, D + WIDE), "exp")
    returned = returned.reshape(EXPERTS * CAP, D + WIDE)
    route_values = exchange(
        jnp.concatenate([produced.reshape(exp_count, per_group * CAP, D), sent_mixed], axis=1),
        "exp",
    )
    head_mixed = route_values[:, per_group * CAP :].reshape(exp_count * row_count, HD)
    route_values = route_values[:, : per_group * CAP].reshape(EXPERTS * CAP, D)
    expert_sums = reduce_rows(*expert_grads)

    summed_back = mat(select, returned)
    tail = summed_back[:, D:]
    grad_gates = (
        tail[:, :EXPERTS] + tail[:, EXPERTS : 2 * EXPERTS] + tail[:, 2 * EXPERTS : 3 * EXPERTS]
    )
    grad_logits = (
        gates * (grad_gates - jnp.sum(gates * grad_gates, axis=-1, keepdims=True))
    ).astype(bf16)
    grad_normed_two = summed_back[:, :D] + mat(grad_logits, full_router)
    scaled_two = grad_normed_two * gain_two
    grad_gain_two = jnp.sum(grad_normed_two * residual * inv_two, axis=0)
    grad_residual = (
        grad_out
        + inv_two * scaled_two
        - residual * inv_two**3 * jnp.mean(scaled_two * residual, axis=-1, keepdims=True)
    )
    grad_attended = grad_residual.astype(bf16)
    all_attended = lax.all_gather(grad_attended, "exp", axis=0, tiled=True)
    grad_mixed = contract_cols(grad_attended, full_output).astype(bf16)
    grad_queries, key_terms, value_terms = attention_call(
        attend_back_kernel, (flat_queries, all_kv), grad_mixed, first_row, "attend_back"
    )
    kv_terms = jnp.concatenate([key_terms, value_terms], axis=1)
    kv_terms = exchange(kv_terms.reshape(ctx_count, row_count, 2 * KV * HD), "ctx")
    grad_query_raw = rotate(
        grad_queries.reshape(row_count, HEADS, HD), cosine, -sine
    ).astype(bf16)
    kv_sums = jnp.sum(kv_terms.astype(jnp.float32), axis=0).reshape(row_count, 2 * KV, HD)
    grad_key_raw = rotate(kv_sums[:, :KV], cosine, -sine).astype(bf16)
    grad_kv_raw = jnp.concatenate([grad_key_raw, kv_sums[:, KV:].astype(bf16)], axis=1)
    grad_projected = jnp.concatenate([grad_query_raw, grad_kv_raw], axis=2)
    grad_normed_one = mat(grad_projected.reshape(row_count, exp_count * 2 * HD), full_qkv)
    scaled_one = grad_normed_one * gain_one
    grad_gain_one = jnp.sum(grad_normed_one * inputs * inv_one, axis=0)
    input_grad = (
        grad_residual
        + inv_one * scaled_one
        - inputs * inv_one**3 * jnp.mean(scaled_one * inputs, axis=-1, keepdims=True)
    )

    small_rows = (per_group * D + 2 * HD) // (2 * HD)
    small = jnp.concatenate(
        [
            contract_rows(grad_logits, normed_two).reshape(exp_count, -1, 2 * HD),
            jnp.stack([grad_gain_one, grad_gain_two])
            .reshape(2, exp_count, HD)
            .transpose(1, 0, 2)
            .reshape(exp_count, 1, 2 * HD),
            jnp.zeros((exp_count, 7, 2 * HD), jnp.float32),
        ],
        axis=1,
    ).astype(bf16)
    head_grads = exchange(
        jnp.concatenate([jnp.transpose(grad_projected, (1, 0, 2)), small], axis=1), "exp"
    )
    small = jnp.sum(head_grads[:, row_count : row_count + small_rows].astype(jnp.float32), axis=0)
    head_grads = head_grads[:, :row_count].reshape(exp_count * row_count, 2 * HD)

    part = jnp.concatenate(
        [contract_rows(all_normed, head_grads), contract_rows(all_attended, head_mixed)], axis=1
    )
    small = jnp.pad(
        small.reshape(2 * small_rows, HD), ((0, D // ctx_count - 2 * small_rows), (0, 0))
    )
    part = jnp.concatenate(
        [
            part.astype(bf16).reshape(ctx_count, D // ctx_count, 3 * HD),
            jnp.broadcast_to(small.astype(bf16)[None], (ctx_count,) + small.shape),
        ],
        axis=2,
    )
    part = jnp.sum(exchange(part, "ctx").astype(jnp.float32), axis=0)
    sums = spread(part[:, : 3 * HD].astype(bf16), "ctx", None, ctx_count)
    sums = sums.reshape(D, 3 * HD).astype(jnp.float32)
    small = part[: 2 * small_rows, 3 * HD :].reshape(small_rows, 2 * HD)
    sum_router = small[:-1].reshape(per_group, D).T
    sum_gains = small[-1].reshape(2, HD)
    router_one, router_two, router_new = adam_update(
        router, router_first, router_second, sum_router, router_rate, decay_rate
    )
    gains_one, gains_two, gains_new = adam_update(
        gains, gains_first, gains_second, sum_gains, gain_rate, 0.0
    )

    head_fresh, head_new = head_blocks(
        sums,
        jnp.concatenate([query_momentum, kv_momentum, output_momentum], axis=1),
        jnp.concatenate([query_weight, kv_weight, output_weight], axis=1),
    )

    momenta = jnp.stack([gate_momentum, up_momentum, down_momentum])
    fresh = mom_rate * momenta + expert_sums
    matrix_count = 3 * per_group
    rows_each = fresh.shape[2]
    sent_fresh = jnp.pad(
        fresh.astype(bf16).reshape(matrix_count, rows_each, -1),
        ((0, ctx_count - matrix_count), (0, 0), (0, 0)),
    )
    owned = exchange(sent_fresh, "ctx").reshape(ctx_count * rows_each, -1)
    ortho = owner_orthogonal(owned).astype(bf16)
    ortho = exchange(ortho.reshape(ctx_count, rows_each, -1), "ctx")
    ortho = ortho[:matrix_count].reshape(fresh.shape).astype(jnp.float32)
    new = step_weight(jnp.stack([gate_weight, up_weight, down_weight]), ortho)

    gates_wide = [mat(part, widen) for part in gate_parts]
    block_value = residual
    for wide in gates_wide:
        weighted = jnp.where(chosen_slot, wide, 0.0).astype(bf16)
        block_value = block_value + mat(weighted, route_values)
    return (
        block_value.astype(bf16)[None],
        input_grad[None],
        head_fresh[:, :HD],
        head_new[:, :HD],
        head_fresh[:, HD : 2 * HD],
        head_new[:, HD : 2 * HD],
        head_fresh[:, 2 * HD :],
        head_new[:, 2 * HD :],
        fresh[0],
        new[0],
        fresh[1],
        new[1],
        fresh[2],
        new[2],
        router_one,
        router_two,
        router_new,
        gains_one,
        gains_two,
        gains_new,
    )


def solution(mesh):
    return jax.shard_map(
        body,
        mesh=mesh,
        in_specs=(
            P("exp", "ctx", None),
            P("exp", "ctx", None),
            P("exp", "ctx", None),
            P(None, "exp"),
            P(None, "exp"),
            P(None, "exp"),
            P(None, "exp"),
            P(None, "exp"),
            P("exp", "ctx", None),
            P("exp", "ctx", None),
            P("exp", "ctx", None),
            P(None, "exp"),
            P(None, "exp"),
            P(None, "exp"),
            P("exp", "ctx", None),
            P("exp", "ctx", None),
            P("exp", "ctx", None),
            P(None, "exp"),
            P(None, "exp"),
            P(None, "exp"),
            P(None, "exp"),
        ),
        out_specs=(
            P("exp", "ctx", None),
            P("exp", "ctx", None),
            P(None, "exp"),
            P(None, "exp"),
            P(None, "exp"),
            P(None, "exp"),
            P(None, "exp"),
            P(None, "exp"),
            P("exp", "ctx", None),
            P("exp", "ctx", None),
            P("exp", "ctx", None),
            P("exp", "ctx", None),
            P("exp", "ctx", None),
            P("exp", "ctx", None),
            P(None, "exp"),
            P(None, "exp"),
            P(None, "exp"),
            P(None, "exp"),
            P(None, "exp"),
            P(None, "exp"),
        ),
        check_vma=False,
    )
```

```python
import math

import jax
import jax.numpy as jnp
from jax import lax
from jax.experimental import pallas as pl
from jax.experimental.pallas import tpu as pltpu
from jax.sharding import PartitionSpec as P

D = 1024
HEADS = 16
KV = 8
HD = 64
TOP = 8
STEP = 10


eps_norm = 1e-05
rope_base = 10000.0
mom_rate = 0.95
muon_rate = 0.15
decay_rate = 0.1
adam_one = 0.9
adam_two = 0.95
adam_eps = 1e-08
router_rate = 0.015
gain_rate = 0.2
coef_one = 3.4445
coef_two = -4.775
coef_three = 2.0315
highest = lax.Precision.HIGHEST


def rope_tables(first_row, token_count):
    half_width = HD // 2
    frequency = rope_base ** (-jnp.arange(half_width, dtype=jnp.float32) * 2.0 / HD)
    position = (first_row + jnp.arange(token_count, dtype=jnp.int32)).astype(jnp.float32)
    angle_grid = position[:, None] * frequency[None, :]
    return (jnp.cos(angle_grid), jnp.sin(angle_grid))


def rotate(vector, cosine, sine):
    half_width = vector.shape[-1] // 2
    front_half = vector[..., :half_width]
    back_half = vector[..., half_width:]
    cos_rows = cosine[:, None, :]
    sin_rows = sine[:, None, :]
    return jnp.concatenate(
        [
            front_half * cos_rows - back_half * sin_rows,
            back_half * cos_rows + front_half * sin_rows,
        ],
        axis=-1,
    )


EXPERTS = 32
CAP = 48
WIDE = 128
FF = 512
ROWS = 16 * CAP
CHUNKS = 2
LOCAL = 128


def exchange(blocks, axis, groups=None):
    return lax.all_to_all(
        blocks, axis, split_axis=0, concat_axis=0, tiled=True, axis_index_groups=groups
    )


def spread(block, axis, groups=None, count=8):
    return exchange(jnp.broadcast_to(block[None], (count,) + block.shape), axis, groups)


def parity_groups(count):
    return [list(range(core, count, 2)) for core in range(2)]


def core_swap(block, count):
    return lax.ppermute(block, "exp", [(i, i ^ 1) for i in range(count)])


def ctx_move(block, up, other):
    pairs = [
        (2 * z + x, 2 * ((z + up) % 4) + (x ^ other)) for z in range(4) for x in range(2)
    ]
    return lax.ppermute(block, "ctx", pairs)


def after(value, *others):
    return lax.optimization_barrier((value,) + others)[0]


def three_parts(value):
    high = value.astype(jnp.bfloat16)
    rest = value - high.astype(jnp.float32)
    middle = rest.astype(jnp.bfloat16)
    low = (rest - middle.astype(jnp.float32)).astype(jnp.bfloat16)
    return high, middle, low


def polynomial(gram, steps, precision):
    total = None
    for step in range(steps):
        square = jnp.matmul(gram, gram, precision=precision)
        eye = jnp.eye(gram.shape[-1], dtype=jnp.float32)
        factor = coef_one * eye + coef_two * gram + coef_three * square
        total = factor if total is None else jnp.matmul(factor, total, precision=precision)
        if step < steps - 1:
            gram = jnp.matmul(
                jnp.matmul(factor, gram, precision=precision), factor, precision=precision
            )
    return total


def step_weight(weight, ortho):
    return (
        weight.astype(jnp.float32) * (1.0 - muon_rate * decay_rate)
        - muon_rate * 0.2 * math.sqrt(D) * ortho
    )


def adam_update(param, first, second, grad, rate, decay):
    first = adam_one * first + (1.0 - adam_one) * grad
    second = adam_two * second + (1.0 - adam_two) * grad * grad
    fixed_one = first / (1.0 - adam_one**STEP)
    fixed_two = second / (1.0 - adam_two**STEP)
    return (
        first,
        second,
        param * (1.0 - rate * decay) - rate * fixed_one / (jnp.sqrt(fixed_two) + adam_eps),
    )


def contract_rows(left, right, precision=None):
    return lax.dot_general(
        left,
        right,
        (((0,), (0,)), ((), ())),
        preferred_element_type=jnp.float32,
        precision=precision,
    )


def contract_cols(left, right):
    return lax.dot_general(
        left, right, (((1,), (1,)), ((), ())), preferred_element_type=jnp.float32
    )


def mat(left, right):
    return jnp.dot(left, right, preferred_element_type=jnp.float32)


def head_blocks(sums, momenta, weights):
    fresh = mom_rate * momenta + sums
    width = fresh.shape[1]
    block = jnp.arange(width) // HD
    same = block[:, None] == block[None, :]
    gram = jnp.where(same, contract_rows(fresh, fresh, highest), 0.0)
    square = jnp.sum(jnp.where(jnp.eye(width, dtype=bool), gram, 0.0), axis=0, keepdims=True)
    total = jnp.sum(jnp.where(same, square.T, 0.0), axis=0, keepdims=True)
    scale = 1.0 / (jnp.sqrt(total) + 1e-07)
    poly = polynomial(gram * scale * scale.T, 5, highest)
    ortho = jnp.dot(fresh * scale, poly, precision=highest)
    return fresh, step_weight(weights, ortho)


def expert_kernel(own_ref, arrived_ref, grads_ref, same_ref, below_ref, above_ref, far_ref, far_two_ref,
                  made_ref, back_ref, sums_ref, sums_up_ref, sums_down_ref, sums_far_ref,
                  weight_ref, rows_ref, hidden_ref, dgate_ref, dup_ref, dy_ref):
    expert = own_ref[0] + pl.program_id(0)
    level, side = own_ref[1], own_ref[2]
    width = D // 8

    def part(up, other):
        index = 2 * lax.rem(level + up, 4) + (1 - side if other else side)
        return pl.ds(pl.multiple_of(index * width, width), width)

    for up, ref in ((0, same_ref), (3, below_ref), (1, above_ref)):
        for other in range(2):
            for kind in range(3):
                weight_ref[kind, part(up, other)] = ref[other, kind, 0]
    for kind in range(3):
        weight_ref[kind, part(2, 0)] = far_ref[kind, 0]
        weight_ref[kind, part(2, 1)] = far_two_ref[kind, 0]
    full_gate, full_up, full_down = weight_ref[0], weight_ref[1], weight_ref[2]
    chunk = ROWS // CHUNKS
    seqs = chunk // CAP

    def forward(step, carry):
        first = pl.multiple_of(step * seqs, seqs)
        where = pl.ds(pl.multiple_of(step * chunk, chunk), chunk)
        both = arrived_ref[pl.ds(first, seqs), 0].reshape(chunk, D + WIDE)
        rows = both[:, :D]
        lane = lax.broadcasted_iota(jnp.int32, (chunk, WIDE), 1)
        pick = (lane % EXPERTS == expert) & (lane < 3 * EXPERTS)
        gate = jnp.sum(
            jnp.where(pick, both[:, D:].astype(jnp.float32), 0.0), axis=1, keepdims=True
        )
        gate_pre = mat(rows, full_gate)
        up_pre = mat(rows, full_up)
        sigma = jax.nn.sigmoid(gate_pre)
        activated = gate_pre * sigma
        hidden = (activated * up_pre).astype(jnp.bfloat16)
        made = contract_cols(hidden, full_down).astype(jnp.bfloat16)
        made_ref[pl.ds(first, seqs), 0] = made.reshape(seqs, CAP, D)
        slot_ids = lax.broadcasted_iota(jnp.int32, (LOCAL, CAP), 1).astype(jnp.float32) + 1.0
        token_lane = lax.broadcasted_iota(jnp.int32, (LOCAL, WIDE), 1)
        taken = []
        for seq in range(seqs):
            source = grads_ref[first + seq]
            places = jnp.where(token_lane == expert, source[:, D:].astype(jnp.float32), 0.0)
            chosen = jnp.sum(places, axis=1, keepdims=True) == slot_ids
            taken.append(contract_rows(chosen.astype(jnp.bfloat16), source[:, :D]))
        grad_f32 = jnp.concatenate(taken, axis=0)
        grad_made = (gate * grad_f32).astype(jnp.bfloat16)
        grad_gate_value = jnp.sum(made.astype(jnp.float32) * grad_f32, axis=1, keepdims=True)
        grad_hidden = mat(grad_made, full_down)
        grad_gate_pre = (
            grad_hidden * up_pre * sigma * (1.0 + gate_pre * (1.0 - sigma))
        ).astype(jnp.bfloat16)
        grad_up_pre = (grad_hidden * activated).astype(jnp.bfloat16)
        back = contract_cols(grad_gate_pre, full_gate) + contract_cols(grad_up_pre, full_up)
        back_ref[pl.ds(first, seqs), 0, :, :D] = back.astype(jnp.bfloat16).reshape(seqs, CAP, D)
        high, middle, low = [
            part.astype(jnp.float32) for part in three_parts(grad_gate_value)
        ]
        slot = jnp.where(
            lane < EXPERTS, high, jnp.where(lane < 2 * EXPERTS, middle, low)
        )
        back_ref[pl.ds(first, seqs), 0, :, D:] = (
            jnp.where(pick, slot, 0.0).astype(jnp.bfloat16).reshape(seqs, CAP, WIDE)
        )
        rows_ref[where] = rows
        hidden_ref[where] = hidden
        dgate_ref[where] = grad_gate_pre
        dup_ref[where] = grad_up_pre
        dy_ref[where] = grad_made
        return carry

    lax.fori_loop(0, CHUNKS, forward, 0)
    for up, ref in ((0, sums_ref), (1, sums_up_ref), (3, sums_down_ref), (2, sums_far_ref)):
        for other in range(2):
            columns = part(up, other)
            rows = rows_ref[:, columns]
            ref[other, 0, 0] = contract_rows(rows, dgate_ref[...]).astype(jnp.bfloat16)
            ref[other, 1, 0] = contract_rows(rows, dup_ref[...]).astype(jnp.bfloat16)
            ref[other, 2, 0] = contract_rows(dy_ref[:, columns], hidden_ref[...]).astype(
                jnp.bfloat16
            )


def expert_math(arrived, all_grads, weights):
    seqs, per_group = arrived.shape[:2]
    place = lax.axis_index("ctx")
    own = jnp.stack([lax.axis_index("exp") * per_group, place // 2, place % 2]).astype(jnp.int32)
    rows_each = D // 8

    def rows_spec(width):
        return pl.BlockSpec((seqs, 1, CAP, width), lambda e, own: (0, e, 0, 0))

    two = pl.BlockSpec((2, 3, 1, rows_each, FF), lambda e, own: (0, 0, e, 0, 0))
    one = pl.BlockSpec((3, 1, rows_each, FF), lambda e, own: (0, e, 0, 0))
    whole = pl.BlockSpec(all_grads.shape, lambda e, own: (0, 0, 0))
    return pl.pallas_call(
        expert_kernel,
        grid_spec=pltpu.PrefetchScalarGridSpec(
            num_scalar_prefetch=1,
            grid=(per_group,),
            in_specs=[rows_spec(D + WIDE), whole, two, two, two, one, one],
            out_specs=[rows_spec(D), rows_spec(D + WIDE), two, two, two, two],
            scratch_shapes=[
                pltpu.VMEM((3, D, FF), jnp.bfloat16),
                pltpu.VMEM((ROWS, D), jnp.bfloat16),
                pltpu.VMEM((ROWS, FF), jnp.bfloat16),
                pltpu.VMEM((ROWS, FF), jnp.bfloat16),
                pltpu.VMEM((ROWS, FF), jnp.bfloat16),
                pltpu.VMEM((ROWS, D), jnp.bfloat16),
            ],
        ),
        out_shape=[
            jax.ShapeDtypeStruct((seqs, per_group, CAP, D), jnp.bfloat16),
            jax.ShapeDtypeStruct((seqs, per_group, CAP, D + WIDE), jnp.bfloat16),
        ]
        + [jax.ShapeDtypeStruct((2, 3, per_group, rows_each, FF), jnp.bfloat16)] * 4,
        compiler_params=pltpu.CompilerParams(vmem_limit_bytes=56 * 2**20),
        cost_estimate=pl.CostEstimate(
            flops=18 * ROWS * per_group * D * FF,
            bytes_accessed=30 * 2**20,
            transcendentals=ROWS * per_group * FF,
        ),
        name="experts",
    )(own, arrived, all_grads, *weights)


def split_two(value):
    high = value.astype(jnp.bfloat16)
    return high, (value - high.astype(jnp.float32)).astype(jnp.bfloat16)


def mat_three(left, right):
    return mat(left[0], right[0]) + (mat(left[0], right[1]) + mat(left[1], right[0]))


def owner_kernel(matrix_ref, out_ref, gram_ref, total_ref):
    gram = contract_rows(matrix_ref[...], matrix_ref[...])
    width = gram_ref.shape[0]
    row = lax.broadcasted_iota(jnp.int32, (width, width), 0)
    column = lax.broadcasted_iota(jnp.int32, (width, width), 1)
    eye = (row == column).astype(jnp.float32)
    square = jnp.sum(jnp.sum(eye * gram, axis=1, keepdims=True), axis=0, keepdims=True)
    scale = 1.0 / (jnp.sqrt(square) + 1e-07)
    gram_ref[...] = gram * scale * scale
    total_ref[...] = eye

    def step(index, carry):
        gram = gram_ref[...]
        gram_two = split_two(gram)
        factor = coef_one * eye + coef_two * gram + coef_three * mat_three(gram_two, gram_two)
        factor_two = split_two(factor)
        total_ref[...] = mat_three(factor_two, split_two(total_ref[...]))
        gram_ref[...] = mat_three(split_two(mat_three(factor_two, gram_two)), factor_two)
        return carry

    lax.fori_loop(0, 5, step, 0)
    high, low = split_two(total_ref[...])
    matrix = matrix_ref[...]
    out_ref[...] = ((mat(matrix, high) + mat(matrix, low)) * scale).astype(out_ref.dtype)


def owner_orthogonal(stacked):
    rows, width = stacked.shape
    return pl.pallas_call(
        owner_kernel,
        out_shape=jax.ShapeDtypeStruct(stacked.shape, jnp.bfloat16),
        in_specs=[pl.BlockSpec(memory_space=pltpu.VMEM)],
        out_specs=pl.BlockSpec(memory_space=pltpu.VMEM),
        scratch_shapes=[
            pltpu.VMEM((width, width), jnp.float32),
            pltpu.VMEM((width, width), jnp.float32),
        ],
        compiler_params=pltpu.CompilerParams(vmem_limit_bytes=48 * 2**20),
        cost_estimate=pl.CostEstimate(
            flops=6 * (22 * width**3 + 2 * rows * width**2),
            bytes_accessed=4 * rows * width,
            transcendentals=0,
        ),
        name="owner",
    )(stacked)


def probabilities(queries, keys, first):
    scores = contract_cols(queries, keys) * HD ** (-0.5)
    token = lax.broadcasted_iota(jnp.int32, scores.shape, 0) % (scores.shape[0] // 2)
    key = lax.broadcasted_iota(jnp.int32, scores.shape, 1)
    scores = jnp.where(key <= first + token, scores, -1e30)
    running_max = jnp.max(scores, axis=1, keepdims=True)
    raised = jnp.exp(scores - running_max)
    return raised * (1.0 / jnp.sum(raised, axis=1, keepdims=True))


def two_heads(block, group):
    left = block[:, 2 * group * HD : (2 * group + 1) * HD]
    right = block[:, (2 * group + 1) * HD : (2 * group + 2) * HD]
    return jnp.concatenate([left, right], axis=0)


def side_by_side(stacked):
    half = stacked.shape[0] // 2
    return jnp.concatenate([stacked[:half], stacked[half:]], axis=1)


def attend_kernel(first_ref, query_ref, key_ref, value_ref, mixed_ref):
    queries, keys, values = query_ref[...], key_ref[...], value_ref[...]
    mixed = []
    for group in range(2):
        columns = slice(group * HD, (group + 1) * HD)
        weights = probabilities(two_heads(queries, group), keys[:, columns], first_ref[0])
        mixed.append(side_by_side(mat(weights.astype(jnp.bfloat16), values[:, columns])))
    mixed_ref[...] = jnp.concatenate(mixed, axis=1).astype(mixed_ref.dtype)


def attend_back_kernel(
    first_ref, query_ref, key_ref, value_ref, grad_ref, dquery_ref, dkey_ref, dvalue_ref
):
    queries, keys, values, grads = query_ref[...], key_ref[...], value_ref[...], grad_ref[...]
    dquery, dkey, dvalue = [], [], []
    for group in range(2):
        columns = slice(group * HD, (group + 1) * HD)
        query, grad = two_heads(queries, group), two_heads(grads, group)
        weights = probabilities(query, keys[:, columns], first_ref[0])
        grad_weights = contract_cols(grad, values[:, columns])
        inner = jnp.sum(weights * grad_weights, axis=1, keepdims=True)
        grad_scores = (weights * (grad_weights - inner)).astype(jnp.bfloat16)
        dquery.append(side_by_side(mat(grad_scores, keys[:, columns]) * HD ** (-0.5)))
        dkey.append(contract_rows(grad_scores, query) * HD ** (-0.5))
        dvalue.append(contract_rows(weights.astype(jnp.bfloat16), grad))
    dquery_ref[...] = jnp.concatenate(dquery, axis=1)
    dkey_ref[...] = jnp.concatenate(dkey, axis=1).astype(dkey_ref.dtype)
    dvalue_ref[...] = jnp.concatenate(dvalue, axis=1).astype(dvalue_ref.dtype)


def attention_call(kernel, operands, grads, first, name):
    queries, all_kv = operands
    rows, keys = queries.shape[0], all_kv.shape[0]
    steps = KV // 2
    wide = pl.BlockSpec((rows, 4 * HD), lambda g, first: (0, g))
    key_spec = pl.BlockSpec((keys, 2 * HD), lambda g, first: (0, g))
    value_spec = pl.BlockSpec((keys, 2 * HD), lambda g, first: (0, g + steps))
    if grads is None:
        arrays, specs = (queries, all_kv, all_kv), [wide, key_spec, value_spec]
        out_shape = jax.ShapeDtypeStruct(queries.shape, jnp.bfloat16)
        out_specs = wide
    else:
        arrays, specs = (queries, all_kv, all_kv, grads), [wide, key_spec, value_spec, wide]
        out_shape = [
            jax.ShapeDtypeStruct(queries.shape, jnp.float32),
            jax.ShapeDtypeStruct((keys, KV * HD), jnp.bfloat16),
            jax.ShapeDtypeStruct((keys, KV * HD), jnp.bfloat16),
        ]
        out_specs = [wide, key_spec, key_spec]
    factor = 4 if grads is None else 10
    return pl.pallas_call(
        kernel,
        grid_spec=pltpu.PrefetchScalarGridSpec(
            num_scalar_prefetch=1, grid=(steps,), in_specs=specs, out_specs=out_specs
        ),
        out_shape=out_shape,
        compiler_params=pltpu.CompilerParams(vmem_limit_bytes=48 * 2**20),
        cost_estimate=pl.CostEstimate(
            flops=factor * rows * keys * HEADS * HD,
            bytes_accessed=4 * 2**20,
            transcendentals=rows * keys * HEADS,
        ),
        name=name,
    )(first.astype(jnp.int32).reshape(1), *arrays)


def body(
    tokens,
    cotangent,
    routes,
    query_weight,
    kv_weight,
    output_weight,
    router,
    gains,
    gate_weight,
    up_weight,
    down_weight,
    query_momentum,
    kv_momentum,
    output_momentum,
    gate_momentum,
    up_momentum,
    down_momentum,
    router_first,
    router_second,
    gains_first,
    gains_second,
):
    bf16 = jnp.bfloat16
    ctx_count = lax.axis_size("ctx")
    exp_count = lax.axis_size("exp")
    exp_index = lax.axis_index("exp")
    row_count = tokens.shape[1]
    per_group = EXPERTS // exp_count
    inputs = tokens[0].astype(jnp.float32)
    grad_out = cotangent[0].astype(jnp.float32)
    route_ids = routes[0]

    packed = jnp.concatenate(
        [
            jnp.concatenate([query_weight, kv_weight], axis=1).T,
            router.astype(bf16).T,
            jnp.pad(gains.astype(bf16).reshape(1, -1), ((0, 0), (0, D - 2 * HD))),
            jnp.zeros((5, D), bf16),
        ],
        axis=0,
    )
    own_experts = jnp.stack([gate_weight, up_weight, down_weight])
    same = jnp.stack([own_experts, ctx_move(own_experts, 0, 1)])
    mine = spread(packed, "exp", parity_groups(exp_count), exp_count // 2)
    mine, same = lax.optimization_barrier((mine, same))
    below, above = ctx_move(same, 1, 0), ctx_move(same, 3, 0)
    other = core_swap(mine, exp_count)
    even = (exp_index % 2 == 0)

    def ordered(first, last):
        left, right = mine[:, first:last], other[:, first:last]
        return jnp.stack(
            [jnp.where(even, left, right), jnp.where(even, right, left)], axis=1
        ).reshape((exp_count, last - first, D))

    full_qkv = ordered(0, 2 * HD).reshape(exp_count * 2 * HD, D)
    full_router = ordered(2 * HD, 2 * HD + per_group).reshape(EXPERTS, D)
    full_gains = ordered(2 * HD + per_group, 2 * HD + per_group + 1)[:, 0, : 2 * HD]
    full_gains = full_gains.reshape(exp_count, 2, HD).transpose(1, 0, 2).reshape(2, D)
    gain_one = full_gains[0].astype(jnp.float32)
    gain_two = full_gains[1].astype(jnp.float32)

    full_output = lax.all_gather(output_weight.T, "exp", axis=0, tiled=True)

    expert_ids = jnp.arange(EXPERTS, dtype=jnp.int32)
    named = jnp.any(route_ids[:, :, None] == expert_ids[None, None, :], axis=1)
    named_low = named.astype(bf16)
    token_ids = jnp.arange(row_count)
    earlier = (token_ids[None, :] < token_ids[:, None]).astype(bf16)
    rank = mat(earlier, named_low)
    place = jnp.where(named, rank + 1.0, 0.0).astype(bf16)
    slot_ids = jnp.arange(EXPERTS * CAP, dtype=jnp.int32)
    widen = (slot_ids[None, :] // CAP == expert_ids[:, None]).astype(bf16)
    chosen_slot = mat(place, widen) == (slot_ids % CAP + 1).astype(jnp.float32)[None, :]
    select = chosen_slot.astype(bf16)

    sent_grads = jnp.concatenate(
        [cotangent[0], place, jnp.zeros((row_count, WIDE - EXPERTS), bf16)], axis=1
    )
    all_grads = lax.all_gather(sent_grads, "exp", axis=0, tiled=False)

    inv_one = lax.rsqrt(jnp.mean(inputs * inputs, axis=-1, keepdims=True) + eps_norm)
    normed_one = (inputs * inv_one * gain_one).astype(bf16)
    projected = contract_cols(normed_one, full_qkv).reshape(row_count, exp_count, 2 * HD)
    query_raw = projected[:, :, :HD]
    kv_raw = projected[:, :, HD:]
    first_row = lax.axis_index("ctx") * row_count
    cosine, sine = rope_tables(first_row, row_count)
    queries = rotate(query_raw, cosine, sine).astype(bf16)
    keys = rotate(kv_raw[:, :KV], cosine, sine).astype(bf16)
    values = kv_raw[:, KV:].astype(bf16)
    sent_kv = jnp.concatenate([keys, values], axis=1).reshape(row_count, 2 * KV * HD)
    sent_kv, below, above = lax.optimization_barrier((sent_kv, below, above))
    full_experts = (same, below, above, ctx_move(below[0], 1, 0), ctx_move(above[1], 3, 0))
    all_kv = spread(sent_kv, "ctx", None, ctx_count).reshape(ctx_count * row_count, 2 * KV * HD)
    flat_queries = queries.reshape(row_count, HEADS * HD)
    mixed_low = attention_call(attend_kernel, (flat_queries, all_kv), None, first_row, "attend")
    sent_mixed = mixed_low.reshape(row_count, exp_count, HD).transpose(1, 0, 2)
    sent_mixed = sent_mixed.reshape(exp_count, row_count * HD // D, D)
    attended = mat(mixed_low, full_output)
    residual = inputs + attended
    inv_two = lax.rsqrt(jnp.mean(residual * residual, axis=-1, keepdims=True) + eps_norm)
    normed_two = (residual * inv_two * gain_two).astype(bf16)
    logits = contract_cols(normed_two, full_router)
    gates = jax.nn.softmax(jnp.where(named, logits, -1e30), axis=-1)
    gates = jnp.where(named, gates, 0.0)
    gate_parts = three_parts(gates)
    extended = jnp.concatenate(
        [normed_two, *gate_parts, jnp.zeros((row_count, WIDE - 3 * EXPERTS), bf16)], axis=1
    )
    sent_rows = contract_rows(select, extended).astype(bf16)
    arrived = exchange(sent_rows.reshape(exp_count, per_group * CAP, D + WIDE), "exp")
    later_normed, arrived = lax.optimization_barrier((normed_one, arrived))
    all_normed = lax.all_gather(later_normed, "exp", axis=0, tiled=True)
    produced, back, *expert_grads = expert_math(
        arrived.reshape(exp_count, per_group, CAP, D + WIDE), all_grads, full_experts
    )
    returned = exchange(back.reshape(exp_count, per_group * CAP, D + WIDE), "exp")
    returned = returned.reshape(EXPERTS * CAP, D + WIDE)
    produced = after(produced, returned)
    route_values = exchange(
        jnp.concatenate([produced.reshape(exp_count, per_group * CAP, D), sent_mixed], axis=1),
        "exp",
    )
    sum_same, sum_up, sum_down, sum_far = expert_grads
    sum_up, sum_down, sum_far = (
        ctx_move(sum_up, 1, 0),
        ctx_move(sum_down, 3, 0),
        ctx_move(sum_far, 2, 0),
    )

    summed_back = mat(select, returned)
    tail = summed_back[:, D:]
    grad_gates = (
        tail[:, :EXPERTS] + tail[:, EXPERTS : 2 * EXPERTS] + tail[:, 2 * EXPERTS : 3 * EXPERTS]
    )
    grad_logits = (
        gates * (grad_gates - jnp.sum(gates * grad_gates, axis=-1, keepdims=True))
    ).astype(bf16)
    grad_normed_two = summed_back[:, :D] + mat(grad_logits, full_router)
    scaled_two = grad_normed_two * gain_two
    grad_gain_two = jnp.sum(grad_normed_two * residual * inv_two, axis=0)
    grad_residual = (
        grad_out
        + inv_two * scaled_two
        - residual * inv_two**3 * jnp.mean(scaled_two * residual, axis=-1, keepdims=True)
    )
    grad_attended = grad_residual.astype(bf16)
    grad_attended, sum_up, sum_down, sum_far = lax.optimization_barrier(
        (grad_attended, sum_up, sum_down, sum_far)
    )
    both_sums = (
        sum_same.astype(jnp.float32)
        + sum_up.astype(jnp.float32)
        + sum_down.astype(jnp.float32)
        + sum_far.astype(jnp.float32)
    )
    other_sums = ctx_move(both_sums[1].astype(bf16), 0, 1)
    all_attended = lax.all_gather(grad_attended, "exp", axis=0, tiled=True)
    grad_mixed = contract_cols(grad_attended, full_output).astype(bf16)
    grad_queries, key_terms, value_terms = attention_call(
        attend_back_kernel, (flat_queries, all_kv), grad_mixed, first_row, "attend_back"
    )
    kv_terms = jnp.concatenate([key_terms, value_terms], axis=1)
    kv_terms, other_sums, route_values = lax.optimization_barrier(
        (kv_terms, other_sums, route_values)
    )
    kv_terms = exchange(kv_terms.reshape(ctx_count, row_count, 2 * KV * HD), "ctx")
    grad_query_raw = rotate(
        grad_queries.reshape(row_count, HEADS, HD), cosine, -sine
    ).astype(bf16)
    expert_sums = both_sums[0] + other_sums.astype(jnp.float32)
    momenta = jnp.stack([gate_momentum, up_momentum, down_momentum])
    fresh = mom_rate * momenta + expert_sums
    matrix_count = 3 * per_group
    rows_each = fresh.shape[2]
    sent_fresh = jnp.pad(
        fresh.astype(bf16).reshape(matrix_count, rows_each, -1),
        ((0, ctx_count - matrix_count), (0, 0), (0, 0)),
    )
    level, side = lax.axis_index("ctx") // 2, lax.axis_index("ctx") % 2
    moves = [(up, other) for up in range(4) for other in range(2)]
    owned = []
    for up, other in moves:
        owner = 2 * ((level + up) % 4) + (side + other) % 2
        block = lax.dynamic_index_in_dim(sent_fresh, owner, 0, keepdims=False)
        owned.append(ctx_move(block, up, other) if up or other else block)
    ortho = owner_orthogonal(jnp.stack(owned).reshape(ctx_count * rows_each, -1))
    ortho = ortho.reshape(ctx_count, rows_each, -1)
    kv_terms, ortho = lax.optimization_barrier((kv_terms, ortho))
    kv_sums = jnp.sum(kv_terms.astype(jnp.float32), axis=0).reshape(row_count, 2 * KV, HD)
    grad_key_raw = rotate(kv_sums[:, :KV], cosine, -sine).astype(bf16)
    grad_kv_raw = jnp.concatenate([grad_key_raw, kv_sums[:, KV:].astype(bf16)], axis=1)
    grad_projected = jnp.concatenate([grad_query_raw, grad_kv_raw], axis=2)
    grad_normed_one = mat(grad_projected.reshape(row_count, exp_count * 2 * HD), full_qkv)
    scaled_one = grad_normed_one * gain_one
    grad_gain_one = jnp.sum(grad_normed_one * inputs * inv_one, axis=0)
    input_grad = (
        grad_residual
        + inv_one * scaled_one
        - inputs * inv_one**3 * jnp.mean(scaled_one * inputs, axis=-1, keepdims=True)
    )

    small_rows = (per_group * D + 2 * HD) // (2 * HD)
    small = jnp.concatenate(
        [
            contract_rows(grad_logits, normed_two).reshape(exp_count, -1, 2 * HD),
            jnp.stack([grad_gain_one, grad_gain_two])
            .reshape(2, exp_count, HD)
            .transpose(1, 0, 2)
            .reshape(exp_count, 1, 2 * HD),
            jnp.zeros((exp_count, 7, 2 * HD), jnp.float32),
        ],
        axis=1,
    ).astype(bf16)
    head_mixed = route_values[:, per_group * CAP :].reshape(exp_count * row_count, HD)
    route_values = route_values[:, : per_group * CAP].reshape(EXPERTS * CAP, D)
    head_grads = exchange(
        jnp.concatenate([jnp.transpose(grad_projected, (1, 0, 2)), small], axis=1), "exp"
    )
    small = jnp.sum(head_grads[:, row_count : row_count + small_rows].astype(jnp.float32), axis=0)
    head_grads = head_grads[:, :row_count].reshape(exp_count * row_count, 2 * HD)

    part = jnp.concatenate(
        [contract_rows(head_grads, all_normed), contract_rows(head_mixed, all_attended)], axis=0
    )
    width = D // ctx_count
    part = jnp.concatenate(
        [
            jnp.transpose(part.astype(bf16).reshape(3 * HD, ctx_count, width), (1, 0, 2)),
            jnp.broadcast_to(
                jnp.pad(small.astype(bf16), ((0, 7), (0, 0)))[None], (ctx_count, 24, width)
            ),
        ],
        axis=1,
    )
    part = jnp.sum(exchange(part, "ctx").astype(jnp.float32), axis=0)
    sums = spread(part[: 3 * HD].astype(bf16), "ctx", None, ctx_count)
    sums = jnp.transpose(sums, (0, 2, 1)).reshape(D, 3 * HD).astype(jnp.float32)
    small = part[3 * HD : 3 * HD + small_rows]
    sum_router = small[:-1].reshape(per_group, D).T
    sum_gains = small[-1].reshape(2, HD)
    router_one, router_two, router_new = adam_update(
        router, router_first, router_second, sum_router, router_rate, decay_rate
    )
    gains_one, gains_two, gains_new = adam_update(
        gains, gains_first, gains_second, sum_gains, gain_rate, 0.0
    )

    head_fresh, head_new = head_blocks(
        sums,
        jnp.concatenate([query_momentum, kv_momentum, output_momentum], axis=1),
        jnp.concatenate([query_weight, kv_weight, output_weight], axis=1),
    )

    returned_rows = [
        ctx_move(ortho[index], (4 - up) % 4, other) if up or other else ortho[index]
        for index, (up, other) in enumerate(moves)
    ]
    returned_rows = jnp.stack(returned_rows)
    ortho = jnp.stack(
        [
            lax.dynamic_index_in_dim(
                returned_rows,
                2 * ((matrix // 2 - level) % 4) + (matrix + side) % 2,
                0,
                keepdims=False,
            )
            for matrix in range(matrix_count)
        ]
    )
    ortho = ortho.reshape(fresh.shape).astype(jnp.float32)
    new = step_weight(jnp.stack([gate_weight, up_weight, down_weight]), ortho)

    gates_wide = [mat(part, widen) for part in gate_parts]
    block_value = residual
    for wide in gates_wide:
        weighted = jnp.where(chosen_slot, wide, 0.0).astype(bf16)
        block_value = block_value + mat(weighted, route_values)
    return (
        block_value.astype(bf16)[None],
        input_grad[None],
        head_fresh[:, :HD],
        head_new[:, :HD],
        head_fresh[:, HD : 2 * HD],
        head_new[:, HD : 2 * HD],
        head_fresh[:, 2 * HD :],
        head_new[:, 2 * HD :],
        fresh[0],
        new[0],
        fresh[1],
        new[1],
        fresh[2],
        new[2],
        router_one,
        router_two,
        router_new,
        gains_one,
        gains_two,
        gains_new,
    )


def solution(mesh):
    return jax.shard_map(
        body,
        mesh=mesh,
        in_specs=(
            P("exp", "ctx", None),
            P("exp", "ctx", None),
            P("exp", "ctx", None),
            P(None, "exp"),
            P(None, "exp"),
            P(None, "exp"),
            P(None, "exp"),
            P(None, "exp"),
            P("exp", "ctx", None),
            P("exp", "ctx", None),
            P("exp", "ctx", None),
            P(None, "exp"),
            P(None, "exp"),
            P(None, "exp"),
            P("exp", "ctx", None),
            P("exp", "ctx", None),
            P("exp", "ctx", None),
            P(None, "exp"),
            P(None, "exp"),
            P(None, "exp"),
            P(None, "exp"),
        ),
        out_specs=(
            P("exp", "ctx", None),
            P("exp", "ctx", None),
            P(None, "exp"),
            P(None, "exp"),
            P(None, "exp"),
            P(None, "exp"),
            P(None, "exp"),
            P(None, "exp"),
            P("exp", "ctx", None),
            P("exp", "ctx", None),
            P("exp", "ctx", None),
            P("exp", "ctx", None),
            P("exp", "ctx", None),
            P("exp", "ctx", None),
            P(None, "exp"),
            P(None, "exp"),
            P(None, "exp"),
            P(None, "exp"),
            P(None, "exp"),
            P(None, "exp"),
        ),
        check_vma=False,
    )
```

```python
import math

import jax
import jax.numpy as jnp
from jax import lax
from jax.experimental import pallas as pl
from jax.experimental.pallas import tpu as pltpu
from jax.sharding import PartitionSpec as P

D = 1024
HEADS = 16
KV = 8
HD = 64
TOP = 8
STEP = 10


eps_norm = 1e-05
rope_base = 10000.0
mom_rate = 0.95
muon_rate = 0.15
decay_rate = 0.1
adam_one = 0.9
adam_two = 0.95
adam_eps = 1e-08
router_rate = 0.015
gain_rate = 0.2
coef_one = 3.4445
coef_two = -4.775
coef_three = 2.0315
highest = lax.Precision.HIGHEST


def rope_tables(first_row, token_count):
    half_width = HD // 2
    frequency = rope_base ** (-jnp.arange(half_width, dtype=jnp.float32) * 2.0 / HD)
    position = (first_row + jnp.arange(token_count, dtype=jnp.int32)).astype(jnp.float32)
    angle_grid = position[:, None] * frequency[None, :]
    return (jnp.cos(angle_grid), jnp.sin(angle_grid))


def rotate(vector, cosine, sine):
    half_width = vector.shape[-1] // 2
    front_half = vector[..., :half_width]
    back_half = vector[..., half_width:]
    cos_rows = cosine[:, None, :]
    sin_rows = sine[:, None, :]
    return jnp.concatenate(
        [
            front_half * cos_rows - back_half * sin_rows,
            back_half * cos_rows + front_half * sin_rows,
        ],
        axis=-1,
    )


EXPERTS = 32
CAP = 48
WIDE = 128
FF = 512
ROWS = 16 * CAP
CHUNKS = 2
LOCAL = 128


def exchange(blocks, axis, groups=None):
    return lax.all_to_all(
        blocks, axis, split_axis=0, concat_axis=0, tiled=True, axis_index_groups=groups
    )


def spread(block, axis, groups=None, count=8):
    return exchange(jnp.broadcast_to(block[None], (count,) + block.shape), axis, groups)


def parity_groups(count):
    return [list(range(core, count, 2)) for core in range(2)]


def core_swap(block, count):
    return lax.ppermute(block, "exp", [(i, i ^ 1) for i in range(count)])


def ctx_move(block, up, other):
    pairs = [
        (2 * z + x, 2 * ((z + up) % 4) + (x ^ other)) for z in range(4) for x in range(2)
    ]
    return lax.ppermute(block, "ctx", pairs)


def exp_move(block, up, far, core):
    pairs = [
        (4 * y + 2 * h + c, 4 * ((y + up) % 4) + 2 * (h ^ far) + (c ^ core))
        for y in range(4)
        for h in range(2)
        for c in range(2)
    ]
    return lax.ppermute(block, "exp", pairs)


def ring_order(blocks, shift, axis):
    double = jnp.concatenate([blocks, blocks], axis=axis)
    return lax.dynamic_slice_in_dim(double, (4 - shift) % 4, 4, axis)


def after(value, *others):
    return lax.optimization_barrier((value,) + others)[0]


def three_parts(value):
    high = value.astype(jnp.bfloat16)
    rest = value - high.astype(jnp.float32)
    middle = rest.astype(jnp.bfloat16)
    low = (rest - middle.astype(jnp.float32)).astype(jnp.bfloat16)
    return high, middle, low


def polynomial(gram, steps, precision):
    total = None
    for step in range(steps):
        square = jnp.matmul(gram, gram, precision=precision)
        eye = jnp.eye(gram.shape[-1], dtype=jnp.float32)
        factor = coef_one * eye + coef_two * gram + coef_three * square
        total = factor if total is None else jnp.matmul(factor, total, precision=precision)
        if step < steps - 1:
            gram = jnp.matmul(
                jnp.matmul(factor, gram, precision=precision), factor, precision=precision
            )
    return total


def step_weight(weight, ortho):
    return (
        weight.astype(jnp.float32) * (1.0 - muon_rate * decay_rate)
        - muon_rate * 0.2 * math.sqrt(D) * ortho
    )


def adam_update(param, first, second, grad, rate, decay):
    first = adam_one * first + (1.0 - adam_one) * grad
    second = adam_two * second + (1.0 - adam_two) * grad * grad
    fixed_one = first / (1.0 - adam_one**STEP)
    fixed_two = second / (1.0 - adam_two**STEP)
    return (
        first,
        second,
        param * (1.0 - rate * decay) - rate * fixed_one / (jnp.sqrt(fixed_two) + adam_eps),
    )


def contract_rows(left, right, precision=None):
    return lax.dot_general(
        left,
        right,
        (((0,), (0,)), ((), ())),
        preferred_element_type=jnp.float32,
        precision=precision,
    )


def contract_cols(left, right):
    return lax.dot_general(
        left, right, (((1,), (1,)), ((), ())), preferred_element_type=jnp.float32
    )


def mat(left, right):
    return jnp.dot(left, right, preferred_element_type=jnp.float32)


def head_blocks(sums, momenta, weights):
    fresh = mom_rate * momenta + sums
    width = fresh.shape[1]
    block = jnp.arange(width) // HD
    same = block[:, None] == block[None, :]
    gram = jnp.where(same, contract_rows(fresh, fresh, highest), 0.0)
    square = jnp.sum(jnp.where(jnp.eye(width, dtype=bool), gram, 0.0), axis=0, keepdims=True)
    total = jnp.sum(jnp.where(same, square.T, 0.0), axis=0, keepdims=True)
    scale = 1.0 / (jnp.sqrt(total) + 1e-07)
    poly = polynomial(gram * scale * scale.T, 5, highest)
    ortho = jnp.dot(fresh * scale, poly, precision=highest)
    return fresh, step_weight(weights, ortho)


def expert_kernel(own_ref, arrived_ref, grads_ref, *refs_in_order):
    blocks, refs = refs_in_order[:8], refs_in_order[8:]
    expert_steps(own_ref, arrived_ref, grads_ref, blocks, *refs)


def expert_steps(own_ref, arrived_ref, grads_ref, blocks,
                  made_ref, back_ref, sums_ref, sums_up_ref, sums_down_ref, sums_far_ref,
                  weight_ref, rows_ref, hidden_ref, dgate_ref, dup_ref, dy_ref):
    expert = own_ref[0] + pl.program_id(0)
    level, side = own_ref[1], own_ref[2]
    width = D // 8

    def part(up, other):
        index = 2 * lax.rem(level + up, 4) + (1 - side if other else side)
        return pl.ds(pl.multiple_of(index * width, width), width)

    for index, up in enumerate((0, 3, 1, 2)):
        for other in range(2):
            for kind in range(3):
                weight_ref[kind, part(up, other)] = blocks[2 * index + other][kind, 0]
    full_gate, full_up, full_down = weight_ref[0], weight_ref[1], weight_ref[2]
    chunk = ROWS // CHUNKS
    seqs = chunk // CAP

    def forward(step, carry):
        first = pl.multiple_of(step * seqs, seqs)
        where = pl.ds(pl.multiple_of(step * chunk, chunk), chunk)
        both = arrived_ref[pl.ds(first, seqs), 0].reshape(chunk, D + WIDE)
        rows = both[:, :D]
        lane = lax.broadcasted_iota(jnp.int32, (chunk, WIDE), 1)
        pick = (lane % EXPERTS == expert) & (lane < 3 * EXPERTS)
        gate = jnp.sum(
            jnp.where(pick, both[:, D:].astype(jnp.float32), 0.0), axis=1, keepdims=True
        )
        gate_pre = mat(rows, full_gate)
        up_pre = mat(rows, full_up)
        sigma = jax.nn.sigmoid(gate_pre)
        activated = gate_pre * sigma
        hidden = (activated * up_pre).astype(jnp.bfloat16)
        made = contract_cols(hidden, full_down).astype(jnp.bfloat16)
        made_ref[pl.ds(first, seqs), 0] = made.reshape(seqs, CAP, D)
        slot_ids = lax.broadcasted_iota(jnp.int32, (LOCAL, CAP), 1).astype(jnp.float32) + 1.0
        token_lane = lax.broadcasted_iota(jnp.int32, (LOCAL, WIDE), 1)
        taken = []
        for seq in range(seqs):
            source = grads_ref[first + seq]
            places = jnp.where(token_lane == expert, source[:, D:].astype(jnp.float32), 0.0)
            chosen = jnp.sum(places, axis=1, keepdims=True) == slot_ids
            taken.append(contract_rows(chosen.astype(jnp.bfloat16), source[:, :D]))
        grad_f32 = jnp.concatenate(taken, axis=0)
        grad_made = (gate * grad_f32).astype(jnp.bfloat16)
        grad_gate_value = jnp.sum(made.astype(jnp.float32) * grad_f32, axis=1, keepdims=True)
        grad_hidden = mat(grad_made, full_down)
        grad_gate_pre = (
            grad_hidden * up_pre * sigma * (1.0 + gate_pre * (1.0 - sigma))
        ).astype(jnp.bfloat16)
        grad_up_pre = (grad_hidden * activated).astype(jnp.bfloat16)
        back = contract_cols(grad_gate_pre, full_gate) + contract_cols(grad_up_pre, full_up)
        back_ref[pl.ds(first, seqs), 0, :, :D] = back.astype(jnp.bfloat16).reshape(seqs, CAP, D)
        high, middle, low = [
            part.astype(jnp.float32) for part in three_parts(grad_gate_value)
        ]
        slot = jnp.where(
            lane < EXPERTS, high, jnp.where(lane < 2 * EXPERTS, middle, low)
        )
        back_ref[pl.ds(first, seqs), 0, :, D:] = (
            jnp.where(pick, slot, 0.0).astype(jnp.bfloat16).reshape(seqs, CAP, WIDE)
        )
        rows_ref[where] = rows
        hidden_ref[where] = hidden
        dgate_ref[where] = grad_gate_pre
        dup_ref[where] = grad_up_pre
        dy_ref[where] = grad_made
        return carry

    lax.fori_loop(0, CHUNKS, forward, 0)
    for up, ref in ((0, sums_ref), (1, sums_up_ref), (3, sums_down_ref), (2, sums_far_ref)):
        for other in range(2):
            columns = part(up, other)
            rows = rows_ref[:, columns]
            ref[other, 0, 0] = contract_rows(rows, dgate_ref[...]).astype(jnp.bfloat16)
            ref[other, 1, 0] = contract_rows(rows, dup_ref[...]).astype(jnp.bfloat16)
            ref[other, 2, 0] = contract_rows(dy_ref[:, columns], hidden_ref[...]).astype(
                jnp.bfloat16
            )


def expert_math(arrived, all_grads, weights):
    seqs, per_group = arrived.shape[:2]
    place = lax.axis_index("ctx")
    own = jnp.stack([lax.axis_index("exp") * per_group, place // 2, place % 2]).astype(jnp.int32)
    rows_each = D // 8

    def rows_spec(width):
        return pl.BlockSpec((seqs, 1, CAP, width), lambda e, own: (0, e, 0, 0))

    two = pl.BlockSpec((2, 3, 1, rows_each, FF), lambda e, own: (0, 0, e, 0, 0))
    one = pl.BlockSpec((3, 1, rows_each, FF), lambda e, own: (0, e, 0, 0))
    whole = pl.BlockSpec(all_grads.shape, lambda e, own: (0, 0, 0))
    return pl.pallas_call(
        expert_kernel,
        grid_spec=pltpu.PrefetchScalarGridSpec(
            num_scalar_prefetch=1,
            grid=(per_group,),
            in_specs=[rows_spec(D + WIDE), whole] + [one] * 8,
            out_specs=[rows_spec(D), rows_spec(D + WIDE), two, two, two, two],
            scratch_shapes=[
                pltpu.VMEM((3, D, FF), jnp.bfloat16),
                pltpu.VMEM((ROWS, D), jnp.bfloat16),
                pltpu.VMEM((ROWS, FF), jnp.bfloat16),
                pltpu.VMEM((ROWS, FF), jnp.bfloat16),
                pltpu.VMEM((ROWS, FF), jnp.bfloat16),
                pltpu.VMEM((ROWS, D), jnp.bfloat16),
            ],
        ),
        out_shape=[
            jax.ShapeDtypeStruct((seqs, per_group, CAP, D), jnp.bfloat16),
            jax.ShapeDtypeStruct((seqs, per_group, CAP, D + WIDE), jnp.bfloat16),
        ]
        + [jax.ShapeDtypeStruct((2, 3, per_group, rows_each, FF), jnp.bfloat16)] * 4,
        compiler_params=pltpu.CompilerParams(vmem_limit_bytes=56 * 2**20),
        cost_estimate=pl.CostEstimate(
            flops=18 * ROWS * per_group * D * FF,
            bytes_accessed=30 * 2**20,
            transcendentals=ROWS * per_group * FF,
        ),
        name="experts",
    )(own, arrived, all_grads, *weights)


def split_two(value):
    high = value.astype(jnp.bfloat16)
    return high, (value - high.astype(jnp.float32)).astype(jnp.bfloat16)


def mat_three(left, right):
    return mat(left[0], right[0]) + (mat(left[0], right[1]) + mat(left[1], right[0]))


def owner_kernel(matrix_ref, out_ref, gram_ref, total_ref):
    gram = contract_rows(matrix_ref[...], matrix_ref[...])
    width = gram_ref.shape[0]
    row = lax.broadcasted_iota(jnp.int32, (width, width), 0)
    column = lax.broadcasted_iota(jnp.int32, (width, width), 1)
    eye = (row == column).astype(jnp.float32)
    square = jnp.sum(jnp.sum(eye * gram, axis=1, keepdims=True), axis=0, keepdims=True)
    scale = 1.0 / (jnp.sqrt(square) + 1e-07)
    gram_ref[...] = gram * scale * scale
    total_ref[...] = eye

    def step(index, carry):
        gram = gram_ref[...]
        gram_two = split_two(gram)
        factor = coef_one * eye + coef_two * gram + coef_three * mat_three(gram_two, gram_two)
        factor_two = split_two(factor)
        total_ref[...] = mat_three(factor_two, split_two(total_ref[...]))
        gram_ref[...] = mat_three(split_two(mat_three(factor_two, gram_two)), factor_two)
        return carry

    lax.fori_loop(0, 5, step, 0)
    high, low = split_two(total_ref[...])
    matrix = matrix_ref[...]
    out_ref[...] = ((mat(matrix, high) + mat(matrix, low)) * scale).astype(out_ref.dtype)


def owner_orthogonal(stacked):
    rows, width = stacked.shape
    return pl.pallas_call(
        owner_kernel,
        out_shape=jax.ShapeDtypeStruct(stacked.shape, jnp.bfloat16),
        in_specs=[pl.BlockSpec(memory_space=pltpu.VMEM)],
        out_specs=pl.BlockSpec(memory_space=pltpu.VMEM),
        scratch_shapes=[
            pltpu.VMEM((width, width), jnp.float32),
            pltpu.VMEM((width, width), jnp.float32),
        ],
        compiler_params=pltpu.CompilerParams(vmem_limit_bytes=48 * 2**20),
        cost_estimate=pl.CostEstimate(
            flops=6 * (22 * width**3 + 2 * rows * width**2),
            bytes_accessed=4 * rows * width,
            transcendentals=0,
        ),
        name="owner",
    )(stacked)


def probabilities(queries, keys, first):
    scores = contract_cols(queries, keys) * HD ** (-0.5)
    token = lax.broadcasted_iota(jnp.int32, scores.shape, 0) % (scores.shape[0] // 2)
    key = lax.broadcasted_iota(jnp.int32, scores.shape, 1)
    scores = jnp.where(key <= first + token, scores, -1e30)
    running_max = jnp.max(scores, axis=1, keepdims=True)
    raised = jnp.exp(scores - running_max)
    return raised * (1.0 / jnp.sum(raised, axis=1, keepdims=True))


def two_heads(block, group):
    left = block[:, 2 * group * HD : (2 * group + 1) * HD]
    right = block[:, (2 * group + 1) * HD : (2 * group + 2) * HD]
    return jnp.concatenate([left, right], axis=0)


def side_by_side(stacked):
    half = stacked.shape[0] // 2
    return jnp.concatenate([stacked[:half], stacked[half:]], axis=1)


def attend_kernel(first_ref, query_ref, key_ref, value_ref, mixed_ref):
    queries, keys, values = query_ref[...], key_ref[...], value_ref[...]
    mixed = []
    for group in range(2):
        columns = slice(group * HD, (group + 1) * HD)
        weights = probabilities(two_heads(queries, group), keys[:, columns], first_ref[0])
        mixed.append(side_by_side(mat(weights.astype(jnp.bfloat16), values[:, columns])))
    mixed_ref[...] = jnp.concatenate(mixed, axis=1).astype(mixed_ref.dtype)


def attend_back_kernel(
    first_ref, query_ref, key_ref, value_ref, grad_ref, dquery_ref, dkey_ref, dvalue_ref
):
    queries, keys, values, grads = query_ref[...], key_ref[...], value_ref[...], grad_ref[...]
    dquery, dkey, dvalue = [], [], []
    for group in range(2):
        columns = slice(group * HD, (group + 1) * HD)
        query, grad = two_heads(queries, group), two_heads(grads, group)
        weights = probabilities(query, keys[:, columns], first_ref[0])
        grad_weights = contract_cols(grad, values[:, columns])
        inner = jnp.sum(weights * grad_weights, axis=1, keepdims=True)
        grad_scores = (weights * (grad_weights - inner)).astype(jnp.bfloat16)
        dquery.append(side_by_side(mat(grad_scores, keys[:, columns]) * HD ** (-0.5)))
        dkey.append(contract_rows(grad_scores, query) * HD ** (-0.5))
        dvalue.append(contract_rows(weights.astype(jnp.bfloat16), grad))
    dquery_ref[...] = jnp.concatenate(dquery, axis=1)
    dkey_ref[...] = jnp.concatenate(dkey, axis=1).astype(dkey_ref.dtype)
    dvalue_ref[...] = jnp.concatenate(dvalue, axis=1).astype(dvalue_ref.dtype)


def attention_call(kernel, operands, grads, first, name):
    queries, all_kv = operands
    rows, keys = queries.shape[0], all_kv.shape[0]
    steps = KV // 2
    wide = pl.BlockSpec((rows, 4 * HD), lambda g, first: (0, g))
    key_spec = pl.BlockSpec((keys, 2 * HD), lambda g, first: (0, g))
    value_spec = pl.BlockSpec((keys, 2 * HD), lambda g, first: (0, g + steps))
    if grads is None:
        arrays, specs = (queries, all_kv, all_kv), [wide, key_spec, value_spec]
        out_shape = jax.ShapeDtypeStruct(queries.shape, jnp.bfloat16)
        out_specs = wide
    else:
        arrays, specs = (queries, all_kv, all_kv, grads), [wide, key_spec, value_spec, wide]
        out_shape = [
            jax.ShapeDtypeStruct(queries.shape, jnp.float32),
            jax.ShapeDtypeStruct((keys, KV * HD), jnp.bfloat16),
            jax.ShapeDtypeStruct((keys, KV * HD), jnp.bfloat16),
        ]
        out_specs = [wide, key_spec, key_spec]
    factor = 4 if grads is None else 10
    return pl.pallas_call(
        kernel,
        grid_spec=pltpu.PrefetchScalarGridSpec(
            num_scalar_prefetch=1, grid=(steps,), in_specs=specs, out_specs=out_specs
        ),
        out_shape=out_shape,
        compiler_params=pltpu.CompilerParams(vmem_limit_bytes=48 * 2**20),
        cost_estimate=pl.CostEstimate(
            flops=factor * rows * keys * HEADS * HD,
            bytes_accessed=4 * 2**20,
            transcendentals=rows * keys * HEADS,
        ),
        name=name,
    )(first.astype(jnp.int32).reshape(1), *arrays)


def body(
    tokens,
    cotangent,
    routes,
    query_weight,
    kv_weight,
    output_weight,
    router,
    gains,
    gate_weight,
    up_weight,
    down_weight,
    query_momentum,
    kv_momentum,
    output_momentum,
    gate_momentum,
    up_momentum,
    down_momentum,
    router_first,
    router_second,
    gains_first,
    gains_second,
):
    bf16 = jnp.bfloat16
    ctx_count = lax.axis_size("ctx")
    exp_count = lax.axis_size("exp")
    exp_index = lax.axis_index("exp")
    row_count = tokens.shape[1]
    per_group = EXPERTS // exp_count
    inputs = tokens[0].astype(jnp.float32)
    grad_out = cotangent[0].astype(jnp.float32)
    route_ids = routes[0]

    packed = jnp.concatenate(
        [
            jnp.concatenate([query_weight, kv_weight], axis=1).T,
            router.astype(bf16).T,
            jnp.pad(gains.astype(bf16).reshape(1, -1), ((0, 0), (0, D - 2 * HD))),
            jnp.zeros((5, D), bf16),
        ],
        axis=0,
    )
    own_experts = jnp.stack([gate_weight, up_weight, down_weight])
    row_y, far_x, core = exp_index // 4, (exp_index // 2) % 2, exp_index % 2
    packed_far = exp_move(packed, 0, 1, 0)
    other_experts = ctx_move(own_experts, 0, 1)
    below, above = ctx_move(own_experts, 1, 0), ctx_move(own_experts, 3, 0)
    pair = jnp.stack(
        [
            jnp.where(far_x == 0, packed, packed_far),
            jnp.where(far_x == 0, packed_far, packed),
        ]
    )
    from_below, from_above = exp_move(pair, 1, 0, 0), exp_move(pair, 3, 0, 0)
    from_below, from_above, other_experts, below, above = lax.optimization_barrier(
        (from_below, from_above, other_experts, below, above)
    )
    below_other, above_other = ctx_move(other_experts, 1, 0), ctx_move(other_experts, 3, 0)
    far = ctx_move(below, 1, 0)
    from_two = jnp.stack([exp_move(from_below[0], 1, 0, 0), exp_move(from_above[1], 3, 0, 0)])
    mine = jnp.stack([pair, from_above, from_two, from_below])
    other = exp_move(mine, 0, 0, 1)

    def ordered(left, right, axis):
        both = jnp.stack(
            [jnp.where(core == 0, left, right), jnp.where(core == 0, right, left)], axis=axis + 2
        )
        return ring_order(both, row_y, axis)

    packed_rows = packed.shape[0]
    mine_flat = mine.reshape(8 * packed_rows, D)
    other_flat = other.reshape(8 * packed_rows, D)
    full_router = ordered(
        mine[:, :, 2 * HD : 2 * HD + per_group], other[:, :, 2 * HD : 2 * HD + per_group], 0
    ).reshape(EXPERTS, D)
    gains_row = 2 * HD + per_group
    full_gains = ordered(mine[:, :, gains_row, : 2 * HD], other[:, :, gains_row, : 2 * HD], 0)
    full_gains = full_gains.reshape(exp_count, 2, HD).transpose(1, 0, 2).reshape(2, D)
    gain_one = full_gains[0].astype(jnp.float32)
    gain_two = full_gains[1].astype(jnp.float32)

    full_output = lax.all_gather(output_weight.T, "exp", axis=0, tiled=True)

    expert_ids = jnp.arange(EXPERTS, dtype=jnp.int32)
    named = jnp.any(route_ids[:, :, None] == expert_ids[None, None, :], axis=1)
    named_low = named.astype(bf16)
    token_ids = jnp.arange(row_count)
    earlier = (token_ids[None, :] < token_ids[:, None]).astype(bf16)
    rank = mat(earlier, named_low)
    place = jnp.where(named, rank + 1.0, 0.0).astype(bf16)
    slot_ids = jnp.arange(EXPERTS * CAP, dtype=jnp.int32)
    widen = (slot_ids[None, :] // CAP == expert_ids[:, None]).astype(bf16)
    chosen_slot = mat(place, widen) == (slot_ids % CAP + 1).astype(jnp.float32)[None, :]
    select = chosen_slot.astype(bf16)

    sent_grads = jnp.concatenate(
        [cotangent[0], place, jnp.zeros((row_count, WIDE - EXPERTS), bf16)], axis=1
    )
    all_grads = lax.all_gather(sent_grads, "exp", axis=0, tiled=False)

    inv_one = lax.rsqrt(jnp.mean(inputs * inputs, axis=-1, keepdims=True) + eps_norm)
    normed_one = (inputs * inv_one * gain_one).astype(bf16)
    halves = [
        contract_cols(normed_one, flat).reshape(row_count, 4, 2, packed_rows)[..., : 2 * HD]
        for flat in (mine_flat, other_flat)
    ]
    projected = ordered(*halves, 1).reshape(row_count, exp_count, 2 * HD)
    query_raw = projected[:, :, :HD]
    kv_raw = projected[:, :, HD:]
    first_row = lax.axis_index("ctx") * row_count
    cosine, sine = rope_tables(first_row, row_count)
    queries = rotate(query_raw, cosine, sine).astype(bf16)
    keys = rotate(kv_raw[:, :KV], cosine, sine).astype(bf16)
    values = kv_raw[:, KV:].astype(bf16)
    sent_kv = jnp.concatenate([keys, values], axis=1).reshape(row_count, 2 * KV * HD)
    sent_kv, below_other, above_other, far = lax.optimization_barrier(
        (sent_kv, below_other, above_other, far)
    )
    far_other = ctx_move(above_other, 3, 0)
    full_experts = (
        own_experts, other_experts, below, below_other, above, above_other, far, far_other
    )
    all_kv = spread(sent_kv, "ctx", None, ctx_count).reshape(ctx_count * row_count, 2 * KV * HD)
    flat_queries = queries.reshape(row_count, HEADS * HD)
    mixed_low = attention_call(attend_kernel, (flat_queries, all_kv), None, first_row, "attend")
    sent_mixed = mixed_low.reshape(row_count, exp_count, HD).transpose(1, 0, 2)
    sent_mixed = sent_mixed.reshape(exp_count, row_count * HD // D, D)
    attended = mat(mixed_low, full_output)
    residual = inputs + attended
    inv_two = lax.rsqrt(jnp.mean(residual * residual, axis=-1, keepdims=True) + eps_norm)
    normed_two = (residual * inv_two * gain_two).astype(bf16)
    logits = contract_cols(normed_two, full_router)
    gates = jax.nn.softmax(jnp.where(named, logits, -1e30), axis=-1)
    gates = jnp.where(named, gates, 0.0)
    gate_parts = three_parts(gates)
    extended = jnp.concatenate(
        [normed_two, *gate_parts, jnp.zeros((row_count, WIDE - 3 * EXPERTS), bf16)], axis=1
    )
    sent_rows = contract_rows(select, extended).astype(bf16)
    arrived = exchange(sent_rows.reshape(exp_count, per_group * CAP, D + WIDE), "exp")
    later_normed, arrived = lax.optimization_barrier((normed_one, arrived))
    all_normed = lax.all_gather(later_normed, "exp", axis=0, tiled=True)
    produced, back, *expert_grads = expert_math(
        arrived.reshape(exp_count, per_group, CAP, D + WIDE), all_grads, full_experts
    )
    returned = exchange(back.reshape(exp_count, per_group * CAP, D + WIDE), "exp")
    returned = returned.reshape(EXPERTS * CAP, D + WIDE)
    sum_same, sum_up, sum_down, sum_far = expert_grads
    sum_up, sum_down, sum_far = (
        ctx_move(sum_up, 1, 0),
        ctx_move(sum_down, 3, 0),
        ctx_move(sum_far, 2, 0),
    )
    returned, sum_up, sum_down = lax.optimization_barrier((returned, sum_up, sum_down))
    produced = after(produced, returned)
    route_values = exchange(
        jnp.concatenate([produced.reshape(exp_count, per_group * CAP, D), sent_mixed], axis=1),
        "exp",
    )
    summed_back = mat(select, returned)
    tail = summed_back[:, D:]
    grad_gates = (
        tail[:, :EXPERTS] + tail[:, EXPERTS : 2 * EXPERTS] + tail[:, 2 * EXPERTS : 3 * EXPERTS]
    )
    grad_logits = (
        gates * (grad_gates - jnp.sum(gates * grad_gates, axis=-1, keepdims=True))
    ).astype(bf16)
    grad_normed_two = summed_back[:, :D] + mat(grad_logits, full_router)
    scaled_two = grad_normed_two * gain_two
    grad_gain_two = jnp.sum(grad_normed_two * residual * inv_two, axis=0)
    grad_residual = (
        grad_out
        + inv_two * scaled_two
        - residual * inv_two**3 * jnp.mean(scaled_two * residual, axis=-1, keepdims=True)
    )
    grad_attended = grad_residual.astype(bf16)
    all_attended = lax.all_gather(grad_attended, "exp", axis=0, tiled=True)
    grad_mixed = contract_cols(grad_attended, full_output).astype(bf16)
    grad_queries, key_terms, value_terms = attention_call(
        attend_back_kernel, (flat_queries, all_kv), grad_mixed, first_row, "attend_back"
    )
    kv_terms = jnp.concatenate([key_terms, value_terms], axis=1)
    kv_terms, route_values, sum_far = lax.optimization_barrier(
        (kv_terms, route_values, sum_far)
    )
    both_sums = (
        sum_same.astype(jnp.float32)
        + sum_up.astype(jnp.float32)
        + sum_down.astype(jnp.float32)
        + sum_far.astype(jnp.float32)
    )
    other_sums = ctx_move(both_sums[1].astype(bf16), 0, 1)
    kv_terms = exchange(kv_terms.reshape(ctx_count, row_count, 2 * KV * HD), "ctx")
    grad_query_raw = rotate(
        grad_queries.reshape(row_count, HEADS, HD), cosine, -sine
    ).astype(bf16)
    expert_sums = both_sums[0] + other_sums.astype(jnp.float32)
    momenta = jnp.stack([gate_momentum, up_momentum, down_momentum])
    fresh = mom_rate * momenta + expert_sums
    matrix_count = 3 * per_group
    rows_each = fresh.shape[2]
    sent_fresh = jnp.pad(
        fresh.astype(bf16).reshape(matrix_count, rows_each, -1),
        ((0, ctx_count - matrix_count), (0, 0), (0, 0)),
    )
    level, side = lax.axis_index("ctx") // 2, lax.axis_index("ctx") % 2
    moves = [(up, other) for up in range(4) for other in range(2)]
    owned = []
    for up, other in moves:
        owner = 2 * ((level + up) % 4) + (side + other) % 2
        block = lax.dynamic_index_in_dim(sent_fresh, owner, 0, keepdims=False)
        owned.append(ctx_move(block, up, other) if up or other else block)
    kv_sums = jnp.sum(kv_terms.astype(jnp.float32), axis=0).reshape(row_count, 2 * KV, HD)
    grad_key_raw = rotate(kv_sums[:, :KV], cosine, -sine).astype(bf16)
    grad_kv_raw = jnp.concatenate([grad_key_raw, kv_sums[:, KV:].astype(bf16)], axis=1)
    grad_projected = jnp.concatenate([grad_query_raw, grad_kv_raw], axis=2)
    by_core = ring_order(grad_projected.reshape(row_count, 4, 2, 2, 2 * HD), -row_y, 1)
    by_core = jnp.pad(by_core, ((0, 0),) * 4 + ((0, packed_rows - 2 * HD),))
    first_core, second_core = by_core[:, :, :, 0], by_core[:, :, :, 1]
    grad_normed_one = mat(
        jnp.where(core == 0, first_core, second_core).reshape(row_count, -1), mine_flat
    ) + mat(jnp.where(core == 0, second_core, first_core).reshape(row_count, -1), other_flat)
    scaled_one = grad_normed_one * gain_one
    grad_gain_one = jnp.sum(grad_normed_one * inputs * inv_one, axis=0)
    input_grad = (
        grad_residual
        + inv_one * scaled_one
        - inputs * inv_one**3 * jnp.mean(scaled_one * inputs, axis=-1, keepdims=True)
    )

    small_rows = (per_group * D + 2 * HD) // (2 * HD)
    small = jnp.concatenate(
        [
            contract_rows(grad_logits, normed_two).reshape(exp_count, -1, 2 * HD),
            jnp.stack([grad_gain_one, grad_gain_two])
            .reshape(2, exp_count, HD)
            .transpose(1, 0, 2)
            .reshape(exp_count, 1, 2 * HD),
            jnp.zeros((exp_count, 7, 2 * HD), jnp.float32),
        ],
        axis=1,
    ).astype(bf16)
    head_mixed = route_values[:, per_group * CAP :].reshape(exp_count * row_count, HD)
    route_values = route_values[:, : per_group * CAP].reshape(EXPERTS * CAP, D)
    head_send = jnp.concatenate([jnp.transpose(grad_projected, (1, 0, 2)), small], axis=1)
    head_send, owned = lax.optimization_barrier((head_send, owned))
    head_grads = exchange(head_send, "exp")
    ortho = owner_orthogonal(jnp.stack(owned).reshape(ctx_count * rows_each, -1))
    head_grads, ortho = lax.optimization_barrier((head_grads, ortho))
    ortho = ortho.reshape(ctx_count, rows_each, -1)
    returned_rows = [
        ctx_move(ortho[index], (4 - up) % 4, other) if up or other else ortho[index]
        for index, (up, other) in enumerate(moves)
    ]
    small = jnp.sum(head_grads[:, row_count : row_count + small_rows].astype(jnp.float32), axis=0)
    head_grads = head_grads[:, :row_count].reshape(exp_count * row_count, 2 * HD)

    part = jnp.concatenate(
        [
            mat(lax.optimization_barrier(head_grads.T), all_normed),
            mat(lax.optimization_barrier(head_mixed.T), all_attended),
        ],
        axis=0,
    )
    width = D // ctx_count
    part = jnp.concatenate(
        [
            jnp.transpose(part.astype(bf16).reshape(3 * HD, ctx_count, width), (1, 0, 2)),
            jnp.broadcast_to(
                jnp.pad(small.astype(bf16), ((0, 7), (0, 0)))[None], (ctx_count, 24, width)
            ),
        ],
        axis=1,
    )
    part, *returned_rows = lax.optimization_barrier((exchange(part, "ctx"), *returned_rows))
    part = jnp.sum(part.astype(jnp.float32), axis=0)
    sums = spread(part[: 3 * HD].astype(bf16), "ctx", None, ctx_count)
    sums = jnp.transpose(sums, (0, 2, 1)).reshape(D, 3 * HD).astype(jnp.float32)
    small = part[3 * HD : 3 * HD + small_rows]
    sum_router = small[:-1].reshape(per_group, D).T
    sum_gains = small[-1].reshape(2, HD)
    router_one, router_two, router_new = adam_update(
        router, router_first, router_second, sum_router, router_rate, decay_rate
    )
    gains_one, gains_two, gains_new = adam_update(
        gains, gains_first, gains_second, sum_gains, gain_rate, 0.0
    )

    head_fresh, head_new = head_blocks(
        sums,
        jnp.concatenate([query_momentum, kv_momentum, output_momentum], axis=1),
        jnp.concatenate([query_weight, kv_weight, output_weight], axis=1),
    )

    returned_rows = jnp.stack(returned_rows)
    ortho = jnp.stack(
        [
            lax.dynamic_index_in_dim(
                returned_rows,
                2 * ((matrix // 2 - level) % 4) + (matrix + side) % 2,
                0,
                keepdims=False,
            )
            for matrix in range(matrix_count)
        ]
    )
    ortho = ortho.reshape(fresh.shape).astype(jnp.float32)
    new = step_weight(jnp.stack([gate_weight, up_weight, down_weight]), ortho)

    gates_wide = [mat(part, widen) for part in gate_parts]
    block_value = residual
    for wide in gates_wide:
        weighted = jnp.where(chosen_slot, wide, 0.0).astype(bf16)
        block_value = block_value + mat(weighted, route_values)
    return (
        block_value.astype(bf16)[None],
        input_grad[None],
        head_fresh[:, :HD],
        head_new[:, :HD],
        head_fresh[:, HD : 2 * HD],
        head_new[:, HD : 2 * HD],
        head_fresh[:, 2 * HD :],
        head_new[:, 2 * HD :],
        fresh[0],
        new[0],
        fresh[1],
        new[1],
        fresh[2],
        new[2],
        router_one,
        router_two,
        router_new,
        gains_one,
        gains_two,
        gains_new,
    )


def solution(mesh):
    return jax.shard_map(
        body,
        mesh=mesh,
        in_specs=(
            P("exp", "ctx", None),
            P("exp", "ctx", None),
            P("exp", "ctx", None),
            P(None, "exp"),
            P(None, "exp"),
            P(None, "exp"),
            P(None, "exp"),
            P(None, "exp"),
            P("exp", "ctx", None),
            P("exp", "ctx", None),
            P("exp", "ctx", None),
            P(None, "exp"),
            P(None, "exp"),
            P(None, "exp"),
            P("exp", "ctx", None),
            P("exp", "ctx", None),
            P("exp", "ctx", None),
            P(None, "exp"),
            P(None, "exp"),
            P(None, "exp"),
            P(None, "exp"),
        ),
        out_specs=(
            P("exp", "ctx", None),
            P("exp", "ctx", None),
            P(None, "exp"),
            P(None, "exp"),
            P(None, "exp"),
            P(None, "exp"),
            P(None, "exp"),
            P(None, "exp"),
            P("exp", "ctx", None),
            P("exp", "ctx", None),
            P("exp", "ctx", None),
            P("exp", "ctx", None),
            P("exp", "ctx", None),
            P("exp", "ctx", None),
            P(None, "exp"),
            P(None, "exp"),
            P(None, "exp"),
            P(None, "exp"),
            P(None, "exp"),
            P(None, "exp"),
        ),
        check_vma=False,
    )
```

```python
import math

import jax
import jax.numpy as jnp
from jax import lax
from jax.experimental import pallas as pl
from jax.experimental.pallas import tpu as pltpu
from jax.sharding import PartitionSpec as P

D = 1024
HEADS = 16
KV = 8
HD = 64
TOP = 8
STEP = 10


eps_norm = 1e-05
rope_base = 10000.0
mom_rate = 0.95
muon_rate = 0.15
decay_rate = 0.1
adam_one = 0.9
adam_two = 0.95
adam_eps = 1e-08
router_rate = 0.015
gain_rate = 0.2
coef_one = 3.4445
coef_two = -4.775
coef_three = 2.0315
highest = lax.Precision.HIGHEST


def rope_tables(first_row, token_count):
    half_width = HD // 2
    frequency = rope_base ** (-jnp.arange(half_width, dtype=jnp.float32) * 2.0 / HD)
    position = (first_row + jnp.arange(token_count, dtype=jnp.int32)).astype(jnp.float32)
    angle_grid = position[:, None] * frequency[None, :]
    return (jnp.cos(angle_grid), jnp.sin(angle_grid))


def rotate(vector, cosine, sine):
    half_width = vector.shape[-1] // 2
    front_half = vector[..., :half_width]
    back_half = vector[..., half_width:]
    cos_rows = cosine[:, None, :]
    sin_rows = sine[:, None, :]
    return jnp.concatenate(
        [
            front_half * cos_rows - back_half * sin_rows,
            back_half * cos_rows + front_half * sin_rows,
        ],
        axis=-1,
    )


EXPERTS = 32
CAP = 48
WIDE = 128
FF = 512
ROWS = 16 * CAP
CHUNKS = 2
LOCAL = 128


def exchange(blocks, axis, groups=None):
    return lax.all_to_all(
        blocks, axis, split_axis=0, concat_axis=0, tiled=True, axis_index_groups=groups
    )


def spread(block, axis, groups=None, count=8):
    return exchange(jnp.broadcast_to(block[None], (count,) + block.shape), axis, groups)


def parity_groups(count):
    return [list(range(core, count, 2)) for core in range(2)]


def core_swap(block, count):
    return lax.ppermute(block, "exp", [(i, i ^ 1) for i in range(count)])


def ctx_move(block, up, other):
    pairs = [
        (2 * z + x, 2 * ((z + up) % 4) + (x ^ other)) for z in range(4) for x in range(2)
    ]
    return lax.ppermute(block, "ctx", pairs)


def plus(left, right):
    return (left.astype(jnp.float32) + right.astype(jnp.float32)).astype(jnp.bfloat16)


def owner_move(block, up):
    pairs = [
        (2 * z + x, 2 * ((z + up) % 4) + x) for z in range(4) for x in range(2) if (z + up) % 4 < 3
    ]
    return lax.ppermute(block, "ctx", pairs)


def exp_move(block, up, far, core):
    pairs = [
        (4 * y + 2 * h + c, 4 * ((y + up) % 4) + 2 * (h ^ far) + (c ^ core))
        for y in range(4)
        for h in range(2)
        for c in range(2)
    ]
    return lax.ppermute(block, "exp", pairs)


def ring_order(blocks, shift, axis):
    double = jnp.concatenate([blocks, blocks], axis=axis)
    return lax.dynamic_slice_in_dim(double, (4 - shift) % 4, 4, axis)


def after(value, *others):
    return lax.optimization_barrier((value,) + others)[0]


def three_parts(value):
    high = value.astype(jnp.bfloat16)
    rest = value - high.astype(jnp.float32)
    middle = rest.astype(jnp.bfloat16)
    low = (rest - middle.astype(jnp.float32)).astype(jnp.bfloat16)
    return high, middle, low


def polynomial(gram, steps, precision):
    total = None
    for step in range(steps):
        square = jnp.matmul(gram, gram, precision=precision)
        eye = jnp.eye(gram.shape[-1], dtype=jnp.float32)
        factor = coef_one * eye + coef_two * gram + coef_three * square
        total = factor if total is None else jnp.matmul(factor, total, precision=precision)
        if step < steps - 1:
            gram = jnp.matmul(
                jnp.matmul(factor, gram, precision=precision), factor, precision=precision
            )
    return total


def step_weight(weight, ortho):
    return (
        weight.astype(jnp.float32) * (1.0 - muon_rate * decay_rate)
        - muon_rate * 0.2 * math.sqrt(D) * ortho
    )


def adam_update(param, first, second, grad, rate, decay):
    first = adam_one * first + (1.0 - adam_one) * grad
    second = adam_two * second + (1.0 - adam_two) * grad * grad
    fixed_one = first / (1.0 - adam_one**STEP)
    fixed_two = second / (1.0 - adam_two**STEP)
    return (
        first,
        second,
        param * (1.0 - rate * decay) - rate * fixed_one / (jnp.sqrt(fixed_two) + adam_eps),
    )


def contract_rows(left, right, precision=None):
    return lax.dot_general(
        left,
        right,
        (((0,), (0,)), ((), ())),
        preferred_element_type=jnp.float32,
        precision=precision,
    )


def contract_cols(left, right):
    return lax.dot_general(
        left, right, (((1,), (1,)), ((), ())), preferred_element_type=jnp.float32
    )


def mat(left, right):
    return jnp.dot(left, right, preferred_element_type=jnp.float32)


def head_blocks(sums, momenta, weights):
    fresh = mom_rate * momenta + sums
    width = fresh.shape[1]
    block = jnp.arange(width) // HD
    same = block[:, None] == block[None, :]
    gram = jnp.where(same, contract_rows(fresh, fresh, highest), 0.0)
    square = jnp.sum(jnp.where(jnp.eye(width, dtype=bool), gram, 0.0), axis=0, keepdims=True)
    total = jnp.sum(jnp.where(same, square.T, 0.0), axis=0, keepdims=True)
    scale = 1.0 / (jnp.sqrt(total) + 1e-07)
    poly = polynomial(gram * scale * scale.T, 5, highest)
    ortho = jnp.dot(fresh * scale, poly, precision=highest)
    return fresh, step_weight(weights, ortho)


def expert_kernel(own_ref, arrived_ref, grads_ref, *refs_in_order):
    blocks, momenta, refs = refs_in_order[:8], refs_in_order[8:11], refs_in_order[11:]
    expert_steps(own_ref, arrived_ref, grads_ref, blocks, momenta, *refs)


def expert_steps(own_ref, arrived_ref, grads_ref, blocks, momenta, made_ref, back_ref, sums_ref,
                  weight_ref, rows_ref, hidden_ref, dgate_ref, dup_ref, dy_ref):
    expert = own_ref[0] + pl.program_id(0)
    level, side = own_ref[1], own_ref[2]
    width = D // 8

    def part(up, other):
        index = 2 * lax.rem(level + up, 4) + (1 - side if other else side)
        return pl.ds(pl.multiple_of(index * width, width), width)

    for index, up in enumerate((0, 3, 1, 2)):
        for other in range(2):
            for kind in range(3):
                weight_ref[kind, part(up, other)] = blocks[2 * index + other][kind, 0]
    full_gate, full_up, full_down = weight_ref[0], weight_ref[1], weight_ref[2]
    chunk = ROWS // CHUNKS
    seqs = chunk // CAP

    def forward(step, carry):
        first = pl.multiple_of(step * seqs, seqs)
        where = pl.ds(pl.multiple_of(step * chunk, chunk), chunk)
        both = arrived_ref[pl.ds(first, seqs), 0].reshape(chunk, D + WIDE)
        rows = both[:, :D]
        lane = lax.broadcasted_iota(jnp.int32, (chunk, WIDE), 1)
        pick = (lane % EXPERTS == expert) & (lane < 3 * EXPERTS)
        gate = jnp.sum(
            jnp.where(pick, both[:, D:].astype(jnp.float32), 0.0), axis=1, keepdims=True
        )
        gate_pre = mat(rows, full_gate)
        up_pre = mat(rows, full_up)
        sigma = jax.nn.sigmoid(gate_pre)
        activated = gate_pre * sigma
        hidden = (activated * up_pre).astype(jnp.bfloat16)
        made = contract_cols(hidden, full_down).astype(jnp.bfloat16)
        made_ref[pl.ds(first, seqs), 0] = made.reshape(seqs, CAP, D)
        slot_ids = lax.broadcasted_iota(jnp.int32, (LOCAL, CAP), 1).astype(jnp.float32) + 1.0
        token_lane = lax.broadcasted_iota(jnp.int32, (LOCAL, WIDE), 1)
        taken = []
        for seq in range(seqs):
            source = grads_ref[first + seq]
            places = jnp.where(token_lane == expert, source[:, D:].astype(jnp.float32), 0.0)
            chosen = jnp.sum(places, axis=1, keepdims=True) == slot_ids
            taken.append(contract_rows(chosen.astype(jnp.bfloat16), source[:, :D]))
        grad_f32 = jnp.concatenate(taken, axis=0)
        grad_made = (gate * grad_f32).astype(jnp.bfloat16)
        grad_gate_value = jnp.sum(made.astype(jnp.float32) * grad_f32, axis=1, keepdims=True)
        grad_hidden = mat(grad_made, full_down)
        grad_gate_pre = (
            grad_hidden * up_pre * sigma * (1.0 + gate_pre * (1.0 - sigma))
        ).astype(jnp.bfloat16)
        grad_up_pre = (grad_hidden * activated).astype(jnp.bfloat16)
        back = contract_cols(grad_gate_pre, full_gate) + contract_cols(grad_up_pre, full_up)
        back_ref[pl.ds(first, seqs), 0, :, :D] = back.astype(jnp.bfloat16).reshape(seqs, CAP, D)
        high, middle, low = [
            part.astype(jnp.float32) for part in three_parts(grad_gate_value)
        ]
        slot = jnp.where(
            lane < EXPERTS, high, jnp.where(lane < 2 * EXPERTS, middle, low)
        )
        back_ref[pl.ds(first, seqs), 0, :, D:] = (
            jnp.where(pick, slot, 0.0).astype(jnp.bfloat16).reshape(seqs, CAP, WIDE)
        )
        rows_ref[where] = rows
        hidden_ref[where] = hidden
        dgate_ref[where] = grad_gate_pre
        dup_ref[where] = grad_up_pre
        dy_ref[where] = grad_made
        return carry

    lax.fori_loop(0, CHUNKS, forward, 0)
    own_part = 2 * level + side
    pairs = ((rows_ref, dgate_ref), (rows_ref, dup_ref), (dy_ref, hidden_ref))
    for kind in range(3):
        slot = lax.rem(kind - level + 4, 4)
        left, right = pairs[kind]
        for index in range(D // width):
            rows = slice(index * width, (index + 1) * width)
            added = jnp.where(index == own_part, mom_rate, 0.0) * momenta[kind][0]
            total = contract_rows(left[:, rows], right[...]) + added
            sums_ref[slot, 0, rows] = total.astype(jnp.bfloat16)
    sums_ref[lax.rem(7 - level, 4), 0] = jnp.zeros((D, FF), jnp.bfloat16)


def expert_math(arrived, all_grads, weights, momenta):
    seqs, per_group = arrived.shape[:2]
    place = lax.axis_index("ctx")
    own = jnp.stack([lax.axis_index("exp") * per_group, place // 2, place % 2]).astype(jnp.int32)
    rows_each = D // 8

    def rows_spec(width):
        return pl.BlockSpec((seqs, 1, CAP, width), lambda e, own: (0, e, 0, 0))

    summed = pl.BlockSpec(
        (4, 1, D, FF), lambda e, own: (0, e + own[2] - 2 * e * own[2], 0, 0)
    )
    momentum = pl.BlockSpec((1, rows_each, FF), lambda e, own: (e, 0, 0))
    one = pl.BlockSpec((3, 1, rows_each, FF), lambda e, own: (0, e, 0, 0))
    whole = pl.BlockSpec(all_grads.shape, lambda e, own: (0, 0, 0))
    return pl.pallas_call(
        expert_kernel,
        grid_spec=pltpu.PrefetchScalarGridSpec(
            num_scalar_prefetch=1,
            grid=(per_group,),
            in_specs=[rows_spec(D + WIDE), whole] + [one] * 8 + [momentum] * 3,
            out_specs=[rows_spec(D), rows_spec(D + WIDE), summed],
            scratch_shapes=[
                pltpu.VMEM((3, D, FF), jnp.bfloat16),
                pltpu.VMEM((ROWS, D), jnp.bfloat16),
                pltpu.VMEM((ROWS, FF), jnp.bfloat16),
                pltpu.VMEM((ROWS, FF), jnp.bfloat16),
                pltpu.VMEM((ROWS, FF), jnp.bfloat16),
                pltpu.VMEM((ROWS, D), jnp.bfloat16),
            ],
        ),
        out_shape=[
            jax.ShapeDtypeStruct((seqs, per_group, CAP, D), jnp.bfloat16),
            jax.ShapeDtypeStruct((seqs, per_group, CAP, D + WIDE), jnp.bfloat16),
            jax.ShapeDtypeStruct((4, per_group, D, FF), jnp.bfloat16),
        ],
        compiler_params=pltpu.CompilerParams(vmem_limit_bytes=56 * 2**20),
        cost_estimate=pl.CostEstimate(
            flops=18 * ROWS * per_group * D * FF,
            bytes_accessed=30 * 2**20,
            transcendentals=ROWS * per_group * FF,
        ),
        name="experts",
    )(own, arrived, all_grads, *weights, *momenta)


def split_two(value):
    high = value.astype(jnp.bfloat16)
    return high, (value - high.astype(jnp.float32)).astype(jnp.bfloat16)


def mat_three(left, right):
    return mat(left[0], right[0]) + (mat(left[0], right[1]) + mat(left[1], right[0]))


def owner_kernel(place_ref, matrix_ref, keep_ref, cross_ref, gram_ref, total_ref, ortho_ref):
    gram = contract_rows(matrix_ref[...], matrix_ref[...])
    width = gram_ref.shape[0]
    row = lax.broadcasted_iota(jnp.int32, (width, width), 0)
    column = lax.broadcasted_iota(jnp.int32, (width, width), 1)
    eye = (row == column).astype(jnp.float32)
    square = jnp.sum(jnp.sum(eye * gram, axis=1, keepdims=True), axis=0, keepdims=True)
    scale = 1.0 / (jnp.sqrt(square) + 1e-07)
    gram_ref[...] = gram * scale * scale
    total_ref[...] = eye

    def step(index, carry):
        gram = gram_ref[...]
        gram_two = split_two(gram)
        factor = coef_one * eye + coef_two * gram + coef_three * mat_three(gram_two, gram_two)
        factor_two = split_two(factor)
        total_ref[...] = mat_three(factor_two, split_two(total_ref[...]))
        gram_ref[...] = mat_three(split_two(mat_three(factor_two, gram_two)), factor_two)
        return carry

    lax.fori_loop(0, 5, step, 0)
    high, low = split_two(total_ref[...])
    matrix = matrix_ref[...]
    ortho_ref[...] = ((mat(matrix, high) + mat(matrix, low)) * scale).astype(ortho_ref.dtype)
    level, side = place_ref[0], place_ref[1]
    rows = keep_ref.shape[2]
    for up in range(4):
        for ref, column in ((keep_ref, side), (cross_ref, 1 - side)):
            index = 2 * lax.rem(level + up, 4) + column
            where = pl.ds(pl.multiple_of(index * rows, rows), rows)
            ref[up, 0] = matrix_ref[where]
            ref[up, 1] = ortho_ref[where]


def owner_orthogonal(matrix, place):
    rows, width = matrix.shape
    whole = pl.BlockSpec(memory_space=pltpu.VMEM)
    sent = jax.ShapeDtypeStruct((4, 2, rows // 8, width), jnp.bfloat16)
    return pl.pallas_call(
        owner_kernel,
        out_shape=[sent, sent],
        in_specs=[pl.BlockSpec(memory_space=pltpu.SMEM), whole],
        out_specs=[whole, whole],
        scratch_shapes=[
            pltpu.VMEM((width, width), jnp.float32),
            pltpu.VMEM((width, width), jnp.float32),
            pltpu.VMEM((rows, width), jnp.bfloat16),
        ],
        compiler_params=pltpu.CompilerParams(vmem_limit_bytes=48 * 2**20),
        cost_estimate=pl.CostEstimate(
            flops=6 * (22 * width**3 + 2 * rows * width**2),
            bytes_accessed=6 * rows * width,
            transcendentals=0,
        ),
        name="owner",
    )(place, matrix)


def probabilities(queries, keys, first):
    scores = contract_cols(queries, keys) * HD ** (-0.5)
    token = lax.broadcasted_iota(jnp.int32, scores.shape, 0) % (scores.shape[0] // 2)
    key = lax.broadcasted_iota(jnp.int32, scores.shape, 1)
    scores = jnp.where(key <= first + token, scores, -1e30)
    running_max = jnp.max(scores, axis=1, keepdims=True)
    raised = jnp.exp(scores - running_max)
    return raised * (1.0 / jnp.sum(raised, axis=1, keepdims=True))


def two_heads(block, group):
    left = block[:, 2 * group * HD : (2 * group + 1) * HD]
    right = block[:, (2 * group + 1) * HD : (2 * group + 2) * HD]
    return jnp.concatenate([left, right], axis=0)


def side_by_side(stacked):
    half = stacked.shape[0] // 2
    return jnp.concatenate([stacked[:half], stacked[half:]], axis=1)


def attend_kernel(first_ref, query_ref, key_ref, value_ref, mixed_ref):
    queries, keys, values = query_ref[...], key_ref[...], value_ref[...]
    mixed = []
    for group in range(2):
        columns = slice(group * HD, (group + 1) * HD)
        weights = probabilities(two_heads(queries, group), keys[:, columns], first_ref[0])
        mixed.append(side_by_side(mat(weights.astype(jnp.bfloat16), values[:, columns])))
    mixed_ref[...] = jnp.concatenate(mixed, axis=1).astype(mixed_ref.dtype)


def attend_back_kernel(
    first_ref, query_ref, key_ref, value_ref, grad_ref, dquery_ref, dkey_ref, dvalue_ref
):
    queries, keys, values, grads = query_ref[...], key_ref[...], value_ref[...], grad_ref[...]
    dquery, dkey, dvalue = [], [], []
    for group in range(2):
        columns = slice(group * HD, (group + 1) * HD)
        query, grad = two_heads(queries, group), two_heads(grads, group)
        weights = probabilities(query, keys[:, columns], first_ref[0])
        grad_weights = contract_cols(grad, values[:, columns])
        inner = jnp.sum(weights * grad_weights, axis=1, keepdims=True)
        grad_scores = (weights * (grad_weights - inner)).astype(jnp.bfloat16)
        dquery.append(side_by_side(mat(grad_scores, keys[:, columns]) * HD ** (-0.5)))
        dkey.append(contract_rows(grad_scores, query) * HD ** (-0.5))
        dvalue.append(contract_rows(weights.astype(jnp.bfloat16), grad))
    dquery_ref[...] = jnp.concatenate(dquery, axis=1)
    dkey_ref[...] = jnp.concatenate(dkey, axis=1).astype(dkey_ref.dtype)
    dvalue_ref[...] = jnp.concatenate(dvalue, axis=1).astype(dvalue_ref.dtype)


def attention_call(kernel, operands, grads, first, name):
    queries, all_kv = operands
    rows, keys = queries.shape[0], all_kv.shape[0]
    steps = KV // 2
    wide = pl.BlockSpec((rows, 4 * HD), lambda g, first: (0, g))
    key_spec = pl.BlockSpec((keys, 2 * HD), lambda g, first: (0, g))
    value_spec = pl.BlockSpec((keys, 2 * HD), lambda g, first: (0, g + steps))
    if grads is None:
        arrays, specs = (queries, all_kv, all_kv), [wide, key_spec, value_spec]
        out_shape = jax.ShapeDtypeStruct(queries.shape, jnp.bfloat16)
        out_specs = wide
    else:
        arrays, specs = (queries, all_kv, all_kv, grads), [wide, key_spec, value_spec, wide]
        out_shape = [
            jax.ShapeDtypeStruct(queries.shape, jnp.float32),
            jax.ShapeDtypeStruct((keys, KV * HD), jnp.bfloat16),
            jax.ShapeDtypeStruct((keys, KV * HD), jnp.bfloat16),
        ]
        out_specs = [wide, key_spec, key_spec]
    factor = 4 if grads is None else 10
    return pl.pallas_call(
        kernel,
        grid_spec=pltpu.PrefetchScalarGridSpec(
            num_scalar_prefetch=1, grid=(steps,), in_specs=specs, out_specs=out_specs
        ),
        out_shape=out_shape,
        compiler_params=pltpu.CompilerParams(vmem_limit_bytes=48 * 2**20),
        cost_estimate=pl.CostEstimate(
            flops=factor * rows * keys * HEADS * HD,
            bytes_accessed=4 * 2**20,
            transcendentals=rows * keys * HEADS,
        ),
        name=name,
    )(first.astype(jnp.int32).reshape(1), *arrays)


def body(
    tokens,
    cotangent,
    routes,
    query_weight,
    kv_weight,
    output_weight,
    router,
    gains,
    gate_weight,
    up_weight,
    down_weight,
    query_momentum,
    kv_momentum,
    output_momentum,
    gate_momentum,
    up_momentum,
    down_momentum,
    router_first,
    router_second,
    gains_first,
    gains_second,
):
    bf16 = jnp.bfloat16
    ctx_count = lax.axis_size("ctx")
    exp_count = lax.axis_size("exp")
    exp_index = lax.axis_index("exp")
    row_count = tokens.shape[1]
    per_group = EXPERTS // exp_count
    inputs = tokens[0].astype(jnp.float32)
    grad_out = cotangent[0].astype(jnp.float32)
    route_ids = routes[0]

    packed = jnp.concatenate(
        [
            jnp.concatenate([query_weight, kv_weight], axis=1).T,
            router.astype(bf16).T,
            jnp.pad(gains.astype(bf16).reshape(1, -1), ((0, 0), (0, D - 2 * HD))),
            jnp.zeros((5, D), bf16),
        ],
        axis=0,
    )
    own_experts = jnp.stack([gate_weight, up_weight, down_weight])
    row_y, far_x, core = exp_index // 4, (exp_index // 2) % 2, exp_index % 2
    packed_far = exp_move(packed, 0, 1, 0)
    other_experts = ctx_move(own_experts, 0, 1)
    below, above = ctx_move(own_experts, 1, 0), ctx_move(own_experts, 3, 0)
    pair = jnp.stack(
        [
            jnp.where(far_x == 0, packed, packed_far),
            jnp.where(far_x == 0, packed_far, packed),
        ]
    )
    from_below, from_above = exp_move(pair, 1, 0, 0), exp_move(pair, 3, 0, 0)
    from_below, from_above, other_experts, below, above = lax.optimization_barrier(
        (from_below, from_above, other_experts, below, above)
    )
    below_other, above_other = ctx_move(other_experts, 1, 0), ctx_move(other_experts, 3, 0)
    far = ctx_move(below, 1, 0)
    from_two = jnp.stack([exp_move(from_below[0], 1, 0, 0), exp_move(from_above[1], 3, 0, 0)])
    mine = jnp.stack([pair, from_above, from_two, from_below])
    other = exp_move(mine, 0, 0, 1)

    def ordered(left, right, axis):
        both = jnp.stack(
            [jnp.where(core == 0, left, right), jnp.where(core == 0, right, left)], axis=axis + 2
        )
        return ring_order(both, row_y, axis)

    packed_rows = packed.shape[0]
    mine_flat = mine.reshape(8 * packed_rows, D)
    other_flat = other.reshape(8 * packed_rows, D)
    full_router = ordered(
        mine[:, :, 2 * HD : 2 * HD + per_group], other[:, :, 2 * HD : 2 * HD + per_group], 0
    ).reshape(EXPERTS, D)
    gains_row = 2 * HD + per_group
    full_gains = ordered(mine[:, :, gains_row, : 2 * HD], other[:, :, gains_row, : 2 * HD], 0)
    full_gains = full_gains.reshape(exp_count, 2, HD).transpose(1, 0, 2).reshape(2, D)
    gain_one = full_gains[0].astype(jnp.float32)
    gain_two = full_gains[1].astype(jnp.float32)

    full_output = lax.all_gather(output_weight.T, "exp", axis=0, tiled=True)

    expert_ids = jnp.arange(EXPERTS, dtype=jnp.int32)
    named = jnp.any(route_ids[:, :, None] == expert_ids[None, None, :], axis=1)
    named_low = named.astype(bf16)
    token_ids = jnp.arange(row_count)
    earlier = (token_ids[None, :] < token_ids[:, None]).astype(bf16)
    rank = mat(earlier, named_low)
    place = jnp.where(named, rank + 1.0, 0.0).astype(bf16)
    slot_ids = jnp.arange(EXPERTS * CAP, dtype=jnp.int32)
    widen = (slot_ids[None, :] // CAP == expert_ids[:, None]).astype(bf16)
    chosen_slot = mat(place, widen) == (slot_ids % CAP + 1).astype(jnp.float32)[None, :]
    select = chosen_slot.astype(bf16)

    sent_grads = jnp.concatenate(
        [cotangent[0], place, jnp.zeros((row_count, WIDE - EXPERTS), bf16)], axis=1
    )
    all_grads = lax.all_gather(sent_grads, "exp", axis=0, tiled=False)

    inv_one = lax.rsqrt(jnp.mean(inputs * inputs, axis=-1, keepdims=True) + eps_norm)
    normed_one = (inputs * inv_one * gain_one).astype(bf16)
    halves = [
        contract_cols(normed_one, flat).reshape(row_count, 4, 2, packed_rows)[..., : 2 * HD]
        for flat in (mine_flat, other_flat)
    ]
    projected = ordered(*halves, 1).reshape(row_count, exp_count, 2 * HD)
    query_raw = projected[:, :, :HD]
    kv_raw = projected[:, :, HD:]
    first_row = lax.axis_index("ctx") * row_count
    cosine, sine = rope_tables(first_row, row_count)
    queries = rotate(query_raw, cosine, sine).astype(bf16)
    keys = rotate(kv_raw[:, :KV], cosine, sine).astype(bf16)
    values = kv_raw[:, KV:].astype(bf16)
    sent_kv = jnp.concatenate([keys, values], axis=1).reshape(row_count, 2 * KV * HD)
    all_kv = spread(sent_kv, "ctx", None, ctx_count).reshape(ctx_count * row_count, 2 * KV * HD)
    flat_queries = queries.reshape(row_count, HEADS * HD)
    mixed_low = attention_call(attend_kernel, (flat_queries, all_kv), None, first_row, "attend")
    sent_mixed = mixed_low.reshape(row_count, exp_count, HD).transpose(1, 0, 2)
    sent_mixed = sent_mixed.reshape(exp_count, row_count // 2, 2 * HD)
    attended = mat(mixed_low, full_output)
    residual = inputs + attended
    inv_two = lax.rsqrt(jnp.mean(residual * residual, axis=-1, keepdims=True) + eps_norm)
    normed_two = (residual * inv_two * gain_two).astype(bf16)
    logits = contract_cols(normed_two, full_router)
    gates = jax.nn.softmax(jnp.where(named, logits, -1e30), axis=-1)
    gates = jnp.where(named, gates, 0.0)
    gate_parts = three_parts(gates)
    extended = jnp.concatenate(
        [normed_two, *gate_parts, jnp.zeros((row_count, WIDE - 3 * EXPERTS), bf16)], axis=1
    )
    sent_rows = contract_rows(select, extended).astype(bf16)
    sent_rows, below_other, above_other, far = lax.optimization_barrier(
        (sent_rows, below_other, above_other, far)
    )
    far_other = ctx_move(above_other, 3, 0)
    arrived = exchange(sent_rows.reshape(exp_count, per_group * CAP, D + WIDE), "exp")
    later_normed, arrived, far_other = lax.optimization_barrier((normed_one, arrived, far_other))
    full_experts = (
        own_experts, other_experts, below, below_other, above, above_other, far, far_other
    )
    all_normed = lax.all_gather(later_normed, "exp", axis=0, tiled=True)
    produced, back, expert_grads = expert_math(
        arrived.reshape(exp_count, per_group, CAP, D + WIDE),
        all_grads,
        full_experts,
        (gate_momentum, up_momentum, down_momentum),
    )
    head_mixed = exchange(after(sent_mixed, arrived), "exp")
    back, head_mixed = lax.optimization_barrier((back, head_mixed))
    head_mixed = head_mixed.reshape(exp_count * row_count, HD)
    returned = exchange(back.reshape(exp_count, per_group * CAP, D + WIDE), "exp")
    returned = returned.reshape(EXPERTS * CAP, D + WIDE)
    far_up, far_down = ctx_move(expert_grads[2, 0], 1, 0), ctx_move(expert_grads[2, 1], 3, 0)
    sum_up = jnp.stack([plus(expert_grads[1, 0], far_up), expert_grads[1, 1]])
    sum_down = jnp.stack([expert_grads[3, 0], plus(expert_grads[3, 1], far_down)])
    returned = after(returned, sum_up, sum_down)
    sum_up, sum_down = owner_move(sum_up, 1), owner_move(sum_down, 3)
    produced = after(produced, returned)
    route_values = exchange(produced.reshape(exp_count, per_group * CAP, D), "exp")
    summed_back = mat(select, returned)
    tail = summed_back[:, D:]
    grad_gates = (
        tail[:, :EXPERTS] + tail[:, EXPERTS : 2 * EXPERTS] + tail[:, 2 * EXPERTS : 3 * EXPERTS]
    )
    grad_logits = (
        gates * (grad_gates - jnp.sum(gates * grad_gates, axis=-1, keepdims=True))
    ).astype(bf16)
    grad_normed_two = summed_back[:, :D] + mat(grad_logits, full_router)
    scaled_two = grad_normed_two * gain_two
    grad_gain_two = jnp.sum(grad_normed_two * residual * inv_two, axis=0)
    grad_residual = (
        grad_out
        + inv_two * scaled_two
        - residual * inv_two**3 * jnp.mean(scaled_two * residual, axis=-1, keepdims=True)
    )
    grad_attended = grad_residual.astype(bf16)
    all_attended = lax.all_gather(grad_attended, "exp", axis=0, tiled=True)
    grad_attended = after(grad_attended, sum_up, sum_down)
    both_sums = (
        expert_grads[0].astype(jnp.float32)
        + sum_up.astype(jnp.float32)
        + sum_down.astype(jnp.float32)
    )
    other_sums = ctx_move(both_sums[1].astype(bf16), 0, 1)
    grad_mixed = contract_cols(grad_attended, full_output).astype(bf16)
    grad_queries, key_terms, value_terms = attention_call(
        attend_back_kernel, (flat_queries, all_kv), grad_mixed, first_row, "attend_back"
    )
    kv_terms = jnp.concatenate([key_terms, value_terms], axis=1)
    kv_terms, route_values = lax.optimization_barrier((kv_terms, route_values))
    kv_terms = exchange(kv_terms.reshape(ctx_count, row_count, 2 * KV * HD), "ctx")
    grad_query_raw = rotate(
        grad_queries.reshape(row_count, HEADS, HD), cosine, -sine
    ).astype(bf16)
    kv_sums = jnp.sum(kv_terms.astype(jnp.float32), axis=0).reshape(row_count, 2 * KV, HD)
    grad_key_raw = rotate(kv_sums[:, :KV], cosine, -sine).astype(bf16)
    grad_kv_raw = jnp.concatenate([grad_key_raw, kv_sums[:, KV:].astype(bf16)], axis=1)
    grad_projected = jnp.concatenate([grad_query_raw, grad_kv_raw], axis=2)
    by_core = ring_order(grad_projected.reshape(row_count, 4, 2, 2, 2 * HD), -row_y, 1)
    by_core = jnp.pad(by_core, ((0, 0),) * 4 + ((0, packed_rows - 2 * HD),))
    first_core, second_core = by_core[:, :, :, 0], by_core[:, :, :, 1]
    grad_normed_one = mat(
        jnp.where(core == 0, first_core, second_core).reshape(row_count, -1), mine_flat
    ) + mat(jnp.where(core == 0, second_core, first_core).reshape(row_count, -1), other_flat)
    scaled_one = grad_normed_one * gain_one
    grad_gain_one = jnp.sum(grad_normed_one * inputs * inv_one, axis=0)
    input_grad = (
        grad_residual
        + inv_one * scaled_one
        - inputs * inv_one**3 * jnp.mean(scaled_one * inputs, axis=-1, keepdims=True)
    )

    small_rows = (per_group * D + 2 * HD) // (2 * HD)
    small = jnp.concatenate(
        [
            contract_rows(grad_logits, normed_two).reshape(exp_count, -1, 2 * HD),
            jnp.stack([grad_gain_one, grad_gain_two])
            .reshape(2, exp_count, HD)
            .transpose(1, 0, 2)
            .reshape(exp_count, 1, 2 * HD),
            jnp.zeros((exp_count, 7, 2 * HD), jnp.float32),
        ],
        axis=1,
    ).astype(bf16)
    route_values = route_values.reshape(EXPERTS * CAP, D)
    head_send = jnp.concatenate([jnp.transpose(grad_projected, (1, 0, 2)), small], axis=1)
    level, side = lax.axis_index("ctx") // 2, lax.axis_index("ctx") % 2
    owned = (both_sums[0] + other_sums.astype(jnp.float32)).astype(bf16)
    head_send, owned = lax.optimization_barrier((head_send, owned))
    head_grads = exchange(head_send, "exp")
    keep, cross = owner_orthogonal(owned, jnp.stack([level, side]).astype(jnp.int32))
    head_grads = after(head_grads, keep, cross)
    crossed = ctx_move(cross, 0, 1)
    small = jnp.sum(head_grads[:, row_count : row_count + small_rows].astype(jnp.float32), axis=0)
    head_grads = head_grads[:, :row_count].reshape(exp_count * row_count, 2 * HD)

    part = jnp.concatenate(
        [
            mat(lax.optimization_barrier(head_grads.T), all_normed),
            mat(lax.optimization_barrier(head_mixed.T), all_attended),
        ],
        axis=0,
    )
    width = D // ctx_count
    part = jnp.concatenate(
        [
            jnp.transpose(part.astype(bf16).reshape(3 * HD, ctx_count, width), (1, 0, 2)),
            jnp.broadcast_to(
                jnp.pad(small.astype(bf16), ((0, 7), (0, 0)))[None], (ctx_count, 24, width)
            ),
        ],
        axis=1,
    )
    part, crossed = lax.optimization_barrier((exchange(part, "ctx"), crossed))
    returned_rows = [
        ctx_move(jnp.stack([keep[up], crossed[up]]), up, 0) if up else jnp.stack([keep[0], crossed[0]])
        for up in range(4)
    ]
    part = jnp.sum(part.astype(jnp.float32), axis=0)
    sums = spread(part[: 3 * HD].astype(bf16), "ctx", None, ctx_count)
    sums = jnp.transpose(sums, (0, 2, 1)).reshape(D, 3 * HD).astype(jnp.float32)
    small = part[3 * HD : 3 * HD + small_rows]
    sum_router = small[:-1].reshape(per_group, D).T
    sum_gains = small[-1].reshape(2, HD)
    router_one, router_two, router_new = adam_update(
        router, router_first, router_second, sum_router, router_rate, decay_rate
    )
    gains_one, gains_two, gains_new = adam_update(
        gains, gains_first, gains_second, sum_gains, gain_rate, 0.0
    )

    head_fresh, head_new = head_blocks(
        sums,
        jnp.concatenate([query_momentum, kv_momentum, output_momentum], axis=1),
        jnp.concatenate([query_weight, kv_weight, output_weight], axis=1),
    )

    returned_rows = jnp.stack(returned_rows).reshape(8, 2, D // ctx_count, -1)
    fresh, ortho = [], []
    for kind in range(3):
        picked = [
            lax.dynamic_index_in_dim(
                returned_rows,
                2 * ((level + 4 - kind) % 4) + (expert + side) % 2,
                0,
                keepdims=False,
            ).astype(jnp.float32)
            for expert in range(per_group)
        ]
        fresh.append(jnp.stack([rows[0] for rows in picked]))
        ortho.append(jnp.stack([rows[1] for rows in picked]))
    new = [
        step_weight(weight, factor)
        for weight, factor in zip((gate_weight, up_weight, down_weight), ortho)
    ]

    gates_wide = [mat(part, widen) for part in gate_parts]
    block_value = residual
    for wide in gates_wide:
        weighted = jnp.where(chosen_slot, wide, 0.0).astype(bf16)
        block_value = block_value + mat(weighted, route_values)
    return (
        block_value.astype(bf16)[None],
        input_grad[None],
        head_fresh[:, :HD],
        head_new[:, :HD],
        head_fresh[:, HD : 2 * HD],
        head_new[:, HD : 2 * HD],
        head_fresh[:, 2 * HD :],
        head_new[:, 2 * HD :],
        fresh[0],
        new[0],
        fresh[1],
        new[1],
        fresh[2],
        new[2],
        router_one,
        router_two,
        router_new,
        gains_one,
        gains_two,
        gains_new,
    )


def solution(mesh):
    return jax.shard_map(
        body,
        mesh=mesh,
        in_specs=(
            P("exp", "ctx", None),
            P("exp", "ctx", None),
            P("exp", "ctx", None),
            P(None, "exp"),
            P(None, "exp"),
            P(None, "exp"),
            P(None, "exp"),
            P(None, "exp"),
            P("exp", "ctx", None),
            P("exp", "ctx", None),
            P("exp", "ctx", None),
            P(None, "exp"),
            P(None, "exp"),
            P(None, "exp"),
            P("exp", "ctx", None),
            P("exp", "ctx", None),
            P("exp", "ctx", None),
            P(None, "exp"),
            P(None, "exp"),
            P(None, "exp"),
            P(None, "exp"),
        ),
        out_specs=(
            P("exp", "ctx", None),
            P("exp", "ctx", None),
            P(None, "exp"),
            P(None, "exp"),
            P(None, "exp"),
            P(None, "exp"),
            P(None, "exp"),
            P(None, "exp"),
            P("exp", "ctx", None),
            P("exp", "ctx", None),
            P("exp", "ctx", None),
            P("exp", "ctx", None),
            P("exp", "ctx", None),
            P("exp", "ctx", None),
            P(None, "exp"),
            P(None, "exp"),
            P(None, "exp"),
            P(None, "exp"),
            P(None, "exp"),
            P(None, "exp"),
        ),
        check_vma=False,
    )
```

```python
import math

import jax
import jax.numpy as jnp
from jax import lax
from jax.experimental import pallas as pl
from jax.experimental.pallas import tpu as pltpu
from jax.sharding import PartitionSpec as P

D = 1024
HEADS = 16
KV = 8
HD = 64
TOP = 8
STEP = 10


eps_norm = 1e-05
rope_base = 10000.0
mom_rate = 0.95
muon_rate = 0.15
decay_rate = 0.1
adam_one = 0.9
adam_two = 0.95
adam_eps = 1e-08
router_rate = 0.015
gain_rate = 0.2
coef_one = 3.4445
coef_two = -4.775
coef_three = 2.0315
highest = lax.Precision.HIGHEST


def rope_tables(first_row, token_count):
    half_width = HD // 2
    frequency = rope_base ** (-jnp.arange(half_width, dtype=jnp.float32) * 2.0 / HD)
    position = (first_row + jnp.arange(token_count, dtype=jnp.int32)).astype(jnp.float32)
    angle_grid = position[:, None] * frequency[None, :]
    return (jnp.cos(angle_grid), jnp.sin(angle_grid))


def rotate(vector, cosine, sine):
    half_width = vector.shape[-1] // 2
    front_half = vector[..., :half_width]
    back_half = vector[..., half_width:]
    cos_rows = cosine[:, None, :]
    sin_rows = sine[:, None, :]
    return jnp.concatenate(
        [
            front_half * cos_rows - back_half * sin_rows,
            back_half * cos_rows + front_half * sin_rows,
        ],
        axis=-1,
    )


EXPERTS = 32
CAP = 48
WIDE = 128
FF = 512
ROWS = 16 * CAP
CHUNKS = 2
LOCAL = 128


def exchange(blocks, axis, groups=None):
    return lax.all_to_all(
        blocks, axis, split_axis=0, concat_axis=0, tiled=True, axis_index_groups=groups
    )


def spread(block, axis, groups=None, count=8):
    return exchange(jnp.broadcast_to(block[None], (count,) + block.shape), axis, groups)


def parity_groups(count):
    return [list(range(core, count, 2)) for core in range(2)]


def core_swap(block, count):
    return lax.ppermute(block, "exp", [(i, i ^ 1) for i in range(count)])


def ctx_move(block, up, other):
    pairs = [
        (2 * z + x, 2 * ((z + up) % 4) + (x ^ other)) for z in range(4) for x in range(2)
    ]
    return lax.ppermute(block, "ctx", pairs)


def plus(left, right):
    return (left.astype(jnp.float32) + right.astype(jnp.float32)).astype(jnp.bfloat16)


def owner_move(block, up):
    pairs = [
        (2 * z + x, 2 * ((z + up) % 4) + x) for z in range(4) for x in range(2) if (z + up) % 4 < 3
    ]
    return lax.ppermute(block, "ctx", pairs)


def exp_move(block, up, far, core):
    pairs = [
        (4 * y + 2 * h + c, 4 * ((y + up) % 4) + 2 * (h ^ far) + (c ^ core))
        for y in range(4)
        for h in range(2)
        for c in range(2)
    ]
    return lax.ppermute(block, "exp", pairs)


def ring_order(blocks, shift, axis):
    double = jnp.concatenate([blocks, blocks], axis=axis)
    return lax.dynamic_slice_in_dim(double, (4 - shift) % 4, 4, axis)


def after(value, *others):
    return lax.optimization_barrier((value,) + others)[0]


def three_parts(value):
    high = value.astype(jnp.bfloat16)
    rest = value - high.astype(jnp.float32)
    middle = rest.astype(jnp.bfloat16)
    low = (rest - middle.astype(jnp.float32)).astype(jnp.bfloat16)
    return high, middle, low


def polynomial(gram, steps, precision):
    total = None
    for step in range(steps):
        square = jnp.matmul(gram, gram, precision=precision)
        eye = jnp.eye(gram.shape[-1], dtype=jnp.float32)
        factor = coef_one * eye + coef_two * gram + coef_three * square
        total = factor if total is None else jnp.matmul(factor, total, precision=precision)
        if step < steps - 1:
            gram = jnp.matmul(
                jnp.matmul(factor, gram, precision=precision), factor, precision=precision
            )
    return total


def step_weight(weight, ortho):
    return (
        weight.astype(jnp.float32) * (1.0 - muon_rate * decay_rate)
        - muon_rate * 0.2 * math.sqrt(D) * ortho
    )


def adam_update(param, first, second, grad, rate, decay):
    first = adam_one * first + (1.0 - adam_one) * grad
    second = adam_two * second + (1.0 - adam_two) * grad * grad
    fixed_one = first / (1.0 - adam_one**STEP)
    fixed_two = second / (1.0 - adam_two**STEP)
    return (
        first,
        second,
        param * (1.0 - rate * decay) - rate * fixed_one / (jnp.sqrt(fixed_two) + adam_eps),
    )


def contract_rows(left, right, precision=None):
    return lax.dot_general(
        left,
        right,
        (((0,), (0,)), ((), ())),
        preferred_element_type=jnp.float32,
        precision=precision,
    )


def contract_cols(left, right):
    return lax.dot_general(
        left, right, (((1,), (1,)), ((), ())), preferred_element_type=jnp.float32
    )


def mat(left, right):
    return jnp.dot(left, right, preferred_element_type=jnp.float32)


def head_blocks(sums, momenta, weights):
    fresh = mom_rate * momenta + sums
    width = fresh.shape[1]
    block = jnp.arange(width) // HD
    same = block[:, None] == block[None, :]
    gram = jnp.where(same, contract_rows(fresh, fresh, highest), 0.0)
    square = jnp.sum(jnp.where(jnp.eye(width, dtype=bool), gram, 0.0), axis=0, keepdims=True)
    total = jnp.sum(jnp.where(same, square.T, 0.0), axis=0, keepdims=True)
    scale = 1.0 / (jnp.sqrt(total) + 1e-07)
    poly = polynomial(gram * scale * scale.T, 5, highest)
    ortho = jnp.dot(fresh * scale, poly, precision=highest)
    return fresh, step_weight(weights, ortho)


def expert_kernel(own_ref, arrived_ref, grads_ref, *refs_in_order):
    blocks, momenta, refs = refs_in_order[:8], refs_in_order[8:11], refs_in_order[11:]
    expert_steps(own_ref, arrived_ref, grads_ref, blocks, momenta, *refs)


def expert_steps(own_ref, arrived_ref, grads_ref, blocks, momenta, made_ref, back_ref, sums_ref,
                  weight_ref, rows_ref, hidden_ref, dgate_ref, dup_ref, dy_ref):
    expert = own_ref[0] + pl.program_id(0)
    level, side = own_ref[1], own_ref[2]
    width = D // 8

    def part(up, other):
        index = 2 * lax.rem(level + up, 4) + (1 - side if other else side)
        return pl.ds(pl.multiple_of(index * width, width), width)

    for index, up in enumerate((0, 3, 1, 2)):
        for other in range(2):
            for kind in range(3):
                weight_ref[kind, part(up, other)] = blocks[2 * index + other][kind, 0]
    full_gate, full_up, full_down = weight_ref[0], weight_ref[1], weight_ref[2]
    chunk = ROWS // CHUNKS
    seqs = chunk // CAP

    def forward(step, carry):
        first = pl.multiple_of(step * seqs, seqs)
        where = pl.ds(pl.multiple_of(step * chunk, chunk), chunk)
        both = arrived_ref[pl.ds(first, seqs), 0].reshape(chunk, D + WIDE)
        rows = both[:, :D]
        lane = lax.broadcasted_iota(jnp.int32, (chunk, WIDE), 1)
        pick = (lane % EXPERTS == expert) & (lane < 3 * EXPERTS)
        gate = jnp.sum(
            jnp.where(pick, both[:, D:].astype(jnp.float32), 0.0), axis=1, keepdims=True
        )
        gate_pre = mat(rows, full_gate)
        up_pre = mat(rows, full_up)
        sigma = jax.nn.sigmoid(gate_pre)
        activated = gate_pre * sigma
        hidden = (activated * up_pre).astype(jnp.bfloat16)
        made = contract_cols(hidden, full_down).astype(jnp.bfloat16)
        made_ref[pl.ds(first, seqs), 0] = made.reshape(seqs, CAP, D)
        slot_ids = lax.broadcasted_iota(jnp.int32, (LOCAL, CAP), 1).astype(jnp.float32) + 1.0
        token_lane = lax.broadcasted_iota(jnp.int32, (LOCAL, WIDE), 1)
        taken = []
        for seq in range(seqs):
            source = grads_ref[first + seq]
            places = jnp.where(token_lane == expert, source[:, D:].astype(jnp.float32), 0.0)
            chosen = jnp.sum(places, axis=1, keepdims=True) == slot_ids
            taken.append(contract_rows(chosen.astype(jnp.bfloat16), source[:, :D]))
        grad_f32 = jnp.concatenate(taken, axis=0)
        grad_made = (gate * grad_f32).astype(jnp.bfloat16)
        grad_gate_value = jnp.sum(made.astype(jnp.float32) * grad_f32, axis=1, keepdims=True)
        grad_hidden = mat(grad_made, full_down)
        grad_gate_pre = (
            grad_hidden * up_pre * sigma * (1.0 + gate_pre * (1.0 - sigma))
        ).astype(jnp.bfloat16)
        grad_up_pre = (grad_hidden * activated).astype(jnp.bfloat16)
        back = contract_cols(grad_gate_pre, full_gate) + contract_cols(grad_up_pre, full_up)
        back_ref[pl.ds(first, seqs), 0, :, :D] = back.astype(jnp.bfloat16).reshape(seqs, CAP, D)
        high, middle, low = [
            part.astype(jnp.float32) for part in three_parts(grad_gate_value)
        ]
        slot = jnp.where(
            lane < EXPERTS, high, jnp.where(lane < 2 * EXPERTS, middle, low)
        )
        back_ref[pl.ds(first, seqs), 0, :, D:] = (
            jnp.where(pick, slot, 0.0).astype(jnp.bfloat16).reshape(seqs, CAP, WIDE)
        )
        rows_ref[where] = rows
        hidden_ref[where] = hidden
        dgate_ref[where] = grad_gate_pre
        dup_ref[where] = grad_up_pre
        dy_ref[where] = grad_made
        return carry

    lax.fori_loop(0, CHUNKS, forward, 0)
    own_part = 2 * level + side
    pairs = ((rows_ref, dgate_ref), (rows_ref, dup_ref), (dy_ref, hidden_ref))
    for kind in range(3):
        slot = lax.rem(kind - level + 4, 4)
        left, right = pairs[kind]
        for index in range(D // width):
            rows = slice(index * width, (index + 1) * width)
            added = jnp.where(index == own_part, mom_rate, 0.0) * momenta[kind][0]
            total = contract_rows(left[:, rows], right[...]) + added
            sums_ref[slot, 0, rows] = total.astype(jnp.bfloat16)
    sums_ref[lax.rem(7 - level, 4), 0] = jnp.zeros((D, FF), jnp.bfloat16)


def expert_math(arrived, all_grads, weights, momenta):
    seqs, per_group = arrived.shape[:2]
    place = lax.axis_index("ctx")
    own = jnp.stack([lax.axis_index("exp") * per_group, place // 2, place % 2]).astype(jnp.int32)
    rows_each = D // 8

    def rows_spec(width):
        return pl.BlockSpec((seqs, 1, CAP, width), lambda e, own: (0, e, 0, 0))

    summed = pl.BlockSpec(
        (4, 1, D, FF), lambda e, own: (0, e + own[2] - 2 * e * own[2], 0, 0)
    )
    momentum = pl.BlockSpec((1, rows_each, FF), lambda e, own: (e, 0, 0))
    one = pl.BlockSpec((3, 1, rows_each, FF), lambda e, own: (0, e, 0, 0))
    whole = pl.BlockSpec(all_grads.shape, lambda e, own: (0, 0, 0))
    return pl.pallas_call(
        expert_kernel,
        grid_spec=pltpu.PrefetchScalarGridSpec(
            num_scalar_prefetch=1,
            grid=(per_group,),
            in_specs=[rows_spec(D + WIDE), whole] + [one] * 8 + [momentum] * 3,
            out_specs=[rows_spec(D), rows_spec(D + WIDE), summed],
            scratch_shapes=[
                pltpu.VMEM((3, D, FF), jnp.bfloat16),
                pltpu.VMEM((ROWS, D), jnp.bfloat16),
                pltpu.VMEM((ROWS, FF), jnp.bfloat16),
                pltpu.VMEM((ROWS, FF), jnp.bfloat16),
                pltpu.VMEM((ROWS, FF), jnp.bfloat16),
                pltpu.VMEM((ROWS, D), jnp.bfloat16),
            ],
        ),
        out_shape=[
            jax.ShapeDtypeStruct((seqs, per_group, CAP, D), jnp.bfloat16),
            jax.ShapeDtypeStruct((seqs, per_group, CAP, D + WIDE), jnp.bfloat16),
            jax.ShapeDtypeStruct((4, per_group, D, FF), jnp.bfloat16),
        ],
        compiler_params=pltpu.CompilerParams(vmem_limit_bytes=56 * 2**20),
        cost_estimate=pl.CostEstimate(
            flops=18 * ROWS * per_group * D * FF,
            bytes_accessed=30 * 2**20,
            transcendentals=ROWS * per_group * FF,
        ),
        name="experts",
    )(own, arrived, all_grads, *weights, *momenta)


def split_two(value):
    high = value.astype(jnp.bfloat16)
    return high, (value - high.astype(jnp.float32)).astype(jnp.bfloat16)


def mat_three(left, right):
    return mat(left[0], right[0]) + (mat(left[0], right[1]) + mat(left[1], right[0]))


def owner_kernel(place_ref, matrix_ref, keep_ref, cross_ref, gram_ref, total_ref, ortho_ref):
    gram = contract_rows(matrix_ref[...], matrix_ref[...])
    width = gram_ref.shape[0]
    row = lax.broadcasted_iota(jnp.int32, (width, width), 0)
    column = lax.broadcasted_iota(jnp.int32, (width, width), 1)
    eye = (row == column).astype(jnp.float32)
    square = jnp.sum(jnp.sum(eye * gram, axis=1, keepdims=True), axis=0, keepdims=True)
    scale = 1.0 / (jnp.sqrt(square) + 1e-07)
    gram_ref[...] = gram * scale * scale
    total_ref[...] = eye

    def step(index, carry):
        gram = gram_ref[...]
        gram_two = split_two(gram)
        factor = coef_one * eye + coef_two * gram + coef_three * mat_three(gram_two, gram_two)
        factor_two = split_two(factor)
        total_ref[...] = mat_three(factor_two, split_two(total_ref[...]))
        gram_ref[...] = mat_three(split_two(mat_three(factor_two, gram_two)), factor_two)
        return carry

    lax.fori_loop(0, 5, step, 0)
    high, low = split_two(total_ref[...])
    matrix = matrix_ref[...]
    ortho_ref[...] = ((mat(matrix, high) + mat(matrix, low)) * scale).astype(ortho_ref.dtype)
    level, side = place_ref[0], place_ref[1]
    rows = keep_ref.shape[2]
    for up in range(4):
        for ref, column in ((keep_ref, side), (cross_ref, 1 - side)):
            index = 2 * lax.rem(level + up, 4) + column
            where = pl.ds(pl.multiple_of(index * rows, rows), rows)
            ref[up, 0] = matrix_ref[where]
            ref[up, 1] = ortho_ref[where]


def owner_orthogonal(matrix, place):
    rows, width = matrix.shape
    whole = pl.BlockSpec(memory_space=pltpu.VMEM)
    sent = jax.ShapeDtypeStruct((4, 2, rows // 8, width), jnp.bfloat16)
    return pl.pallas_call(
        owner_kernel,
        out_shape=[sent, sent],
        in_specs=[pl.BlockSpec(memory_space=pltpu.SMEM), whole],
        out_specs=[whole, whole],
        scratch_shapes=[
            pltpu.VMEM((width, width), jnp.float32),
            pltpu.VMEM((width, width), jnp.float32),
            pltpu.VMEM((rows, width), jnp.bfloat16),
        ],
        compiler_params=pltpu.CompilerParams(vmem_limit_bytes=48 * 2**20),
        cost_estimate=pl.CostEstimate(
            flops=6 * (22 * width**3 + 2 * rows * width**2),
            bytes_accessed=6 * rows * width,
            transcendentals=0,
        ),
        name="owner",
    )(place, matrix)


def probabilities(queries, keys, first):
    scores = contract_cols(queries, keys) * HD ** (-0.5)
    token = lax.broadcasted_iota(jnp.int32, scores.shape, 0) % (scores.shape[0] // 2)
    key = lax.broadcasted_iota(jnp.int32, scores.shape, 1)
    scores = jnp.where(key <= first + token, scores, -1e30)
    running_max = jnp.max(scores, axis=1, keepdims=True)
    raised = jnp.exp(scores - running_max)
    return raised * (1.0 / jnp.sum(raised, axis=1, keepdims=True))


def two_heads(block, group):
    left = block[:, 2 * group * HD : (2 * group + 1) * HD]
    right = block[:, (2 * group + 1) * HD : (2 * group + 2) * HD]
    return jnp.concatenate([left, right], axis=0)


def side_by_side(stacked):
    half = stacked.shape[0] // 2
    return jnp.concatenate([stacked[:half], stacked[half:]], axis=1)


def attend_kernel(first_ref, query_ref, key_ref, value_ref, mixed_ref):
    queries, keys, values = query_ref[...], key_ref[...], value_ref[...]
    mixed = []
    for group in range(2):
        columns = slice(group * HD, (group + 1) * HD)
        weights = probabilities(two_heads(queries, group), keys[:, columns], first_ref[0])
        mixed.append(side_by_side(mat(weights.astype(jnp.bfloat16), values[:, columns])))
    mixed_ref[...] = jnp.concatenate(mixed, axis=1).astype(mixed_ref.dtype)


def attend_back_kernel(
    first_ref, query_ref, key_ref, value_ref, grad_ref, dquery_ref, dkey_ref, dvalue_ref
):
    queries, keys, values, grads = query_ref[...], key_ref[...], value_ref[...], grad_ref[...]
    dquery, dkey, dvalue = [], [], []
    for group in range(2):
        columns = slice(group * HD, (group + 1) * HD)
        query, grad = two_heads(queries, group), two_heads(grads, group)
        weights = probabilities(query, keys[:, columns], first_ref[0])
        grad_weights = contract_cols(grad, values[:, columns])
        inner = jnp.sum(weights * grad_weights, axis=1, keepdims=True)
        grad_scores = (weights * (grad_weights - inner)).astype(jnp.bfloat16)
        dquery.append(side_by_side(mat(grad_scores, keys[:, columns]) * HD ** (-0.5)))
        dkey.append(contract_rows(grad_scores, query) * HD ** (-0.5))
        dvalue.append(contract_rows(weights.astype(jnp.bfloat16), grad))
    dquery_ref[...] = jnp.concatenate(dquery, axis=1)
    dkey_ref[...] = jnp.concatenate(dkey, axis=1).astype(dkey_ref.dtype)
    dvalue_ref[...] = jnp.concatenate(dvalue, axis=1).astype(dvalue_ref.dtype)


def attention_call(kernel, operands, grads, first, name):
    queries, all_kv = operands
    rows, keys = queries.shape[0], all_kv.shape[0]
    steps = KV // 2
    wide = pl.BlockSpec((rows, 4 * HD), lambda g, first: (0, g))
    key_spec = pl.BlockSpec((keys, 2 * HD), lambda g, first: (0, g))
    value_spec = pl.BlockSpec((keys, 2 * HD), lambda g, first: (0, g + steps))
    if grads is None:
        arrays, specs = (queries, all_kv, all_kv), [wide, key_spec, value_spec]
        out_shape = jax.ShapeDtypeStruct(queries.shape, jnp.bfloat16)
        out_specs = wide
    else:
        arrays, specs = (queries, all_kv, all_kv, grads), [wide, key_spec, value_spec, wide]
        out_shape = [
            jax.ShapeDtypeStruct(queries.shape, jnp.float32),
            jax.ShapeDtypeStruct((keys, KV * HD), jnp.bfloat16),
            jax.ShapeDtypeStruct((keys, KV * HD), jnp.bfloat16),
        ]
        out_specs = [wide, key_spec, key_spec]
    factor = 4 if grads is None else 10
    return pl.pallas_call(
        kernel,
        grid_spec=pltpu.PrefetchScalarGridSpec(
            num_scalar_prefetch=1, grid=(steps,), in_specs=specs, out_specs=out_specs
        ),
        out_shape=out_shape,
        compiler_params=pltpu.CompilerParams(vmem_limit_bytes=48 * 2**20),
        cost_estimate=pl.CostEstimate(
            flops=factor * rows * keys * HEADS * HD,
            bytes_accessed=4 * 2**20,
            transcendentals=rows * keys * HEADS,
        ),
        name=name,
    )(first.astype(jnp.int32).reshape(1), *arrays)


def body(
    tokens,
    cotangent,
    routes,
    query_weight,
    kv_weight,
    output_weight,
    router,
    gains,
    gate_weight,
    up_weight,
    down_weight,
    query_momentum,
    kv_momentum,
    output_momentum,
    gate_momentum,
    up_momentum,
    down_momentum,
    router_first,
    router_second,
    gains_first,
    gains_second,
):
    bf16 = jnp.bfloat16
    ctx_count = lax.axis_size("ctx")
    exp_count = lax.axis_size("exp")
    exp_index = lax.axis_index("exp")
    row_count = tokens.shape[1]
    per_group = EXPERTS // exp_count
    inputs = tokens[0].astype(jnp.float32)
    grad_out = cotangent[0].astype(jnp.float32)
    route_ids = routes[0]

    packed = jnp.concatenate(
        [
            jnp.concatenate([query_weight, kv_weight], axis=1).T,
            router.astype(bf16).T,
            jnp.pad(gains.astype(bf16).reshape(1, -1), ((0, 0), (0, D - 2 * HD))),
            jnp.zeros((5, D), bf16),
        ],
        axis=0,
    )
    own_experts = jnp.stack([gate_weight, up_weight, down_weight])
    row_y, far_x, core = exp_index // 4, (exp_index // 2) % 2, exp_index % 2
    packed_far = exp_move(packed, 0, 1, 0)
    other_experts = ctx_move(own_experts, 0, 1)
    below, above = ctx_move(own_experts, 1, 0), ctx_move(own_experts, 3, 0)
    pair = jnp.stack(
        [
            jnp.where(far_x == 0, packed, packed_far),
            jnp.where(far_x == 0, packed_far, packed),
        ]
    )
    from_below, from_above = exp_move(pair, 1, 0, 0), exp_move(pair, 3, 0, 0)
    from_below, from_above, other_experts, below, above = lax.optimization_barrier(
        (from_below, from_above, other_experts, below, above)
    )
    below_other, above_other = ctx_move(other_experts, 1, 0), ctx_move(other_experts, 3, 0)
    far = ctx_move(below, 1, 0)
    from_two = jnp.stack([exp_move(from_below[0], 1, 0, 0), exp_move(from_above[1], 3, 0, 0)])
    mine = jnp.stack([pair, from_above, from_two, from_below])
    other = exp_move(mine, 0, 0, 1)

    def ordered(left, right, axis):
        both = jnp.stack(
            [jnp.where(core == 0, left, right), jnp.where(core == 0, right, left)], axis=axis + 2
        )
        return ring_order(both, row_y, axis)

    packed_rows = packed.shape[0]
    mine_flat = mine.reshape(8 * packed_rows, D)
    other_flat = other.reshape(8 * packed_rows, D)
    full_router = ordered(
        mine[:, :, 2 * HD : 2 * HD + per_group], other[:, :, 2 * HD : 2 * HD + per_group], 0
    ).reshape(EXPERTS, D)
    gains_row = 2 * HD + per_group
    full_gains = ordered(mine[:, :, gains_row, : 2 * HD], other[:, :, gains_row, : 2 * HD], 0)
    full_gains = full_gains.reshape(exp_count, 2, HD).transpose(1, 0, 2).reshape(2, D)
    gain_one = full_gains[0].astype(jnp.float32)
    gain_two = full_gains[1].astype(jnp.float32)

    full_output = lax.all_gather(output_weight.T, "exp", axis=0, tiled=True)

    expert_ids = jnp.arange(EXPERTS, dtype=jnp.int32)
    named = jnp.any(route_ids[:, :, None] == expert_ids[None, None, :], axis=1)
    named_low = named.astype(bf16)
    token_ids = jnp.arange(row_count)
    earlier = (token_ids[None, :] < token_ids[:, None]).astype(bf16)
    rank = mat(earlier, named_low)
    place = jnp.where(named, rank + 1.0, 0.0).astype(bf16)
    slot_ids = jnp.arange(EXPERTS * CAP, dtype=jnp.int32)
    widen = (slot_ids[None, :] // CAP == expert_ids[:, None]).astype(bf16)
    chosen_slot = mat(place, widen) == (slot_ids % CAP + 1).astype(jnp.float32)[None, :]
    select = chosen_slot.astype(bf16)

    sent_grads = jnp.concatenate(
        [cotangent[0], place, jnp.zeros((row_count, WIDE - EXPERTS), bf16)], axis=1
    )
    all_grads = lax.all_gather(sent_grads, "exp", axis=0, tiled=False)

    inv_one = lax.rsqrt(jnp.mean(inputs * inputs, axis=-1, keepdims=True) + eps_norm)
    normed_one = (inputs * inv_one * gain_one).astype(bf16)
    halves = [
        contract_cols(normed_one, flat).reshape(row_count, 4, 2, packed_rows)[..., : 2 * HD]
        for flat in (mine_flat, other_flat)
    ]
    projected = ordered(*halves, 1).reshape(row_count, exp_count, 2 * HD)
    query_raw = projected[:, :, :HD]
    kv_raw = projected[:, :, HD:]
    first_row = lax.axis_index("ctx") * row_count
    cosine, sine = rope_tables(first_row, row_count)
    queries = rotate(query_raw, cosine, sine).astype(bf16)
    keys = rotate(kv_raw[:, :KV], cosine, sine).astype(bf16)
    values = kv_raw[:, KV:].astype(bf16)
    sent_kv = jnp.concatenate([keys, values], axis=1).reshape(row_count, 2 * KV * HD)
    sent_kv = after(sent_kv, far)
    all_kv = spread(sent_kv, "ctx", None, ctx_count).reshape(ctx_count * row_count, 2 * KV * HD)
    flat_queries = queries.reshape(row_count, HEADS * HD)
    mixed_low = attention_call(attend_kernel, (flat_queries, all_kv), None, first_row, "attend")
    sent_mixed = mixed_low.reshape(row_count, exp_count, HD).transpose(1, 0, 2)
    sent_mixed = sent_mixed.reshape(exp_count, row_count // 2, 2 * HD)
    attended = mat(mixed_low, full_output)
    residual = inputs + attended
    inv_two = lax.rsqrt(jnp.mean(residual * residual, axis=-1, keepdims=True) + eps_norm)
    normed_two = (residual * inv_two * gain_two).astype(bf16)
    logits = contract_cols(normed_two, full_router)
    gates = jax.nn.softmax(jnp.where(named, logits, -1e30), axis=-1)
    gates = jnp.where(named, gates, 0.0)
    gate_parts = three_parts(gates)
    extended = jnp.concatenate(
        [normed_two, *gate_parts, jnp.zeros((row_count, WIDE - 3 * EXPERTS), bf16)], axis=1
    )
    sent_rows = contract_rows(select, extended).astype(bf16)
    sent_rows, below_other, above_other = lax.optimization_barrier(
        (sent_rows, below_other, above_other)
    )
    far_other = ctx_move(above_other, 3, 0)
    arrived = exchange(sent_rows.reshape(exp_count, per_group * CAP, D + WIDE), "exp")
    later_normed, arrived, far_other = lax.optimization_barrier((normed_one, arrived, far_other))
    full_experts = (
        own_experts, other_experts, below, below_other, above, above_other, far, far_other
    )
    all_normed = lax.all_gather(later_normed, "exp", axis=0, tiled=True)
    produced, back, expert_grads = expert_math(
        arrived.reshape(exp_count, per_group, CAP, D + WIDE),
        all_grads,
        full_experts,
        (gate_momentum, up_momentum, down_momentum),
    )
    head_mixed = exchange(after(sent_mixed, arrived), "exp")
    back, head_mixed = lax.optimization_barrier((back, head_mixed))
    head_mixed = head_mixed.reshape(exp_count * row_count, HD)
    returned = exchange(back.reshape(exp_count, per_group * CAP, D + WIDE), "exp")
    returned = returned.reshape(EXPERTS * CAP, D + WIDE)
    far_up, far_down = ctx_move(expert_grads[2, 0], 1, 0), ctx_move(expert_grads[2, 1], 3, 0)
    sum_up = jnp.stack([plus(expert_grads[1, 0], far_up), expert_grads[1, 1]])
    sum_down = jnp.stack([expert_grads[3, 0], plus(expert_grads[3, 1], far_down)])
    returned = after(returned, sum_up, sum_down)
    sum_up, sum_down = owner_move(sum_up, 1), owner_move(sum_down, 3)
    produced = after(produced, returned)
    route_values = exchange(produced.reshape(exp_count, per_group * CAP, D), "exp")
    summed_back = mat(select, returned)
    tail = summed_back[:, D:]
    grad_gates = (
        tail[:, :EXPERTS] + tail[:, EXPERTS : 2 * EXPERTS] + tail[:, 2 * EXPERTS : 3 * EXPERTS]
    )
    grad_logits = (
        gates * (grad_gates - jnp.sum(gates * grad_gates, axis=-1, keepdims=True))
    ).astype(bf16)
    grad_normed_two = summed_back[:, :D] + mat(grad_logits, full_router)
    scaled_two = grad_normed_two * gain_two
    grad_gain_two = jnp.sum(grad_normed_two * residual * inv_two, axis=0)
    grad_residual = (
        grad_out
        + inv_two * scaled_two
        - residual * inv_two**3 * jnp.mean(scaled_two * residual, axis=-1, keepdims=True)
    )
    grad_attended = grad_residual.astype(bf16)
    all_attended = lax.all_gather(grad_attended, "exp", axis=0, tiled=True)
    grad_mixed = contract_cols(grad_attended, full_output).astype(bf16)
    grad_queries, key_terms, value_terms = attention_call(
        attend_back_kernel, (flat_queries, all_kv), grad_mixed, first_row, "attend_back"
    )
    kv_terms = jnp.concatenate([key_terms, value_terms], axis=1)
    kv_terms, route_values, sum_up, sum_down = lax.optimization_barrier(
        (kv_terms, route_values, sum_up, sum_down)
    )
    both_sums = (
        expert_grads[0].astype(jnp.float32)
        + sum_up.astype(jnp.float32)
        + sum_down.astype(jnp.float32)
    )
    other_sums = ctx_move(both_sums[1].astype(bf16), 0, 1)
    kv_terms = exchange(kv_terms.reshape(ctx_count, row_count, 2 * KV * HD), "ctx")
    grad_query_raw = rotate(
        grad_queries.reshape(row_count, HEADS, HD), cosine, -sine
    ).astype(bf16)
    kv_sums = jnp.sum(kv_terms.astype(jnp.float32), axis=0).reshape(row_count, 2 * KV, HD)
    grad_key_raw = rotate(kv_sums[:, :KV], cosine, -sine).astype(bf16)
    grad_kv_raw = jnp.concatenate([grad_key_raw, kv_sums[:, KV:].astype(bf16)], axis=1)
    grad_projected = jnp.concatenate([grad_query_raw, grad_kv_raw], axis=2)
    by_core = ring_order(grad_projected.reshape(row_count, 4, 2, 2, 2 * HD), -row_y, 1)
    by_core = jnp.pad(by_core, ((0, 0),) * 4 + ((0, packed_rows - 2 * HD),))
    first_core, second_core = by_core[:, :, :, 0], by_core[:, :, :, 1]
    grad_normed_one = mat(
        jnp.where(core == 0, first_core, second_core).reshape(row_count, -1), mine_flat
    ) + mat(jnp.where(core == 0, second_core, first_core).reshape(row_count, -1), other_flat)
    scaled_one = grad_normed_one * gain_one
    grad_gain_one = jnp.sum(grad_normed_one * inputs * inv_one, axis=0)
    input_grad = (
        grad_residual
        + inv_one * scaled_one
        - inputs * inv_one**3 * jnp.mean(scaled_one * inputs, axis=-1, keepdims=True)
    )

    small_rows = (per_group * D + 2 * HD) // (2 * HD)
    small = jnp.concatenate(
        [
            contract_rows(grad_logits, normed_two).reshape(exp_count, -1, 2 * HD),
            jnp.stack([grad_gain_one, grad_gain_two])
            .reshape(2, exp_count, HD)
            .transpose(1, 0, 2)
            .reshape(exp_count, 1, 2 * HD),
            jnp.zeros((exp_count, 7, 2 * HD), jnp.float32),
        ],
        axis=1,
    ).astype(bf16)
    route_values = route_values.reshape(EXPERTS * CAP, D)
    head_send = jnp.concatenate([jnp.transpose(grad_projected, (1, 0, 2)), small], axis=1)
    level, side = lax.axis_index("ctx") // 2, lax.axis_index("ctx") % 2
    owned = (both_sums[0] + other_sums.astype(jnp.float32)).astype(bf16)
    head_send, owned = lax.optimization_barrier((head_send, owned))
    head_grads = exchange(head_send, "exp")
    keep, cross = owner_orthogonal(owned, jnp.stack([level, side]).astype(jnp.int32))
    head_grads = after(head_grads, keep, cross)
    crossed = ctx_move(cross, 0, 1)
    small = jnp.sum(head_grads[:, row_count : row_count + small_rows].astype(jnp.float32), axis=0)
    head_grads = head_grads[:, :row_count].reshape(exp_count * row_count, 2 * HD)

    part = jnp.concatenate(
        [
            mat(lax.optimization_barrier(head_grads.T), all_normed),
            mat(lax.optimization_barrier(head_mixed.T), all_attended),
        ],
        axis=0,
    )
    width = D // ctx_count
    part = jnp.concatenate(
        [
            jnp.transpose(part.astype(bf16).reshape(3 * HD, ctx_count, width), (1, 0, 2)),
            jnp.broadcast_to(
                jnp.pad(small.astype(bf16), ((0, 7), (0, 0)))[None], (ctx_count, 24, width)
            ),
        ],
        axis=1,
    )
    part, crossed = lax.optimization_barrier((exchange(part, "ctx"), crossed))
    returned_rows = [
        ctx_move(jnp.stack([keep[up], crossed[up]]), up, 0) if up else jnp.stack([keep[0], crossed[0]])
        for up in range(4)
    ]
    part = jnp.sum(part.astype(jnp.float32), axis=0)
    sums = spread(part[: 3 * HD].astype(bf16), "ctx", None, ctx_count)
    sums = jnp.transpose(sums, (0, 2, 1)).reshape(D, 3 * HD).astype(jnp.float32)
    small = part[3 * HD : 3 * HD + small_rows]
    sum_router = small[:-1].reshape(per_group, D).T
    sum_gains = small[-1].reshape(2, HD)
    router_one, router_two, router_new = adam_update(
        router, router_first, router_second, sum_router, router_rate, decay_rate
    )
    gains_one, gains_two, gains_new = adam_update(
        gains, gains_first, gains_second, sum_gains, gain_rate, 0.0
    )

    head_fresh, head_new = head_blocks(
        sums,
        jnp.concatenate([query_momentum, kv_momentum, output_momentum], axis=1),
        jnp.concatenate([query_weight, kv_weight, output_weight], axis=1),
    )

    returned_rows = jnp.stack(returned_rows).reshape(8, 2, D // ctx_count, -1)
    fresh, ortho = [], []
    for kind in range(3):
        picked = [
            lax.dynamic_index_in_dim(
                returned_rows,
                2 * ((level + 4 - kind) % 4) + (expert + side) % 2,
                0,
                keepdims=False,
            ).astype(jnp.float32)
            for expert in range(per_group)
        ]
        fresh.append(jnp.stack([rows[0] for rows in picked]))
        ortho.append(jnp.stack([rows[1] for rows in picked]))
    new = [
        step_weight(weight, factor)
        for weight, factor in zip((gate_weight, up_weight, down_weight), ortho)
    ]

    gates_wide = [mat(part, widen) for part in gate_parts]
    block_value = residual
    for wide in gates_wide:
        weighted = jnp.where(chosen_slot, wide, 0.0).astype(bf16)
        block_value = block_value + mat(weighted, route_values)
    return (
        block_value.astype(bf16)[None],
        input_grad[None],
        head_fresh[:, :HD],
        head_new[:, :HD],
        head_fresh[:, HD : 2 * HD],
        head_new[:, HD : 2 * HD],
        head_fresh[:, 2 * HD :],
        head_new[:, 2 * HD :],
        fresh[0],
        new[0],
        fresh[1],
        new[1],
        fresh[2],
        new[2],
        router_one,
        router_two,
        router_new,
        gains_one,
        gains_two,
        gains_new,
    )


def solution(mesh):
    return jax.shard_map(
        body,
        mesh=mesh,
        in_specs=(
            P("exp", "ctx", None),
            P("exp", "ctx", None),
            P("exp", "ctx", None),
            P(None, "exp"),
            P(None, "exp"),
            P(None, "exp"),
            P(None, "exp"),
            P(None, "exp"),
            P("exp", "ctx", None),
            P("exp", "ctx", None),
            P("exp", "ctx", None),
            P(None, "exp"),
            P(None, "exp"),
            P(None, "exp"),
            P("exp", "ctx", None),
            P("exp", "ctx", None),
            P("exp", "ctx", None),
            P(None, "exp"),
            P(None, "exp"),
            P(None, "exp"),
            P(None, "exp"),
        ),
        out_specs=(
            P("exp", "ctx", None),
            P("exp", "ctx", None),
            P(None, "exp"),
            P(None, "exp"),
            P(None, "exp"),
            P(None, "exp"),
            P(None, "exp"),
            P(None, "exp"),
            P("exp", "ctx", None),
            P("exp", "ctx", None),
            P("exp", "ctx", None),
            P("exp", "ctx", None),
            P("exp", "ctx", None),
            P("exp", "ctx", None),
            P(None, "exp"),
            P(None, "exp"),
            P(None, "exp"),
            P(None, "exp"),
            P(None, "exp"),
            P(None, "exp"),
        ),
        check_vma=False,
    )
```

```python
import math

import jax
import jax.numpy as jnp
from jax import lax
from jax.experimental import pallas as pl
from jax.experimental.pallas import tpu as pltpu
from jax.sharding import PartitionSpec as P

D = 1024
HEADS = 16
KV = 8
HD = 64
TOP = 8
STEP = 10


eps_norm = 1e-05
rope_base = 10000.0
mom_rate = 0.95
muon_rate = 0.15
decay_rate = 0.1
adam_one = 0.9
adam_two = 0.95
adam_eps = 1e-08
router_rate = 0.015
gain_rate = 0.2
coef_one = 3.4445
coef_two = -4.775
coef_three = 2.0315
highest = lax.Precision.HIGHEST


def rope_tables(first_row, token_count):
    half_width = HD // 2
    frequency = rope_base ** (-jnp.arange(half_width, dtype=jnp.float32) * 2.0 / HD)
    position = (first_row + jnp.arange(token_count, dtype=jnp.int32)).astype(jnp.float32)
    angle_grid = position[:, None] * frequency[None, :]
    return (jnp.cos(angle_grid), jnp.sin(angle_grid))


def rotate(vector, cosine, sine):
    half_width = vector.shape[-1] // 2
    front_half = vector[..., :half_width]
    back_half = vector[..., half_width:]
    cos_rows = cosine[:, None, :]
    sin_rows = sine[:, None, :]
    return jnp.concatenate(
        [
            front_half * cos_rows - back_half * sin_rows,
            back_half * cos_rows + front_half * sin_rows,
        ],
        axis=-1,
    )


EXPERTS = 32
CAP = 48
WIDE = 128
FF = 512
ROWS = 16 * CAP
CHUNKS = 2
LOCAL = 128


def exchange(blocks, axis, groups=None):
    return lax.all_to_all(
        blocks, axis, split_axis=0, concat_axis=0, tiled=True, axis_index_groups=groups
    )


def spread(block, axis, groups=None, count=8):
    return exchange(jnp.broadcast_to(block[None], (count,) + block.shape), axis, groups)


def parity_groups(count):
    return [list(range(core, count, 2)) for core in range(2)]


def core_swap(block, count):
    return lax.ppermute(block, "exp", [(i, i ^ 1) for i in range(count)])


def ctx_move(block, up, other):
    pairs = [
        (2 * z + x, 2 * ((z + up) % 4) + (x ^ other)) for z in range(4) for x in range(2)
    ]
    return lax.ppermute(block, "ctx", pairs)


def plus(left, right):
    return (left.astype(jnp.float32) + right.astype(jnp.float32)).astype(jnp.bfloat16)


def owner_move(block, up):
    pairs = [
        (2 * z + x, 2 * ((z + up) % 4) + x) for z in range(4) for x in range(2) if (z + up) % 4 < 3
    ]
    return lax.ppermute(block, "ctx", pairs)


def exp_move(block, up, far, core):
    pairs = [
        (4 * y + 2 * h + c, 4 * ((y + up) % 4) + 2 * (h ^ far) + (c ^ core))
        for y in range(4)
        for h in range(2)
        for c in range(2)
    ]
    return lax.ppermute(block, "exp", pairs)


def ring_order(blocks, shift, axis):
    double = jnp.concatenate([blocks, blocks], axis=axis)
    return lax.dynamic_slice_in_dim(double, (4 - shift) % 4, 4, axis)


def after(value, *others):
    return lax.optimization_barrier((value,) + others)[0]


def three_parts(value):
    high = value.astype(jnp.bfloat16)
    rest = value - high.astype(jnp.float32)
    middle = rest.astype(jnp.bfloat16)
    low = (rest - middle.astype(jnp.float32)).astype(jnp.bfloat16)
    return high, middle, low


def polynomial(gram, steps, precision):
    total = None
    for step in range(steps):
        square = jnp.matmul(gram, gram, precision=precision)
        eye = jnp.eye(gram.shape[-1], dtype=jnp.float32)
        factor = coef_one * eye + coef_two * gram + coef_three * square
        total = factor if total is None else jnp.matmul(factor, total, precision=precision)
        if step < steps - 1:
            gram = jnp.matmul(
                jnp.matmul(factor, gram, precision=precision), factor, precision=precision
            )
    return total


def step_weight(weight, ortho):
    return (
        weight.astype(jnp.float32) * (1.0 - muon_rate * decay_rate)
        - muon_rate * 0.2 * math.sqrt(D) * ortho
    )


def adam_update(param, first, second, grad, rate, decay):
    first = adam_one * first + (1.0 - adam_one) * grad
    second = adam_two * second + (1.0 - adam_two) * grad * grad
    fixed_one = first / (1.0 - adam_one**STEP)
    fixed_two = second / (1.0 - adam_two**STEP)
    return (
        first,
        second,
        param * (1.0 - rate * decay) - rate * fixed_one / (jnp.sqrt(fixed_two) + adam_eps),
    )


def contract_rows(left, right, precision=None):
    return lax.dot_general(
        left,
        right,
        (((0,), (0,)), ((), ())),
        preferred_element_type=jnp.float32,
        precision=precision,
    )


def contract_cols(left, right):
    return lax.dot_general(
        left, right, (((1,), (1,)), ((), ())), preferred_element_type=jnp.float32
    )


def mat(left, right):
    return jnp.dot(left, right, preferred_element_type=jnp.float32)


def head_blocks(sums, momenta, weights):
    fresh = mom_rate * momenta + sums
    width = fresh.shape[1]
    block = jnp.arange(width) // HD
    same = block[:, None] == block[None, :]
    gram = jnp.where(same, contract_rows(fresh, fresh, highest), 0.0)
    square = jnp.sum(jnp.where(jnp.eye(width, dtype=bool), gram, 0.0), axis=0, keepdims=True)
    total = jnp.sum(jnp.where(same, square.T, 0.0), axis=0, keepdims=True)
    scale = 1.0 / (jnp.sqrt(total) + 1e-07)
    poly = polynomial(gram * scale * scale.T, 5, highest)
    ortho = jnp.dot(fresh * scale, poly, precision=highest)
    return fresh, step_weight(weights, ortho)


def expert_kernel(own_ref, arrived_ref, grads_ref, *refs_in_order):
    blocks, momenta, refs = refs_in_order[:8], refs_in_order[8:11], refs_in_order[11:]
    expert_steps(own_ref, arrived_ref, grads_ref, blocks, momenta, *refs)


def expert_steps(own_ref, arrived_ref, grads_ref, blocks, momenta, made_ref, back_ref, sums_ref,
                  weight_ref, rows_ref, hidden_ref, dgate_ref, dup_ref, dy_ref):
    expert = own_ref[0] + pl.program_id(0)
    level, side = own_ref[1], own_ref[2]
    width = D // 8

    def part(up, other):
        index = 2 * lax.rem(level + up, 4) + (1 - side if other else side)
        return pl.ds(pl.multiple_of(index * width, width), width)

    for index, up in enumerate((0, 3, 1, 2)):
        for other in range(2):
            for kind in range(3):
                weight_ref[kind, part(up, other)] = blocks[2 * index + other][kind, 0]
    full_gate, full_up, full_down = weight_ref[0], weight_ref[1], weight_ref[2]
    chunk = ROWS // CHUNKS
    seqs = chunk // CAP

    def forward(step, carry):
        first = pl.multiple_of(step * seqs, seqs)
        where = pl.ds(pl.multiple_of(step * chunk, chunk), chunk)
        both = arrived_ref[pl.ds(first, seqs), 0].reshape(chunk, D + WIDE)
        rows = both[:, :D]
        lane = lax.broadcasted_iota(jnp.int32, (chunk, WIDE), 1)
        pick = (lane % EXPERTS == expert) & (lane < 3 * EXPERTS)
        gate = jnp.sum(
            jnp.where(pick, both[:, D:].astype(jnp.float32), 0.0), axis=1, keepdims=True
        )
        gate_pre = mat(rows, full_gate)
        up_pre = mat(rows, full_up)
        sigma = jax.nn.sigmoid(gate_pre)
        activated = gate_pre * sigma
        hidden = (activated * up_pre).astype(jnp.bfloat16)
        made = contract_cols(hidden, full_down).astype(jnp.bfloat16)
        made_ref[pl.ds(first, seqs), 0] = made.reshape(seqs, CAP, D)
        slot_ids = lax.broadcasted_iota(jnp.int32, (LOCAL, CAP), 1).astype(jnp.float32) + 1.0
        token_lane = lax.broadcasted_iota(jnp.int32, (LOCAL, WIDE), 1)
        taken = []
        for seq in range(seqs):
            source = grads_ref[first + seq]
            places = jnp.where(token_lane == expert, source[:, D:].astype(jnp.float32), 0.0)
            chosen = jnp.sum(places, axis=1, keepdims=True) == slot_ids
            taken.append(contract_rows(chosen.astype(jnp.bfloat16), source[:, :D]))
        grad_f32 = jnp.concatenate(taken, axis=0)
        grad_made = (gate * grad_f32).astype(jnp.bfloat16)
        grad_gate_value = jnp.sum(made.astype(jnp.float32) * grad_f32, axis=1, keepdims=True)
        grad_hidden = mat(grad_made, full_down)
        grad_gate_pre = (
            grad_hidden * up_pre * sigma * (1.0 + gate_pre * (1.0 - sigma))
        ).astype(jnp.bfloat16)
        grad_up_pre = (grad_hidden * activated).astype(jnp.bfloat16)
        back = contract_cols(grad_gate_pre, full_gate) + contract_cols(grad_up_pre, full_up)
        back_ref[pl.ds(first, seqs), 0, :, :D] = back.astype(jnp.bfloat16).reshape(seqs, CAP, D)
        high, middle, low = [
            part.astype(jnp.float32) for part in three_parts(grad_gate_value)
        ]
        slot = jnp.where(
            lane < EXPERTS, high, jnp.where(lane < 2 * EXPERTS, middle, low)
        )
        back_ref[pl.ds(first, seqs), 0, :, D:] = (
            jnp.where(pick, slot, 0.0).astype(jnp.bfloat16).reshape(seqs, CAP, WIDE)
        )
        rows_ref[where] = rows
        hidden_ref[where] = hidden
        dgate_ref[where] = grad_gate_pre
        dup_ref[where] = grad_up_pre
        dy_ref[where] = grad_made
        return carry

    lax.fori_loop(0, CHUNKS, forward, 0)
    own_part = 2 * level + side
    pairs = ((rows_ref, dgate_ref), (rows_ref, dup_ref), (dy_ref, hidden_ref))
    for kind in range(3):
        slot = lax.rem(kind - level + 4, 4)
        left, right = pairs[kind]
        for index in range(D // width):
            rows = slice(index * width, (index + 1) * width)
            added = jnp.where(index == own_part, mom_rate, 0.0) * momenta[kind][0]
            total = contract_rows(left[:, rows], right[...]) + added
            sums_ref[slot, 0, rows] = total.astype(jnp.bfloat16)
    sums_ref[lax.rem(7 - level, 4), 0] = jnp.zeros((D, FF), jnp.bfloat16)


def expert_math(arrived, all_grads, weights, momenta):
    seqs, per_group = arrived.shape[:2]
    place = lax.axis_index("ctx")
    own = jnp.stack([lax.axis_index("exp") * per_group, place // 2, place % 2]).astype(jnp.int32)
    rows_each = D // 8

    def rows_spec(width):
        return pl.BlockSpec((seqs, 1, CAP, width), lambda e, own: (0, e, 0, 0))

    summed = pl.BlockSpec(
        (4, 1, D, FF), lambda e, own: (0, e + own[2] - 2 * e * own[2], 0, 0)
    )
    momentum = pl.BlockSpec((1, rows_each, FF), lambda e, own: (e, 0, 0))
    one = pl.BlockSpec((3, 1, rows_each, FF), lambda e, own: (0, e, 0, 0))
    whole = pl.BlockSpec(all_grads.shape, lambda e, own: (0, 0, 0))
    return pl.pallas_call(
        expert_kernel,
        grid_spec=pltpu.PrefetchScalarGridSpec(
            num_scalar_prefetch=1,
            grid=(per_group,),
            in_specs=[rows_spec(D + WIDE), whole] + [one] * 8 + [momentum] * 3,
            out_specs=[rows_spec(D), rows_spec(D + WIDE), summed],
            scratch_shapes=[
                pltpu.VMEM((3, D, FF), jnp.bfloat16),
                pltpu.VMEM((ROWS, D), jnp.bfloat16),
                pltpu.VMEM((ROWS, FF), jnp.bfloat16),
                pltpu.VMEM((ROWS, FF), jnp.bfloat16),
                pltpu.VMEM((ROWS, FF), jnp.bfloat16),
                pltpu.VMEM((ROWS, D), jnp.bfloat16),
            ],
        ),
        out_shape=[
            jax.ShapeDtypeStruct((seqs, per_group, CAP, D), jnp.bfloat16),
            jax.ShapeDtypeStruct((seqs, per_group, CAP, D + WIDE), jnp.bfloat16),
            jax.ShapeDtypeStruct((4, per_group, D, FF), jnp.bfloat16),
        ],
        compiler_params=pltpu.CompilerParams(vmem_limit_bytes=56 * 2**20),
        cost_estimate=pl.CostEstimate(
            flops=18 * ROWS * per_group * D * FF,
            bytes_accessed=30 * 2**20,
            transcendentals=ROWS * per_group * FF,
        ),
        name="experts",
    )(own, arrived, all_grads, *weights, *momenta)


def split_two(value):
    high = value.astype(jnp.bfloat16)
    return high, (value - high.astype(jnp.float32)).astype(jnp.bfloat16)


def mat_three(left, right):
    return mat(left[0], right[0]) + (mat(left[0], right[1]) + mat(left[1], right[0]))


def owner_kernel(place_ref, matrix_ref, keep_ref, cross_ref, gram_ref, total_ref, ortho_ref):
    gram = contract_rows(matrix_ref[...], matrix_ref[...])
    width = gram_ref.shape[0]
    row = lax.broadcasted_iota(jnp.int32, (width, width), 0)
    column = lax.broadcasted_iota(jnp.int32, (width, width), 1)
    eye = (row == column).astype(jnp.float32)
    square = jnp.sum(jnp.sum(eye * gram, axis=1, keepdims=True), axis=0, keepdims=True)
    scale = 1.0 / (jnp.sqrt(square) + 1e-07)
    gram_ref[...] = gram * scale * scale
    total_ref[...] = eye

    def step(index, carry):
        gram = gram_ref[...]
        gram_two = split_two(gram)
        factor = coef_one * eye + coef_two * gram + coef_three * mat_three(gram_two, gram_two)
        factor_two = split_two(factor)
        total_ref[...] = mat_three(factor_two, split_two(total_ref[...]))
        gram_ref[...] = mat_three(split_two(mat_three(factor_two, gram_two)), factor_two)
        return carry

    lax.fori_loop(0, 5, step, 0)
    high, low = split_two(total_ref[...])
    matrix = matrix_ref[...]
    ortho_ref[...] = ((mat(matrix, high) + mat(matrix, low)) * scale).astype(ortho_ref.dtype)
    level, side = place_ref[0], place_ref[1]
    rows = keep_ref.shape[2]
    for up in range(4):
        for ref, column in ((keep_ref, side), (cross_ref, 1 - side)):
            index = 2 * lax.rem(level + up, 4) + column
            where = pl.ds(pl.multiple_of(index * rows, rows), rows)
            ref[up, 0] = matrix_ref[where]
            ref[up, 1] = ortho_ref[where]


def owner_orthogonal(matrix, place):
    rows, width = matrix.shape
    whole = pl.BlockSpec(memory_space=pltpu.VMEM)
    sent = jax.ShapeDtypeStruct((4, 2, rows // 8, width), jnp.bfloat16)
    return pl.pallas_call(
        owner_kernel,
        out_shape=[sent, sent],
        in_specs=[pl.BlockSpec(memory_space=pltpu.SMEM), whole],
        out_specs=[whole, whole],
        scratch_shapes=[
            pltpu.VMEM((width, width), jnp.float32),
            pltpu.VMEM((width, width), jnp.float32),
            pltpu.VMEM((rows, width), jnp.bfloat16),
        ],
        compiler_params=pltpu.CompilerParams(vmem_limit_bytes=48 * 2**20),
        cost_estimate=pl.CostEstimate(
            flops=6 * (22 * width**3 + 2 * rows * width**2),
            bytes_accessed=6 * rows * width,
            transcendentals=0,
        ),
        name="owner",
    )(place, matrix)


def probabilities(queries, keys, first):
    scores = contract_cols(queries, keys) * HD ** (-0.5)
    token = lax.broadcasted_iota(jnp.int32, scores.shape, 0) % (scores.shape[0] // 2)
    key = lax.broadcasted_iota(jnp.int32, scores.shape, 1)
    scores = jnp.where(key <= first + token, scores, -1e30)
    running_max = jnp.max(scores, axis=1, keepdims=True)
    raised = jnp.exp(scores - running_max)
    return raised * (1.0 / jnp.sum(raised, axis=1, keepdims=True))


def two_heads(block, group):
    left = block[:, 2 * group * HD : (2 * group + 1) * HD]
    right = block[:, (2 * group + 1) * HD : (2 * group + 2) * HD]
    return jnp.concatenate([left, right], axis=0)


def side_by_side(stacked):
    half = stacked.shape[0] // 2
    return jnp.concatenate([stacked[:half], stacked[half:]], axis=1)


def attend_kernel(first_ref, query_ref, key_ref, value_ref, mixed_ref):
    queries, keys, values = query_ref[...], key_ref[...], value_ref[...]
    mixed = []
    for group in range(2):
        columns = slice(group * HD, (group + 1) * HD)
        weights = probabilities(two_heads(queries, group), keys[:, columns], first_ref[0])
        mixed.append(side_by_side(mat(weights.astype(jnp.bfloat16), values[:, columns])))
    mixed_ref[...] = jnp.concatenate(mixed, axis=1).astype(mixed_ref.dtype)


def attend_back_kernel(
    first_ref, query_ref, key_ref, value_ref, grad_ref, dquery_ref, dkey_ref, dvalue_ref
):
    queries, keys, values, grads = query_ref[...], key_ref[...], value_ref[...], grad_ref[...]
    dquery, dkey, dvalue = [], [], []
    for group in range(2):
        columns = slice(group * HD, (group + 1) * HD)
        query, grad = two_heads(queries, group), two_heads(grads, group)
        weights = probabilities(query, keys[:, columns], first_ref[0])
        grad_weights = contract_cols(grad, values[:, columns])
        inner = jnp.sum(weights * grad_weights, axis=1, keepdims=True)
        grad_scores = (weights * (grad_weights - inner)).astype(jnp.bfloat16)
        dquery.append(side_by_side(mat(grad_scores, keys[:, columns]) * HD ** (-0.5)))
        dkey.append(contract_rows(grad_scores, query) * HD ** (-0.5))
        dvalue.append(contract_rows(weights.astype(jnp.bfloat16), grad))
    dquery_ref[...] = jnp.concatenate(dquery, axis=1)
    dkey_ref[...] = jnp.concatenate(dkey, axis=1).astype(dkey_ref.dtype)
    dvalue_ref[...] = jnp.concatenate(dvalue, axis=1).astype(dvalue_ref.dtype)


def attention_call(kernel, operands, grads, first, name):
    queries, all_kv = operands
    rows, keys = queries.shape[0], all_kv.shape[0]
    steps = KV // 2
    wide = pl.BlockSpec((rows, 4 * HD), lambda g, first: (0, g))
    key_spec = pl.BlockSpec((keys, 2 * HD), lambda g, first: (0, g))
    value_spec = pl.BlockSpec((keys, 2 * HD), lambda g, first: (0, g + steps))
    if grads is None:
        arrays, specs = (queries, all_kv, all_kv), [wide, key_spec, value_spec]
        out_shape = jax.ShapeDtypeStruct(queries.shape, jnp.bfloat16)
        out_specs = wide
    else:
        arrays, specs = (queries, all_kv, all_kv, grads), [wide, key_spec, value_spec, wide]
        out_shape = [
            jax.ShapeDtypeStruct(queries.shape, jnp.float32),
            jax.ShapeDtypeStruct((keys, KV * HD), jnp.bfloat16),
            jax.ShapeDtypeStruct((keys, KV * HD), jnp.bfloat16),
        ]
        out_specs = [wide, key_spec, key_spec]
    factor = 4 if grads is None else 10
    return pl.pallas_call(
        kernel,
        grid_spec=pltpu.PrefetchScalarGridSpec(
            num_scalar_prefetch=1, grid=(steps,), in_specs=specs, out_specs=out_specs
        ),
        out_shape=out_shape,
        compiler_params=pltpu.CompilerParams(vmem_limit_bytes=48 * 2**20),
        cost_estimate=pl.CostEstimate(
            flops=factor * rows * keys * HEADS * HD,
            bytes_accessed=4 * 2**20,
            transcendentals=rows * keys * HEADS,
        ),
        name=name,
    )(first.astype(jnp.int32).reshape(1), *arrays)


def body(
    tokens,
    cotangent,
    routes,
    query_weight,
    kv_weight,
    output_weight,
    router,
    gains,
    gate_weight,
    up_weight,
    down_weight,
    query_momentum,
    kv_momentum,
    output_momentum,
    gate_momentum,
    up_momentum,
    down_momentum,
    router_first,
    router_second,
    gains_first,
    gains_second,
):
    bf16 = jnp.bfloat16
    ctx_count = lax.axis_size("ctx")
    exp_count = lax.axis_size("exp")
    exp_index = lax.axis_index("exp")
    row_count = tokens.shape[1]
    per_group = EXPERTS // exp_count
    inputs = tokens[0].astype(jnp.float32)
    grad_out = cotangent[0].astype(jnp.float32)
    route_ids = routes[0]

    packed = jnp.concatenate(
        [
            jnp.concatenate([query_weight, kv_weight], axis=1).T,
            router.astype(bf16).T,
            jnp.pad(gains.astype(bf16).reshape(1, -1), ((0, 0), (0, D - 2 * HD))),
            jnp.zeros((5, D), bf16),
        ],
        axis=0,
    )
    own_experts = jnp.stack([gate_weight, up_weight, down_weight])
    row_y, far_x, core = exp_index // 4, (exp_index // 2) % 2, exp_index % 2
    packed_far = exp_move(packed, 0, 1, 0)
    other_experts = ctx_move(own_experts, 0, 1)
    below, above = ctx_move(own_experts, 1, 0), ctx_move(own_experts, 3, 0)
    pair = jnp.stack(
        [
            jnp.where(far_x == 0, packed, packed_far),
            jnp.where(far_x == 0, packed_far, packed),
        ]
    )
    from_below, from_above = exp_move(pair, 1, 0, 0), exp_move(pair, 3, 0, 0)
    from_below, from_above, other_experts, below, above = lax.optimization_barrier(
        (from_below, from_above, other_experts, below, above)
    )
    below_other, above_other = ctx_move(other_experts, 1, 0), ctx_move(other_experts, 3, 0)
    far = ctx_move(below, 1, 0)
    from_two = jnp.stack([exp_move(from_below[0], 1, 0, 0), exp_move(from_above[1], 3, 0, 0)])
    mine = jnp.stack([pair, from_above, from_two, from_below])
    other = exp_move(mine, 0, 0, 1)

    def ordered(left, right, axis):
        both = jnp.stack(
            [jnp.where(core == 0, left, right), jnp.where(core == 0, right, left)], axis=axis + 2
        )
        return ring_order(both, row_y, axis)

    packed_rows = packed.shape[0]
    mine_flat = mine.reshape(8 * packed_rows, D)
    other_flat = other.reshape(8 * packed_rows, D)
    full_router = ordered(
        mine[:, :, 2 * HD : 2 * HD + per_group], other[:, :, 2 * HD : 2 * HD + per_group], 0
    ).reshape(EXPERTS, D)
    gains_row = 2 * HD + per_group
    full_gains = ordered(mine[:, :, gains_row, : 2 * HD], other[:, :, gains_row, : 2 * HD], 0)
    full_gains = full_gains.reshape(exp_count, 2, HD).transpose(1, 0, 2).reshape(2, D)
    gain_one = full_gains[0].astype(jnp.float32)
    gain_two = full_gains[1].astype(jnp.float32)

    full_output = lax.all_gather(output_weight.T, "exp", axis=0, tiled=True)

    expert_ids = jnp.arange(EXPERTS, dtype=jnp.int32)
    named = jnp.any(route_ids[:, :, None] == expert_ids[None, None, :], axis=1)
    named_low = named.astype(bf16)
    token_ids = jnp.arange(row_count)
    earlier = (token_ids[None, :] < token_ids[:, None]).astype(bf16)
    rank = mat(earlier, named_low)
    place = jnp.where(named, rank + 1.0, 0.0).astype(bf16)
    slot_ids = jnp.arange(EXPERTS * CAP, dtype=jnp.int32)
    widen = (slot_ids[None, :] // CAP == expert_ids[:, None]).astype(bf16)
    chosen_slot = mat(place, widen) == (slot_ids % CAP + 1).astype(jnp.float32)[None, :]
    select = chosen_slot.astype(bf16)

    sent_grads = jnp.concatenate(
        [cotangent[0], place, jnp.zeros((row_count, WIDE - EXPERTS), bf16)], axis=1
    )
    all_grads = lax.all_gather(sent_grads, "exp", axis=0, tiled=False)

    inv_one = lax.rsqrt(jnp.mean(inputs * inputs, axis=-1, keepdims=True) + eps_norm)
    normed_one = (inputs * inv_one * gain_one).astype(bf16)
    halves = [
        contract_cols(normed_one, flat).reshape(row_count, 4, 2, packed_rows)[..., : 2 * HD]
        for flat in (mine_flat, other_flat)
    ]
    projected = ordered(*halves, 1).reshape(row_count, exp_count, 2 * HD)
    query_raw = projected[:, :, :HD]
    kv_raw = projected[:, :, HD:]
    first_row = lax.axis_index("ctx") * row_count
    cosine, sine = rope_tables(first_row, row_count)
    queries = rotate(query_raw, cosine, sine).astype(bf16)
    keys = rotate(kv_raw[:, :KV], cosine, sine).astype(bf16)
    values = kv_raw[:, KV:].astype(bf16)
    sent_kv = jnp.concatenate([keys, values], axis=1).reshape(row_count, 2 * KV * HD)
    all_kv = spread(sent_kv, "ctx", None, ctx_count).reshape(ctx_count * row_count, 2 * KV * HD)
    flat_queries = queries.reshape(row_count, HEADS * HD)
    mixed_low = attention_call(attend_kernel, (flat_queries, all_kv), None, first_row, "attend")
    sent_mixed = mixed_low.reshape(row_count, exp_count, HD).transpose(1, 0, 2)
    sent_mixed = sent_mixed.reshape(exp_count, row_count // 2, 2 * HD)
    attended = mat(mixed_low, full_output)
    residual = inputs + attended
    inv_two = lax.rsqrt(jnp.mean(residual * residual, axis=-1, keepdims=True) + eps_norm)
    normed_two = (residual * inv_two * gain_two).astype(bf16)
    logits = contract_cols(normed_two, full_router)
    gates = jax.nn.softmax(jnp.where(named, logits, -1e30), axis=-1)
    gates = jnp.where(named, gates, 0.0)
    gate_parts = three_parts(gates)
    extended = jnp.concatenate(
        [normed_two, *gate_parts, jnp.zeros((row_count, WIDE - 3 * EXPERTS), bf16)], axis=1
    )
    sent_rows = contract_rows(select, extended).astype(bf16)
    sent_rows, below_other, above_other = lax.optimization_barrier(
        (sent_rows, below_other, above_other)
    )
    far_other = ctx_move(above_other, 3, 0)
    arrived = exchange(sent_rows.reshape(exp_count, per_group * CAP, D + WIDE), "exp")
    later_normed, arrived, far, far_other = lax.optimization_barrier(
        (normed_one, arrived, far, far_other)
    )
    full_experts = (
        own_experts, other_experts, below, below_other, above, above_other, far, far_other
    )
    all_normed = lax.all_gather(later_normed, "exp", axis=0, tiled=True)
    produced, back, expert_grads = expert_math(
        arrived.reshape(exp_count, per_group, CAP, D + WIDE),
        all_grads,
        full_experts,
        (gate_momentum, up_momentum, down_momentum),
    )
    head_mixed = exchange(after(sent_mixed, arrived), "exp")
    back, head_mixed = lax.optimization_barrier((back, head_mixed))
    head_mixed = head_mixed.reshape(exp_count * row_count, HD)
    returned = exchange(back.reshape(exp_count, per_group * CAP, D + WIDE), "exp")
    returned = returned.reshape(EXPERTS * CAP, D + WIDE)
    far_up, far_down = ctx_move(expert_grads[2, 0], 1, 0), ctx_move(expert_grads[2, 1], 3, 0)
    added_up = plus(expert_grads[1, 0], far_up)
    added_down = plus(expert_grads[3, 1], far_down)
    returned = after(returned, added_up, added_down)
    sum_up, sum_down = owner_move(expert_grads[1, 1], 1), owner_move(expert_grads[3, 0], 3)
    added_up, added_down = owner_move(added_up, 1), owner_move(added_down, 3)
    produced = after(produced, returned)
    route_values = exchange(produced.reshape(exp_count, per_group * CAP, D), "exp")
    summed_back = mat(select, returned)
    tail = summed_back[:, D:]
    grad_gates = (
        tail[:, :EXPERTS] + tail[:, EXPERTS : 2 * EXPERTS] + tail[:, 2 * EXPERTS : 3 * EXPERTS]
    )
    grad_logits = (
        gates * (grad_gates - jnp.sum(gates * grad_gates, axis=-1, keepdims=True))
    ).astype(bf16)
    grad_normed_two = summed_back[:, :D] + mat(grad_logits, full_router)
    scaled_two = grad_normed_two * gain_two
    grad_gain_two = jnp.sum(grad_normed_two * residual * inv_two, axis=0)
    grad_residual = (
        grad_out
        + inv_two * scaled_two
        - residual * inv_two**3 * jnp.mean(scaled_two * residual, axis=-1, keepdims=True)
    )
    grad_attended = grad_residual.astype(bf16)
    all_attended = lax.all_gather(grad_attended, "exp", axis=0, tiled=True)
    grad_attended = after(grad_attended, sum_up, sum_down)
    grad_mixed = contract_cols(grad_attended, full_output).astype(bf16)
    grad_queries, key_terms, value_terms = attention_call(
        attend_back_kernel, (flat_queries, all_kv), grad_mixed, first_row, "attend_back"
    )
    kv_terms = jnp.concatenate([key_terms, value_terms], axis=1)
    kv_terms, added_up, added_down = lax.optimization_barrier((kv_terms, added_up, added_down))
    both_sums = [
        sum((part.astype(jnp.float32) for part in parts), expert_grads[0, slot].astype(jnp.float32))
        for slot, parts in enumerate(((added_up, sum_down), (sum_up, added_down)))
    ]
    other_sums = both_sums[1].astype(bf16)
    kv_terms = after(kv_terms, route_values, other_sums)
    other_sums = ctx_move(other_sums, 0, 1)
    kv_terms = exchange(kv_terms.reshape(ctx_count, row_count, 2 * KV * HD), "ctx")
    grad_query_raw = rotate(
        grad_queries.reshape(row_count, HEADS, HD), cosine, -sine
    ).astype(bf16)
    kv_sums = jnp.sum(kv_terms.astype(jnp.float32), axis=0).reshape(row_count, 2 * KV, HD)
    grad_key_raw = rotate(kv_sums[:, :KV], cosine, -sine).astype(bf16)
    grad_kv_raw = jnp.concatenate([grad_key_raw, kv_sums[:, KV:].astype(bf16)], axis=1)
    grad_projected = jnp.concatenate([grad_query_raw, grad_kv_raw], axis=2)
    by_core = ring_order(grad_projected.reshape(row_count, 4, 2, 2, 2 * HD), -row_y, 1)
    by_core = jnp.pad(by_core, ((0, 0),) * 4 + ((0, packed_rows - 2 * HD),))
    first_core, second_core = by_core[:, :, :, 0], by_core[:, :, :, 1]
    grad_normed_one = mat(
        jnp.where(core == 0, first_core, second_core).reshape(row_count, -1), mine_flat
    ) + mat(jnp.where(core == 0, second_core, first_core).reshape(row_count, -1), other_flat)
    scaled_one = grad_normed_one * gain_one
    grad_gain_one = jnp.sum(grad_normed_one * inputs * inv_one, axis=0)
    input_grad = (
        grad_residual
        + inv_one * scaled_one
        - inputs * inv_one**3 * jnp.mean(scaled_one * inputs, axis=-1, keepdims=True)
    )

    small_rows = (per_group * D + 2 * HD) // (2 * HD)
    small = jnp.concatenate(
        [
            contract_rows(grad_logits, normed_two).reshape(exp_count, -1, 2 * HD),
            jnp.stack([grad_gain_one, grad_gain_two])
            .reshape(2, exp_count, HD)
            .transpose(1, 0, 2)
            .reshape(exp_count, 1, 2 * HD),
            jnp.zeros((exp_count, 7, 2 * HD), jnp.float32),
        ],
        axis=1,
    ).astype(bf16)
    route_values = route_values.reshape(EXPERTS * CAP, D)
    head_send = jnp.concatenate([jnp.transpose(grad_projected, (1, 0, 2)), small], axis=1)
    level, side = lax.axis_index("ctx") // 2, lax.axis_index("ctx") % 2
    owned = (both_sums[0] + other_sums.astype(jnp.float32)).astype(bf16)
    head_send, owned = lax.optimization_barrier((head_send, owned))
    head_grads = exchange(head_send, "exp")
    keep, cross = owner_orthogonal(owned, jnp.stack([level, side]).astype(jnp.int32))
    head_grads = after(head_grads, keep, cross)
    crossed = ctx_move(cross, 0, 1)
    small = jnp.sum(head_grads[:, row_count : row_count + small_rows].astype(jnp.float32), axis=0)
    head_grads = head_grads[:, :row_count].reshape(exp_count * row_count, 2 * HD)

    part = jnp.concatenate(
        [
            mat(lax.optimization_barrier(head_grads.T), all_normed),
            mat(lax.optimization_barrier(head_mixed.T), all_attended),
        ],
        axis=0,
    )
    width = D // ctx_count
    part = jnp.concatenate(
        [
            jnp.transpose(part.astype(bf16).reshape(3 * HD, ctx_count, width), (1, 0, 2)),
            jnp.broadcast_to(
                jnp.pad(small.astype(bf16), ((0, 7), (0, 0)))[None], (ctx_count, 24, width)
            ),
        ],
        axis=1,
    )
    part, crossed = lax.optimization_barrier((exchange(part, "ctx"), crossed))
    returned_rows = [
        ctx_move(jnp.stack([keep[up], crossed[up]]), up, 0) if up else jnp.stack([keep[0], crossed[0]])
        for up in range(4)
    ]
    part = jnp.sum(part.astype(jnp.float32), axis=0)
    sums = spread(part[: 3 * HD].astype(bf16), "ctx", None, ctx_count)
    sums = jnp.transpose(sums, (0, 2, 1)).reshape(D, 3 * HD).astype(jnp.float32)
    small = part[3 * HD : 3 * HD + small_rows]
    sum_router = small[:-1].reshape(per_group, D).T
    sum_gains = small[-1].reshape(2, HD)
    router_one, router_two, router_new = adam_update(
        router, router_first, router_second, sum_router, router_rate, decay_rate
    )
    gains_one, gains_two, gains_new = adam_update(
        gains, gains_first, gains_second, sum_gains, gain_rate, 0.0
    )

    head_fresh, head_new = head_blocks(
        sums,
        jnp.concatenate([query_momentum, kv_momentum, output_momentum], axis=1),
        jnp.concatenate([query_weight, kv_weight, output_weight], axis=1),
    )

    returned_rows = jnp.stack(returned_rows).reshape(8, 2, D // ctx_count, -1)
    fresh, ortho = [], []
    for kind in range(3):
        picked = [
            lax.dynamic_index_in_dim(
                returned_rows,
                2 * ((level + 4 - kind) % 4) + (expert + side) % 2,
                0,
                keepdims=False,
            ).astype(jnp.float32)
            for expert in range(per_group)
        ]
        fresh.append(jnp.stack([rows[0] for rows in picked]))
        ortho.append(jnp.stack([rows[1] for rows in picked]))
    new = [
        step_weight(weight, factor)
        for weight, factor in zip((gate_weight, up_weight, down_weight), ortho)
    ]

    gates_wide = [mat(part, widen) for part in gate_parts]
    block_value = residual
    for wide in gates_wide:
        weighted = jnp.where(chosen_slot, wide, 0.0).astype(bf16)
        block_value = block_value + mat(weighted, route_values)
    return (
        block_value.astype(bf16)[None],
        input_grad[None],
        head_fresh[:, :HD],
        head_new[:, :HD],
        head_fresh[:, HD : 2 * HD],
        head_new[:, HD : 2 * HD],
        head_fresh[:, 2 * HD :],
        head_new[:, 2 * HD :],
        fresh[0],
        new[0],
        fresh[1],
        new[1],
        fresh[2],
        new[2],
        router_one,
        router_two,
        router_new,
        gains_one,
        gains_two,
        gains_new,
    )


def solution(mesh):
    return jax.shard_map(
        body,
        mesh=mesh,
        in_specs=(
            P("exp", "ctx", None),
            P("exp", "ctx", None),
            P("exp", "ctx", None),
            P(None, "exp"),
            P(None, "exp"),
            P(None, "exp"),
            P(None, "exp"),
            P(None, "exp"),
            P("exp", "ctx", None),
            P("exp", "ctx", None),
            P("exp", "ctx", None),
            P(None, "exp"),
            P(None, "exp"),
            P(None, "exp"),
            P("exp", "ctx", None),
            P("exp", "ctx", None),
            P("exp", "ctx", None),
            P(None, "exp"),
            P(None, "exp"),
            P(None, "exp"),
            P(None, "exp"),
        ),
        out_specs=(
            P("exp", "ctx", None),
            P("exp", "ctx", None),
            P(None, "exp"),
            P(None, "exp"),
            P(None, "exp"),
            P(None, "exp"),
            P(None, "exp"),
            P(None, "exp"),
            P("exp", "ctx", None),
            P("exp", "ctx", None),
            P("exp", "ctx", None),
            P("exp", "ctx", None),
            P("exp", "ctx", None),
            P("exp", "ctx", None),
            P(None, "exp"),
            P(None, "exp"),
            P(None, "exp"),
            P(None, "exp"),
            P(None, "exp"),
            P(None, "exp"),
        ),
        check_vma=False,
    )
```
